32 devices in a mesh: depth: 4 (over x, core), rows: 8 (over z, y).
Axes of the slice: x: 2, y: 2, z: 4, core: 2. Of those that a mesh axis runs over, the one named last changes fastest.
Arguments:
- source_top: bfloat16 [2, 2, 512, 512], P(None, None, 'rows'), may hold values from -8 to 8
- adjoint_bottom: bfloat16 [2, 2, 512, 512], P(None, None, 'rows'), may hold values from -8 to 8
- slowness: float32 [4, 512, 512], P('depth', 'rows'), may hold values from 0.7 to 1.3
- correction: float32 [4, 512, 512], P('depth', 'rows'), may hold values from -0.16 to 0.16
- slowness_ref: float32 [4], P('depth'), may hold values from 0.9 to 1.1
- omega: float32 [2], replicated, may hold values from 0.8 to 1.6
Outputs:
- gradient: float32 [4, 512, 512], P('depth', 'rows')
The draws below stay inside these ranges and needn't reach their ends.
All inputs are finite; a program needn't handle non-finite values.
Results may differ from the reference program's by a relative error of at most 0.025.
Values may be sent and summed in bfloat16 or wider, within the bound.
No kernel may reach another device: no remote copies, remote signals or barrier semaphores. Data moves between devices by JAX's collectives and lax.ppermute only.
A program may use at most 64 MiB of HBM per device.

```python
import math
import jax
import jax.numpy as jnp
from jax import lax

NX = 512
NY = 512
NF = 2
NZ = 4


def steps_of(rng, extent, split, low, largest):
    def one(dim, parts):
        draws = jax.random.uniform(jax.random.fold_in(jax.random.fold_in(rng, 6), dim), (parts,), jnp.float32, low / len(split), largest / len(split))
        return jnp.repeat(jnp.exp(draws), extent[dim] // parts).reshape((-1,) + (1,) * (len(extent) - dim - 1))

    level = one(*split[0])
    for cut in split[1:]:
        level = level * one(*cut)
    return level


def normal_values(rng, shape, deviation, reach, cuts=(), held_as=jnp.bfloat16):
    drawn = deviation * jax.random.normal(rng, shape, jnp.float32)
    if cuts:
        drawn = drawn * steps_of(rng, shape, cuts, -0.22, 0.18)
    return jnp.clip(drawn, -reach, reach).astype(held_as)


def setup_inputs(seed: int = 0) -> dict:
    arg_keys = jax.random.split(jax.random.key(seed), 7)
    return {
        "source_top": normal_values(arg_keys[0], (NF, 2, NX, NY), 2.0, 8.0, ((2, 8),)),
        "adjoint_bottom": normal_values(arg_keys[1], (NF, 2, NX, NY), 2.0, 8.0, ((2, 8),)),
        "slowness": jnp.clip(0.7 + 0.59999996 * jax.random.uniform(arg_keys[2], (NZ, NX, NY), jnp.float32) ** steps_of(arg_keys[2], (NZ, NX, NY), ((0, 4), (1, 8)), -0.2, 0.2), 0.7, 1.3),
        "correction": jnp.clip(jax.random.uniform(arg_keys[3], (NZ, NX, NY), jnp.float32, -0.16, 0.16) * steps_of(arg_keys[3], (NZ, NX, NY), ((0, 4), (1, 8)), -0.4, 0.0), -0.16, 0.16),
        "slowness_ref": jnp.clip(0.9 + 0.20000005 * jax.random.uniform(arg_keys[4], (NZ,), jnp.float32) ** steps_of(arg_keys[4], (NZ,), ((0, 4),), -0.2, 0.2), 0.9, 1.1),
        "omega": jnp.clip(jnp.exp(jax.random.uniform(arg_keys[5], (NF,), jnp.float32, math.log(0.8), math.log(1.6))), 0.8, 1.6),
    }


depth_step = 1.0

def rounded(values):
    return lax.optimization_barrier(values.astype(jnp.bfloat16)).astype(jnp.float32)

def rounded_complex(values):
    return rounded(jnp.real(values)) + 1j * rounded(jnp.imag(values))

def wavenumbers(length):
    positions = jnp.arange(length, dtype=jnp.int32)
    signed = jnp.where(positions >= length // 2, positions - length, positions)
    return signed.astype(jnp.float32) * (2.0 * math.pi / length)

def phase_for(omega_value, reference_slow):
    wave_x = wavenumbers(NX)[:, None]
    wave_y = wavenumbers(NY)[None, :]
    squared = (omega_value * reference_slow) ** 2 - wave_x ** 2 - wave_y ** 2
    damping = jnp.exp(-jnp.sqrt(jnp.maximum(-squared, 0.0)) * depth_step)
    angles = jnp.sqrt(jnp.maximum(squared, 0.0)) * depth_step
    return damping * jnp.cos(angles) + 1j * (damping * jnp.sin(angles))

def transform(values):
    half_way = rounded_complex(jnp.fft.fft(values, axis=1, norm='ortho'))
    return jnp.fft.fft(half_way, axis=0, norm='ortho')

def inverse(values):
    half_way = rounded_complex(jnp.fft.ifft(values, axis=0, norm='ortho'))
    return jnp.fft.ifft(half_way, axis=1, norm='ortho')

def laplace(values):
    return jnp.roll(values, 1, 0) + jnp.roll(values, -1, 0) + jnp.roll(values, 1, 1) + jnp.roll(values, -1, 1) - 4.0 * values

def reference(source_top, adjoint_bottom, slowness, correction, slowness_ref, omega):
    gradient = [jnp.zeros((NX, NY), jnp.float32) for depth_level in range(NZ)]
    for frequency in range(NF):
        omega_value = omega[frequency]
        phases = [phase_for(omega_value, slowness_ref[depth_level]) for depth_level in range(NZ)]
        lenses = []
        for depth_level in range(NZ):
            angles = omega_value * (slowness[depth_level] - slowness_ref[depth_level]) * depth_step
            lenses.append(jnp.cos(angles) + 1j * jnp.sin(angles))
        plane = source_top[frequency, 0].astype(jnp.float32) + 1j * source_top[frequency, 1].astype(jnp.float32)
        planes_below = []
        for depth_level in range(NZ):
            lensed = lenses[depth_level] * inverse(phases[depth_level] * transform(plane))
            scaled = rounded_complex(correction[depth_level] * lensed)
            plane = rounded_complex(lensed + 1j * laplace(scaled))
            planes_below.append(plane)
        adjoint = adjoint_bottom[frequency, 0].astype(jnp.float32) + 1j * adjoint_bottom[frequency, 1].astype(jnp.float32)
        for depth_level in reversed(range(NZ)):
            below_plane = planes_below[depth_level]
            product = jnp.real(below_plane) * jnp.imag(adjoint) - jnp.imag(below_plane) * jnp.real(adjoint)
            gradient[depth_level] = gradient[depth_level] + omega_value * product
            pulled = jnp.conj(lenses[depth_level]) * (adjoint - 1j * correction[depth_level] * laplace(adjoint))
            adjoint = rounded_complex(inverse(jnp.conj(phases[depth_level]) * transform(pulled)))
    return jnp.stack(gradient).astype(jnp.float32)
```

```python
from functools import partial
import math

import jax
import jax.numpy as jnp
import numpy as np
from jax import lax
from jax.experimental import pallas as pl
from jax.experimental.pallas import tpu as pltpu
from jax.sharding import PartitionSpec as P

bf16 = jnp.bfloat16
f32 = jnp.float32
vmem_bytes = 48 * 1024 * 1024


def basis(length):
    half, quarter = length // 2, length // 4
    n = np.arange(half)[:, None]
    j = np.arange(quarter)[None, :]
    scale = math.sqrt(2.0 / length)
    even_cos = scale * np.cos(2 * np.pi * ((2 * j * n) % length) / length)
    even_sin = scale * np.sin(2 * np.pi * ((2 * j * n) % length) / length)
    even_cos[:, 0] = 1.0 / math.sqrt(length)
    even_sin[:, 0] = (1.0 - 2.0 * (np.arange(half) % 2)) / math.sqrt(length)
    odd_cos = scale * np.cos(2 * np.pi * (((2 * j + 1) * n) % length) / length)
    odd_sin = scale * np.sin(2 * np.pi * (((2 * j + 1) * n) % length) / length)
    even = np.concatenate([even_cos, even_sin], 1).astype(np.float32)
    odd = np.concatenate([odd_cos, odd_sin], 1).astype(np.float32)
    return even, odd


def basis_tables(length):
    even, odd = basis(length)
    return jnp.asarray(np.stack([even, odd, even.T, odd.T]), bf16)


def dot(a, b):
    return jnp.dot(a, b, preferred_element_type=f32)


def small_cos_sin(a):
    s = a * a
    cos = 1.0 + s * (-0.5 + s * (1.0 / 24 + s * (-1.0 / 720 + s * (1.0 / 40320))))
    sin = a * (1.0 + s * (-1.0 / 6 + s * (1.0 / 120 + s * (-1.0 / 5040 + s * (1.0 / 362880)))))
    return cos, sin


def phase_kernel(nx, ny, ks_ref, sign_ref, out_ref):
    qx, qy = nx // 4, ny // 4
    slot = pl.program_id(0)
    level = ks_ref[slot]
    sign = sign_ref[0]

    def waves(rows, cols, axis, parity, length):
        j = lax.broadcasted_iota(jnp.int32, (rows, cols), axis)
        return (2 * j + parity).astype(f32) * (2.0 * math.pi / length)

    def values(kx, ky):
        squared = level * level - kx * kx - ky * ky
        damping = jnp.exp(-jnp.sqrt(jnp.maximum(-squared, 0.0)))
        angle = jnp.sqrt(jnp.maximum(squared, 0.0))
        return damping * jnp.cos(angle), sign * damping * jnp.sin(angle)

    edge = math.pi
    for px in range(2):
        for py in range(2):
            kx = waves(qx, qy, 0, px, nx)
            ky = waves(qx, qy, 1, py, ny)
            first_row = lax.broadcasted_iota(jnp.int32, (qx, qy), 0) == 0
            first_col = lax.broadcasted_iota(jnp.int32, (qx, qy), 1) == 0
            for sx in range(2):
                for sy in range(2):
                    if (sx and not px) or (sy and not py):
                        kxs = jnp.where(first_row, edge, kx) if (sx and not px) else kx
                        kys = jnp.where(first_col, edge, ky) if (sy and not py) else ky
                    else:
                        kxs, kys = kx, ky
                    re, im = values(kxs, kys)
                    rows = pl.ds((2 * px + sx) * qx, qx)
                    cols = pl.ds((2 * py + sy) * qy, qy)
                    out_ref[0, 0, rows, cols] = re.astype(bf16)
                    out_ref[0, 1, rows, cols] = im.astype(bf16)


def phase_table(nx, ny, levels, sign):
    slots = levels.shape[0]
    return pl.pallas_call(
        partial(phase_kernel, nx, ny),
        out_shape=jax.ShapeDtypeStruct((slots, 2, nx, ny), bf16),
        grid=(slots,),
        in_specs=[pl.BlockSpec(memory_space=pltpu.SMEM)] * 2,
        out_specs=pl.BlockSpec((1, 2, nx, ny), lambda i: (i, 0, 0, 0)),
        compiler_params=pltpu.CompilerParams(vmem_limit_bytes=vmem_bytes),
        name="phase_table",
    )(levels, sign)


def fold_cols(values):
    half = values.shape[1] // 2
    a, b = values[:, :half], values[:, half:]
    return (a + b).astype(bf16), (a - b).astype(bf16)


def transform(nx, ny, folded, phase, qx_ref, qy_ref, mid, spec, out):
    hx, hy = nx // 2, ny // 2
    step = min(128, hx)
    for part in range(2):
        for start in range(0, hx, step):
            top, low = pl.ds(start, step), pl.ds(hx + start, step)
            for par in range(2):
                cols = pl.ds(par * hy, hy)
                a = dot(folded[part, top, cols], qy_ref[par])
                b = dot(folded[part, low, cols], qy_ref[par])
                mid[part, top, cols] = (a + b).astype(bf16)
                mid[part, low, cols] = (a - b).astype(bf16)
    for start in range(0, ny, hy):
        cols = pl.ds(start, hy)
        back = []
        for par in range(2):
            rows = pl.ds(par * hx, hx)
            zr = dot(qx_ref[2 + par], mid[0, rows, cols])
            zi = dot(qx_ref[2 + par], mid[1, rows, cols])
            pr = phase[0, 0, rows, cols].astype(f32)
            pi = phase[0, 1, rows, cols].astype(f32)
            yr = (zr * pr - zi * pi).astype(bf16)
            yi = (zr * pi + zi * pr).astype(bf16)
            back.append((dot(qx_ref[par], yr), dot(qx_ref[par], yi)))
        for part in range(2):
            a, b = back[0][part], back[1][part]
            spec[part, pl.ds(0, hx), cols] = (a + b).astype(bf16)
            spec[part, pl.ds(hx, hx), cols] = (a - b).astype(bf16)
    for part in range(2):
        for start in range(0, nx, 2 * step):
            rows = pl.ds(start, 2 * step)
            a = dot(spec[part, rows, pl.ds(0, hy)], qy_ref[2])
            b = dot(spec[part, rows, pl.ds(hy, hy)], qy_ref[3])
            out[part, rows, pl.ds(0, hy)] = (a + b).astype(bf16)
            out[part, rows, pl.ds(hy, hy)] = (a - b).astype(bf16)


def first_kernel(dims, orders, ints_ref, phase, qx_ref, qy_ref, *rest):
    nx, ny, rows_here = dims
    counts = [len(o) for o in orders]
    pieces, (out, folded, mid, spec) = rest[: sum(counts)], rest[sum(counts) :]
    part_id, forward = ints_ref[0], ints_ref[1]
    at = 0
    for part, order in enumerate(orders):
        for piece_order in order:
            piece = pieces[at]
            at += 1
            for i, offset in enumerate(piece_order):
                block = part_id ^ offset
                rows = pl.ds(pl.multiple_of(block * rows_here, rows_here), rows_here)
                values = piece[i]

                @pl.when(forward == 1)
                def _():
                    a, b = fold_cols(values.astype(f32))
                    folded[part, rows, pl.ds(0, ny // 2)] = a
                    folded[part, rows, pl.ds(ny // 2, ny // 2)] = b

                @pl.when(forward == 0)
                def _():
                    out[part, rows, :] = values

    @pl.when(forward == 1)
    def _():
        transform(nx, ny, folded, phase, qx_ref, qy_ref, mid, spec, out)


def laplace_rows(ref, part, start, count):
    center = ref[part, pl.ds(start + 8, count), :]
    width = center.shape[1]
    return (
        ref[part, pl.ds(start + 7, count), :]
        + ref[part, pl.ds(start + 9, count), :]
        + pltpu.roll(center, 1, 1)
        + pltpu.roll(center, width - 1, 1)
        - 4.0 * center
    )


def wrap_rows(ref, nx):
    for part in range(2):
        ref[part, pl.ds(7, 1), :] = ref[part, pl.ds(nx + 7, 1), :]
        ref[part, pl.ds(nx + 8, 1), :] = ref[part, pl.ds(8, 1), :]


def step_kernel(
    dims, pos, last, ints_ref, omega_ref, w_ref, own_ref, other_ref, phase, qx_ref, qy_ref, *rest
):
    nx, ny, rows_here = dims
    if last:
        (coef_rows, edges, out_rows, end_rows, out, coef, lens, plane, halo, folded, mid, spec, tall) = rest
    else:
        out, out_rows, coef, lens, plane, halo, folded, mid, spec = rest
    part_id, forward, side = ints_ref[0], ints_ref[1], ints_ref[2]
    omega = omega_ref[0]
    hy = ny // 2
    blocks = nx // rows_here
    for q, src in enumerate((own_ref, other_ref)):
        cols = pl.ds(pl.multiple_of((side ^ q) * hy, hy), hy)
        for offset in range(blocks):
            block = part_id ^ offset
            rows = pl.ds(pl.multiple_of(block * rows_here, rows_here), rows_here)
            coef[rows, cols] = src[pos[0][offset]].astype(f32)
            cos, sin = small_cos_sin(omega * src[blocks + pos[1][offset]].astype(f32))
            lens[0, rows, cols] = cos
            lens[1, rows, cols] = sin
    chunk = 32

    @pl.when(forward == 1)
    def _():
        for start in range(0, nx, chunk):
            rows = pl.ds(start, chunk)
            lr, li = lens[0, rows, :], lens[1, rows, :]
            wr, wi = w_ref[0, rows, :].astype(f32), w_ref[1, rows, :].astype(f32)
            c = coef[rows, :]
            ur, ui = wr * lr - wi * li, wr * li + wi * lr
            plane[0, rows, :] = ur
            plane[1, rows, :] = ui
            halo[0, pl.ds(start + 8, chunk), :] = c * ur
            halo[1, pl.ds(start + 8, chunk), :] = c * ui
        wrap_rows(halo, nx)
        for start in range(0, nx, chunk):
            rows = pl.ds(start, chunk)
            ur = plane[0, rows, :] - laplace_rows(halo, 1, start, chunk)
            ui = plane[1, rows, :] + laplace_rows(halo, 0, start, chunk)
            plane[0, rows, :] = ur
            plane[1, rows, :] = ui
            for part, u in enumerate((ur, ui)):
                a, b = fold_cols(u)
                folded[part, rows, pl.ds(0, hy)] = a
                folded[part, rows, pl.ds(hy, hy)] = b
        mine = pl.ds(pl.multiple_of(part_id * rows_here, rows_here), rows_here)
        for part in range(2):
            out_rows[part] = plane[part, mine, :].astype(bf16)

    @pl.when(forward == 0)
    def _():
        for part in range(2):
            halo[part, pl.ds(8, nx), :] = w_ref[part].astype(f32)
        wrap_rows(halo, nx)
        for start in range(0, nx, chunk):
            rows = pl.ds(start, chunk)
            lr, li = lens[0, rows, :], lens[1, rows, :]
            c = coef[rows, :]
            tr = halo[0, pl.ds(start + 8, chunk), :] + c * laplace_rows(halo, 1, start, chunk)
            ti = halo[1, pl.ds(start + 8, chunk), :] - c * laplace_rows(halo, 0, start, chunk)
            for part, u in enumerate((tr * lr + ti * li, ti * lr - tr * li)):
                a, b = fold_cols(u)
                folded[part, rows, pl.ds(0, hy)] = a
                folded[part, rows, pl.ds(hy, hy)] = b

    transform(nx, ny, folded, phase, qx_ref, qy_ref, mid, spec, out)
    first = pl.multiple_of(part_id * rows_here, rows_here)
    mine = pl.ds(first, rows_here)

    @pl.when(forward == 0)
    def _():
        for part in range(2):
            out_rows[part] = out[part, mine, :]

    if not last:
        return

    @pl.when(forward == 0)
    def _():
        end_rows[...] = jnp.zeros_like(end_rows)

    @pl.when(forward == 1)
    def _():
        before = pl.ds(pl.multiple_of(lax.rem(first + nx - 16, nx), 16), 16)
        after = pl.ds(pl.multiple_of(lax.rem(first + rows_here, nx), 16), 16)

        def scaled(values, c, d):
            lr, li = small_cos_sin(omega * d.astype(f32))
            wr, wi = values[0].astype(f32), values[1].astype(f32)
            ur, ui = wr * lr - wi * li, wr * li + wi * lr
            cf = c.astype(f32)
            return ur, ui, cf * ur, cf * ui

        ur, ui, gr, gi = scaled(
            (out[0, mine, :], out[1, mine, :]), coef_rows[0], coef_rows[1]
        )
        tall[0, pl.ds(8, rows_here), :] = gr
        tall[1, pl.ds(8, rows_here), :] = gi
        _, _, gr, gi = scaled(
            (out[0, before, :][15:16], out[1, before, :][15:16]), edges[0, 0], edges[0, 1]
        )
        tall[0, pl.ds(7, 1), :] = gr
        tall[1, pl.ds(7, 1), :] = gi
        _, _, gr, gi = scaled(
            (out[0, after, :][0:1], out[1, after, :][0:1]), edges[1, 0], edges[1, 1]
        )
        tall[0, pl.ds(rows_here + 8, 1), :] = gr
        tall[1, pl.ds(rows_here + 8, 1), :] = gi
        end_rows[0] = (ur - laplace_rows(tall, 1, 0, rows_here)).astype(bf16)
        end_rows[1] = (ui + laplace_rows(tall, 0, 0, rows_here)).astype(bf16)


vm = pl.BlockSpec(memory_space=pltpu.VMEM)
sm = pl.BlockSpec(memory_space=pltpu.SMEM)


def phase_spec(slot, nx, ny):
    return pl.BlockSpec((1, 2, nx, ny), lambda i: (slot, 0, 0, 0))


def run_first(dims, orders, ints, phases, qx, qy, pieces):
    nx, ny, _ = dims
    return pl.pallas_call(
        partial(first_kernel, dims, orders),
        out_shape=jax.ShapeDtypeStruct((2, nx, ny), bf16),
        grid=(1,),
        in_specs=[sm, phase_spec(0, nx, ny), vm, vm] + [vm] * len(pieces),
        out_specs=vm,
        scratch_shapes=[pltpu.VMEM((2, nx, ny), bf16)] * 3,
        compiler_params=pltpu.CompilerParams(vmem_limit_bytes=vmem_bytes),
        cost_estimate=pl.CostEstimate(flops=2**30, bytes_accessed=2**22, transcendentals=0),
        name="first_step",
    )(ints, phases, qx, qy, *pieces)


def run_step(dims, pos, slot, ints, omega, w, own, other, phases, qx, qy, ends=None):
    nx, ny, rows_here = dims
    last = ends is not None
    rows_shape = jax.ShapeDtypeStruct((2, rows_here, ny), bf16)
    full = pltpu.VMEM((2, nx, ny), bf16)
    scratch = [
        pltpu.VMEM((nx, ny), f32),
        pltpu.VMEM((2, nx, ny), f32),
        pltpu.VMEM((2, nx, ny), f32),
        pltpu.VMEM((2, nx + 16, ny), f32),
        full,
        full,
        full,
    ]
    if last:
        outs = (rows_shape, rows_shape)
        scratch = [full] + scratch + [pltpu.VMEM((2, rows_here + 16, ny), f32)]
    else:
        outs = (jax.ShapeDtypeStruct((2, nx, ny), bf16), rows_shape)
    return pl.pallas_call(
        partial(step_kernel, dims, pos, last),
        out_shape=outs,
        grid=(1,),
        in_specs=[sm, sm, vm, vm, vm, phase_spec(slot, nx, ny), vm, vm] + [vm] * (2 if last else 0),
        out_specs=(vm, vm),
        scratch_shapes=scratch,
        compiler_params=pltpu.CompilerParams(vmem_limit_bytes=vmem_bytes),
        cost_estimate=pl.CostEstimate(flops=2**31, bytes_accessed=2**23, transcendentals=0),
        name="end_step" if last else "depth_step",
    )(ints, omega, w, own, other, phases, qx, qy, *(ends or ()))


def swap(values, axis, mask):
    size = lax.axis_size(axis)
    return lax.ppermute(values, axis, [(i, i ^ mask) for i in range(size)])


def doubling_masks(size):
    masks = []
    mask = size // 2
    while mask:
        masks.append(mask)
        mask //= 2
    descending = masks
    ascending = masks[:1] + masks[1:][::-1]
    return descending, ascending


def doubling_orders(masks):
    orders = [[0]]
    seen = [0]
    for mask in masks:
        new = [mask ^ o for o in seen]
        orders.append(new)
        seen = seen + new
    return orders


def gathered_pair(pair, axis):
    size = lax.axis_size(axis)
    order_pair = doubling_masks(size)
    pieces = [[pair[0:1]], [pair[1:2]]]
    got = swap(pair, axis, order_pair[0][0])
    pieces[0].append(got[0:1])
    pieces[1].append(got[1:2])
    for level in range(1, len(order_pair[0])):
        for which in range(2):
            have = jnp.concatenate(pieces[which], 0)
            pieces[which].append(swap(have, axis, order_pair[which][level]))
    return pieces


def per_device(source_top, adjoint_bottom, slowness, correction, slowness_ref, omega):
    row_parts = lax.axis_size("rows")
    sections = lax.axis_size("depth")
    group = lax.axis_index("depth")
    part_id = lax.axis_index("rows")
    freq_count = omega.shape[0]
    chains = 2 * freq_count
    rep = sections // chains
    rows_here, ny = slowness.shape[1:]
    nx = rows_here * row_parts
    dims = (nx, ny, rows_here)
    hy = ny // 2
    chain = group // rep
    forward = chain // freq_count
    freq = chain % freq_count
    side = group % 2
    omega_here = lax.dynamic_slice_in_dim(omega, freq, 1, 0)
    masks = doubling_masks(row_parts)
    orders = [doubling_orders(m) for m in masks]
    flat = [sum(o, []) for o in orders]
    pos = [[f.index(o) for o in range(row_parts)] for f in flat]

    def pick(values, index):
        return lax.dynamic_index_in_dim(values, index, 0, keepdims=False)

    plane = jnp.where(forward == 1, pick(source_top, freq), pick(adjoint_bottom, freq))
    plane_pieces = gathered_pair(plane, "rows")

    own = jnp.concatenate([correction, slowness - slowness_ref[:, None, None]], 0).astype(bf16)
    by_mask = jnp.stack([own] + [swap(own, "depth", k) for k in range(1, sections)])
    refs = jnp.stack([slowness_ref] + [swap(slowness_ref, "depth", k) for k in range(1, sections)])

    def depth_at(slot):
        return jnp.where(forward == 1, slot, sections - 1 - slot)

    def slot_coefs(slot):
        mine = pick(by_mask, group ^ depth_at(slot))
        half = lax.dynamic_slice_in_dim(mine, side * hy, hy, 2)
        pieces = gathered_pair(half, "rows")
        every = jnp.concatenate(pieces[0] + pieces[1], 0)
        return every, swap(every, "depth", 1)

    levels = jnp.concatenate(
        [pick(refs, group ^ jnp.where(forward == 1, t, (sections - t) % sections)) for t in range(sections)]
    )
    sign = jnp.where(forward == 1, 1.0, -1.0).astype(f32)[None]
    phases = phase_table(nx, ny, levels * omega_here, sign)

    coef_rows = pick(by_mask, group ^ (sections - 1))
    rows_up = [(i, (i + 1) % row_parts) for i in range(row_parts)]
    rows_down = [(j, i) for i, j in rows_up]
    edges = jnp.stack(
        [
            lax.ppermute(coef_rows[:, rows_here - 1 :], "rows", rows_up),
            lax.ppermute(coef_rows[:, :1], "rows", rows_down),
        ]
    )

    ints = jnp.stack([part_id, forward, side]).astype(jnp.int32)
    qx, qy = basis_tables(nx), basis_tables(ny)
    w = run_first(dims, orders, ints, phases, qx, qy, plane_pieces[0] + plane_pieces[1])
    row_outs = []
    for slot in range(sections - 1):
        every, other = slot_coefs(slot)
        ends = (coef_rows, edges) if slot == sections - 2 else None
        first, second = run_step(
            dims, pos, slot + 1, ints, omega_here, w, every, other, phases, qx, qy, ends
        )
        if ends is None:
            w = first
            row_outs.append(second)
        else:
            row_outs += [first, second]

    half_sections = sections // 2

    def index_for(g, target):
        return target if g >= half_sections else sections - 2 - target

    def to_target(mask):
        used = sorted(
            {index_for(g, g ^ mask) for g in range(sections) if index_for(g, g ^ mask) >= 0}
        )
        low = used[0]
        stack = jnp.stack(row_outs[low : used[-1] + 1])
        target = group ^ mask
        index = jnp.where(forward == 1, target, sections - 2 - target)
        payload = pick(stack, jnp.clip(index - low, 0, len(stack) - 1))
        return payload if mask == 0 else swap(payload, "depth", mask)

    fields = [to_target(i * rep) for i in range(chains)]
    gradient = jnp.zeros((rows_here, ny), f32)
    for i in range(freq_count):
        freq_i = freq ^ i
        a = fields[i].astype(f32)
        adjoint = jnp.where(
            group == sections - 1, pick(adjoint_bottom, freq_i), fields[i + freq_count]
        )
        b = adjoint.astype(f32)
        weight = pick(omega, freq_i) * sign[0]
        gradient = gradient + weight * (a[0] * b[1] - a[1] * b[0])
    return gradient[None]


def solution(mesh):
    in_specs = (
        P(None, None, "rows", None),
        P(None, None, "rows", None),
        P("depth", "rows", None),
        P("depth", "rows", None),
        P("depth"),
        P(),
    )
    out_specs = P("depth", "rows", None)
    return jax.shard_map(
        per_device, mesh=mesh, in_specs=in_specs, out_specs=out_specs, check_vma=False
    )
```

```python
from functools import partial
import math

import jax
import jax.numpy as jnp
import numpy as np
from jax import lax
from jax.experimental import pallas as pl
from jax.experimental.pallas import tpu as pltpu
from jax.sharding import PartitionSpec as P

bf16 = jnp.bfloat16
f32 = jnp.float32
vmem_bytes = 20 * 1024 * 1024


def basis(length):
    half, quarter = length // 2, length // 4
    n = np.arange(half)[:, None]
    j = np.arange(quarter)[None, :]
    scale = math.sqrt(2.0 / length)
    even_cos = scale * np.cos(2 * np.pi * ((2 * j * n) % length) / length)
    even_sin = scale * np.sin(2 * np.pi * ((2 * j * n) % length) / length)
    even_cos[:, 0] = 1.0 / math.sqrt(length)
    even_sin[:, 0] = (1.0 - 2.0 * (np.arange(half) % 2)) / math.sqrt(length)
    odd_cos = scale * np.cos(2 * np.pi * (((2 * j + 1) * n) % length) / length)
    odd_sin = scale * np.sin(2 * np.pi * (((2 * j + 1) * n) % length) / length)
    even = np.concatenate([even_cos, even_sin], 1).astype(np.float32)
    odd = np.concatenate([odd_cos, odd_sin], 1).astype(np.float32)
    return even, odd


def basis_tables(length):
    even, odd = basis(length)
    return jnp.asarray(np.stack([even, odd, even.T, odd.T]), bf16)


def dot(a, b):
    return jnp.dot(a, b, preferred_element_type=f32)


def fitted(function, top, degree):
    fit = np.polynomial.Chebyshev.interpolate(function, degree, [0.0, top])
    return [float(c) for c in fit.convert(kind=np.polynomial.Polynomial).coef]


def horner(coefs, x):
    total = coefs[-1] * x + coefs[-2]
    for c in coefs[-3::-1]:
        total = total * x + c
    return total


def sinc_root(x):
    return np.sinc(np.sqrt(x) / np.pi)


def cos_root(x):
    return np.cos(np.sqrt(x))


lens_top = 0.45
lens_cos, lens_sin = fitted(cos_root, lens_top, 3), fitted(sinc_root, lens_top, 3)
phase_top = 3.2
phase_cos, phase_sin = fitted(cos_root, phase_top, 7), fitted(sinc_root, phase_top, 7)


def small_cos_sin(a):
    s = a * a
    return horner(lens_cos, s), a * horner(lens_sin, s)


def phase_kernel(nx, ny, ints_ref, omega_ref, refs_ref, out_ref):
    qx, qy = nx // 4, ny // 4
    sign = (2 * ints_ref[1] - 1).astype(f32)
    level = omega_ref[ints_ref[3]] * refs_ref[0, 0:1, 0:1]

    def waves(rows, cols, axis, parity, length):
        j = lax.broadcasted_iota(jnp.int32, (rows, cols), axis)
        return (2 * j + parity).astype(f32) * (2.0 * math.pi / length)

    def values(kx, ky):
        squared = level * level - kx * kx - ky * ky
        inside = jnp.maximum(squared, 0.0)
        damping = jnp.exp(-jnp.sqrt(jnp.maximum(-squared, 0.0)))
        sine = jnp.sqrt(inside) * horner(phase_sin, inside)
        return damping * horner(phase_cos, inside), sign * damping * sine

    edge = math.pi
    row_zero = lax.broadcasted_iota(jnp.int32, (qx, qy), 0) == 0
    col_zero = lax.broadcasted_iota(jnp.int32, (qx, qy), 1) == 0
    for px in range(2):
        for py in range(2):
            kx = waves(qx, qy, 0, px, nx)
            ky = waves(qx, qy, 1, py, ny)
            base = values(kx, ky)
            across = values(jnp.full((8, qy), edge), waves(8, qy, 1, py, ny))
            along = values(waves(qx, 1, 0, px, nx), jnp.full((qx, 1), edge))
            corner = values(jnp.full((8, 1), edge), jnp.full((8, 1), edge))
            for sx in range(2):
                for sy in range(2):
                    new_row, new_col = sx and not px, sy and not py
                    for part in range(2):
                        v = base[part]
                        if new_col:
                            v = jnp.where(col_zero, along[part], v)
                        if new_row:
                            v = jnp.where(row_zero, across[part][0:1], v)
                        if new_row and new_col:
                            v = jnp.where(row_zero & col_zero, corner[part][0:1], v)
                        rows = pl.ds((2 * px + sx) * qx, qx)
                        cols = pl.ds((2 * py + sy) * qy, qy)
                        out_ref[0, part, rows, cols] = v.astype(bf16)


def phase_table(nx, ny, ints, omega, refs):
    slots = refs.shape[0]
    return pl.pallas_call(
        partial(phase_kernel, nx, ny),
        out_shape=jax.ShapeDtypeStruct((slots, 2, nx, ny), bf16),
        grid=(slots,),
        in_specs=[
            pl.BlockSpec(memory_space=pltpu.SMEM),
            pl.BlockSpec(memory_space=pltpu.SMEM),
            pl.BlockSpec((1, 8, 128), lambda i: (i, 0, 0)),
        ],
        out_specs=pl.BlockSpec((1, 2, nx, ny), lambda i: (i, 0, 0, 0)),
        compiler_params=pltpu.CompilerParams(vmem_limit_bytes=vmem_bytes),
        name="phase_table",
    )(ints, omega, refs)


def pack_kernel(
    rows_here, hy, ints_ref, ref_ref, source, adjoint, slow_ref, coef_ref, plane, packed, same, other, slow, coef, sems
):
    forward, side, freq = ints_ref[1], ints_ref[2], ints_ref[3]
    slow_copy = pltpu.make_async_copy(slow_ref, slow, sems.at[0])
    coef_copy = pltpu.make_async_copy(coef_ref, coef, sems.at[1])

    @pl.when(forward == 1)
    def _():
        pltpu.make_async_copy(source.at[freq], plane, sems.at[2]).start()

    @pl.when(forward == 0)
    def _():
        pltpu.make_async_copy(adjoint.at[freq], plane, sems.at[2]).start()

    slow_copy.start()
    coef_copy.start()
    slow_copy.wait()
    coef_copy.wait()
    level = jnp.full((16, hy), ref_ref[0], f32)
    high = level.astype(bf16)
    rest = level - high.astype(f32)
    middle = rest.astype(bf16)
    low = (rest - middle.astype(f32)).astype(bf16)
    row = lax.broadcasted_iota(jnp.int32, (16, hy), 0)
    parts = jnp.where(row == 0, high.astype(f32), jnp.where(row == 1, middle.astype(f32), low.astype(f32)))
    parts = parts.astype(bf16)
    for i, alone in enumerate((same, other)):
        cols = pl.ds(pl.multiple_of((side ^ i) * hy, hy), hy)
        c = coef[0, :, cols].astype(bf16)
        d = (slow[0, :, cols] - ref_ref[0]).astype(bf16)
        for out in (packed.at[i], alone):
            out[pl.ds(0, rows_here), :] = c
            out[pl.ds(rows_here, rows_here), :] = d
            out[pl.ds(2 * rows_here, 16), :] = parts
    pltpu.make_async_copy(source.at[freq], plane, sems.at[2]).wait()


def run_pack(ints, slowness_ref, source_top, adjoint_bottom, slowness, correction):
    rows_here, ny = slowness.shape[1:]
    hy = ny // 2
    half = jax.ShapeDtypeStruct((2 * rows_here + 16, hy), bf16)
    return pl.pallas_call(
        partial(pack_kernel, rows_here, hy),
        out_shape=(
            jax.ShapeDtypeStruct((2, rows_here, ny), bf16),
            jax.ShapeDtypeStruct((2,) + half.shape, bf16),
            half,
            half,
        ),
        in_specs=[sm, sm] + [pl.BlockSpec(memory_space=pl.ANY)] * 4,
        out_specs=(vm, vm, vm, vm),
        scratch_shapes=[
            pltpu.VMEM((1, rows_here, ny), f32),
            pltpu.VMEM((1, rows_here, ny), f32),
            pltpu.SemaphoreType.DMA((3,)),
        ],
        compiler_params=pltpu.CompilerParams(vmem_limit_bytes=60 * 1024 * 1024),
        name="pack_rows",
    )(ints, slowness_ref, source_top, adjoint_bottom, slowness, correction)


def sort_kernel(rows_here, hy, sections, ints_ref, *refs):
    blocks, (early, late, refs_out, coef_rows, ends) = refs[:sections], refs[sections:]
    forward, side, group = ints_ref[1], ints_ref[2], ints_ref[4]
    half_sections = sections // 2

    def block_of(k):
        return blocks[k].at[k % 2] if k < half_sections else blocks[k]

    def chosen(index, body):
        for k in range(sections):
            pl.when(index == k)(partial(body, k))

    for slot in range(sections - 1):
        depth = jnp.where(forward == 1, slot, sections - 1 - slot)

        def place(k, slot=slot):
            block = block_of(k)
            for j in range(2):
                out = early.at[j, 0] if slot == 0 else late.at[j, slot - 1]
                out[...] = block[pl.ds(j * rows_here, rows_here), :]

        chosen(group ^ depth, place)
    for slot in range(sections):
        depth = jnp.where(forward == 1, slot, (sections - slot) % sections)

        def level(k, slot=slot):
            parts = block_of(k)[pl.ds(2 * rows_here, 16), pl.ds(0, 128)].astype(f32)
            refs_out[slot] = jnp.broadcast_to(parts[0:1] + parts[1:2] + parts[2:3], (8, 128))

        chosen(group ^ depth, level)

    for k in range(half_sections):

        @pl.when(jnp.clip(group ^ (sections - 1), 0, half_sections - 1) == k)
        def _(k=k):
            for i in range(2):
                cols = pl.ds(pl.multiple_of((side ^ (k % 2) ^ i) * hy, hy), hy)
                block = blocks[k].at[i]
                for j in range(2):
                    part = block[pl.ds(j * rows_here, rows_here), :]
                    coef_rows[j, :, cols] = part
                    ends[0, j, :, cols] = part[rows_here - 1 :]
                    ends[1, j, :, cols] = part[:1]


def run_sort(ints, blocks, rows_here, hy):
    sections = len(blocks)
    return pl.pallas_call(
        partial(sort_kernel, rows_here, hy, sections),
        out_shape=(
            jax.ShapeDtypeStruct((2, 1, rows_here, hy), bf16),
            jax.ShapeDtypeStruct((2, sections - 2, rows_here, hy), bf16),
            jax.ShapeDtypeStruct((sections, 8, 128), f32),
            jax.ShapeDtypeStruct((2, rows_here, 2 * hy), bf16),
            jax.ShapeDtypeStruct((2, 2, 1, 2 * hy), bf16),
        ),
        in_specs=[sm] + [vm] * sections,
        out_specs=(vm, vm, vm, vm, vm),
        compiler_params=pltpu.CompilerParams(vmem_limit_bytes=vmem_bytes),
        name="sort_depths",
    )(ints, *blocks)


vm = pl.BlockSpec(memory_space=pltpu.VMEM)
sm = pl.BlockSpec(memory_space=pltpu.SMEM)


def fold_cols(values):
    half = values.shape[1] // 2
    a, b = values[:, :half], values[:, half:]
    return (a + b).astype(bf16), (a - b).astype(bf16)


def transform(nx, ny, folded, phase, qx_ref, qy_ref, mid, spec, out):
    hx, hy = nx // 2, ny // 2
    step = min(128, hx)
    for part in range(2):
        for start in range(0, hx, step):
            top, low = pl.ds(start, step), pl.ds(hx + start, step)
            for par in range(2):
                cols = pl.ds(par * hy, hy)
                a = dot(folded[part, top, cols], qy_ref[par])
                b = dot(folded[part, low, cols], qy_ref[par])
                mid[part, top, cols] = (a + b).astype(bf16)
                mid[part, low, cols] = (a - b).astype(bf16)
    for start in range(0, ny, hy):
        cols = pl.ds(start, hy)
        back = []
        for par in range(2):
            rows = pl.ds(par * hx, hx)
            zr = dot(qx_ref[2 + par], mid[0, rows, cols])
            zi = dot(qx_ref[2 + par], mid[1, rows, cols])
            pr = phase[0, 0, rows, cols].astype(f32)
            pi = phase[0, 1, rows, cols].astype(f32)
            yr = (zr * pr - zi * pi).astype(bf16)
            yi = (zr * pi + zi * pr).astype(bf16)
            back.append((dot(qx_ref[par], yr), dot(qx_ref[par], yi)))
        for part in range(2):
            a, b = back[0][part], back[1][part]
            spec[part, pl.ds(0, hx), cols] = (a + b).astype(bf16)
            spec[part, pl.ds(hx, hx), cols] = (a - b).astype(bf16)
    for part in range(2):
        for start in range(0, nx, 2 * step):
            rows = pl.ds(start, 2 * step)
            a = dot(spec[part, rows, pl.ds(0, hy)], qy_ref[2])
            b = dot(spec[part, rows, pl.ds(hy, hy)], qy_ref[3])
            out[part, rows, pl.ds(0, hy)] = (a + b).astype(bf16)
            out[part, rows, pl.ds(hy, hy)] = (a - b).astype(bf16)


def first_kernel(dims, orders, ints_ref, phase, qx_ref, qy_ref, *rest):
    nx, ny, rows_here = dims
    counts = [len(o) for o in orders]
    pieces, (out, folded, mid, spec) = rest[: sum(counts)], rest[sum(counts) :]
    part_id, forward = ints_ref[0], ints_ref[1]
    at = 0
    for part, order in enumerate(orders):
        for piece_order in order:
            piece = pieces[at]
            at += 1
            for i, offset in enumerate(piece_order):
                block = part_id ^ offset
                rows = pl.ds(pl.multiple_of(block * rows_here, rows_here), rows_here)
                values = piece[i]

                @pl.when(forward == 1)
                def _():
                    a, b = fold_cols(values.astype(f32))
                    folded[part, rows, pl.ds(0, ny // 2)] = a
                    folded[part, rows, pl.ds(ny // 2, ny // 2)] = b

                @pl.when(forward == 0)
                def _():
                    out[part, rows, :] = values

    @pl.when(forward == 1)
    def _():
        transform(nx, ny, folded, phase, qx_ref, qy_ref, mid, spec, out)


def laplace_rows(ref, part, start, count):
    center = ref[part, pl.ds(start + 8, count), :]
    width = center.shape[1]
    return (
        ref[part, pl.ds(start + 7, count), :]
        + ref[part, pl.ds(start + 9, count), :]
        + pltpu.roll(center, 1, 1)
        + pltpu.roll(center, width - 1, 1)
        - 4.0 * center
    )


def wrap_rows(ref, nx):
    for part in range(2):
        ref[part, pl.ds(7, 1), :] = ref[part, pl.ds(nx + 7, 1), :]
        ref[part, pl.ds(nx + 8, 1), :] = ref[part, pl.ds(8, 1), :]


def step_kernel(dims, orders, slot, last, ints_ref, omega_ref, w_ref, phase, qx_ref, qy_ref, *rest):
    nx, ny, rows_here = dims
    count = sum(len(o) for o in orders)
    coefs, rest = (rest[:count], rest[count : 2 * count]), rest[2 * count :]
    if last:
        coef_rows, before_row, after_row, out_rows, end_rows, out, plane, halo, folded, mid, spec, tall = rest
    else:
        out, out_rows, plane, halo, folded, mid, spec = rest
    part_id, forward, side = ints_ref[0], ints_ref[1], ints_ref[2]
    omega = omega_ref[ints_ref[3]]
    hy = ny // 2
    blocks = nx // rows_here
    place = []
    at = 0
    for order in orders:
        where = {}
        for piece_order in order:
            for i, offset in enumerate(piece_order):
                where[offset] = (at, i)
            at += 1
        place.append(where)
    step = min(32, rows_here)

    def portions():
        for offset in range(blocks):
            for sub in range(0, rows_here, step):
                start = pl.multiple_of((part_id ^ offset) * rows_here + sub, step)
                yield offset, sub, start

    def lens_at(q, offset, sub):
        cols = pl.ds(pl.multiple_of((side ^ q) * hy, hy), hy)
        (ca, ci), (da, di) = place[0][offset], place[1][offset]
        rows = pl.ds(sub, step)
        c = coefs[q][ca][ci, slot, rows, :].astype(f32)
        cos, sin = small_cos_sin(omega * coefs[q][da][di, slot, rows, :].astype(f32))
        return cols, c, cos, sin

    chunk = 32

    @pl.when(forward == 1)
    def _():
        for offset, sub, start in portions():
            rows, shifted = pl.ds(start, step), pl.ds(start + 8, step)
            for q in range(2):
                cols, c, lr, li = lens_at(q, offset, sub)
                wr, wi = w_ref[0, rows, cols].astype(f32), w_ref[1, rows, cols].astype(f32)
                ur, ui = wr * lr - wi * li, wr * li + wi * lr
                plane[0, rows, cols] = ur
                plane[1, rows, cols] = ui
                halo[0, shifted, cols] = c * ur
                halo[1, shifted, cols] = c * ui
        wrap_rows(halo, nx)
        for start in range(0, nx, chunk):
            rows = pl.ds(start, chunk)
            ur = plane[0, rows, :] - laplace_rows(halo, 1, start, chunk)
            ui = plane[1, rows, :] + laplace_rows(halo, 0, start, chunk)
            for part, u in enumerate((ur, ui)):
                mid[part, rows, :] = u.astype(bf16)
                a, b = fold_cols(u)
                folded[part, rows, pl.ds(0, hy)] = a
                folded[part, rows, pl.ds(hy, hy)] = b
        mine = pl.ds(pl.multiple_of(part_id * rows_here, rows_here), rows_here)
        for part in range(2):
            out_rows[part] = mid[part, mine, :]

    @pl.when(forward == 0)
    def _():
        for part in range(2):
            halo[part, pl.ds(8, nx), :] = w_ref[part].astype(f32)
        wrap_rows(halo, nx)
        for start in range(0, nx, chunk):
            for part in range(2):
                plane[part, pl.ds(start, chunk), :] = laplace_rows(halo, part, start, chunk)
        flip = (1 - 2 * side).astype(f32)
        for offset, sub, start in portions():
            rows = pl.ds(start, step)
            shifted = pl.ds(start + 8, step)
            halves = []
            for q in range(2):
                cols, c, lr, li = lens_at(q, offset, sub)
                tr = halo[0, shifted, cols] + c * plane[1, rows, cols]
                ti = halo[1, shifted, cols] - c * plane[0, rows, cols]
                halves.append((tr * lr + ti * li, ti * lr - tr * li))
            for part in range(2):
                a, b = halves[0][part], halves[1][part]
                folded[part, rows, pl.ds(0, hy)] = (a + b).astype(bf16)
                folded[part, rows, pl.ds(hy, hy)] = (flip * (a - b)).astype(bf16)

    transform(nx, ny, folded, phase, qx_ref, qy_ref, mid, spec, out)
    first = pl.multiple_of(part_id * rows_here, rows_here)
    mine = pl.ds(first, rows_here)

    @pl.when(forward == 0)
    def _():
        for part in range(2):
            out_rows[part] = out[part, mine, :]

    if not last:
        return

    @pl.when(forward == 0)
    def _():
        end_rows[...] = jnp.zeros_like(end_rows)

    @pl.when(forward == 1)
    def _():
        before = pl.ds(pl.multiple_of(lax.rem(first + nx - 16, nx), 16), 16)
        after = pl.ds(pl.multiple_of(lax.rem(first + rows_here, nx), 16), 16)

        def scaled(values, c, d):
            lr, li = small_cos_sin(omega * d.astype(f32))
            wr, wi = values[0].astype(f32), values[1].astype(f32)
            ur, ui = wr * lr - wi * li, wr * li + wi * lr
            cf = c.astype(f32)
            return ur, ui, cf * ur, cf * ui

        ur, ui, gr, gi = scaled(
            (out[0, mine, :], out[1, mine, :]), coef_rows[0], coef_rows[1]
        )
        tall[0, pl.ds(8, rows_here), :] = gr
        tall[1, pl.ds(8, rows_here), :] = gi
        _, _, gr, gi = scaled(
            (out[0, before, :][15:16], out[1, before, :][15:16]), before_row[0], before_row[1]
        )
        tall[0, pl.ds(7, 1), :] = gr
        tall[1, pl.ds(7, 1), :] = gi
        _, _, gr, gi = scaled(
            (out[0, after, :][0:1], out[1, after, :][0:1]), after_row[0], after_row[1]
        )
        tall[0, pl.ds(rows_here + 8, 1), :] = gr
        tall[1, pl.ds(rows_here + 8, 1), :] = gi
        end_rows[0] = (ur - laplace_rows(tall, 1, 0, rows_here)).astype(bf16)
        end_rows[1] = (ui + laplace_rows(tall, 0, 0, rows_here)).astype(bf16)


def phase_spec(slot, nx, ny):
    return pl.BlockSpec((1, 2, nx, ny), lambda i: (slot, 0, 0, 0))


def run_first(dims, orders, ints, phases, qx, qy, pieces):
    nx, ny, _ = dims
    return pl.pallas_call(
        partial(first_kernel, dims, orders),
        out_shape=jax.ShapeDtypeStruct((2, nx, ny), bf16),
        grid=(1,),
        in_specs=[sm, phase_spec(0, nx, ny), vm, vm] + [vm] * len(pieces),
        out_specs=vm,
        scratch_shapes=[pltpu.VMEM((2, nx, ny), bf16)] * 3,
        compiler_params=pltpu.CompilerParams(vmem_limit_bytes=vmem_bytes),
        cost_estimate=pl.CostEstimate(flops=2**30, bytes_accessed=2**22, transcendentals=0),
        name="first_step",
    )(ints, phases, qx, qy, *pieces)


def run_step(dims, orders, slot, index, ints, omega, w, coefs, phases, qx, qy, ends=None):
    nx, ny, rows_here = dims
    last = ends is not None
    rows_shape = jax.ShapeDtypeStruct((2, rows_here, ny), bf16)
    full = pltpu.VMEM((2, nx, ny), bf16)
    scratch = [pltpu.VMEM((2, nx, ny), f32), pltpu.VMEM((2, nx + 16, ny), f32), full, full, full]
    if last:
        outs = (rows_shape, rows_shape)
        scratch = [full] + scratch + [pltpu.VMEM((2, rows_here + 16, ny), f32)]
    else:
        outs = (jax.ShapeDtypeStruct((2, nx, ny), bf16), rows_shape)
    return pl.pallas_call(
        partial(step_kernel, dims, orders, index, last),
        out_shape=outs,
        grid=(1,),
        in_specs=[sm, sm, vm, phase_spec(slot + 1, nx, ny), vm, vm]
        + [vm] * (len(coefs) + (3 if last else 0)),
        out_specs=(vm, vm),
        scratch_shapes=scratch,
        compiler_params=pltpu.CompilerParams(vmem_limit_bytes=vmem_bytes),
        cost_estimate=pl.CostEstimate(flops=2**32, bytes_accessed=2**24, transcendentals=0),
        name="end_step" if last else "depth_step",
    )(ints, omega, w, phases, qx, qy, *coefs, *(ends or ()))


def image_kernel(freq_count, last_group, ints_ref, omega_ref, *refs):
    fields, (bottom, out) = refs[:-2], refs[-2:]
    forward, freq, group = ints_ref[1], ints_ref[3], ints_ref[4]

    def total(adjoint_at):
        result = None
        for i in range(freq_count):
            freq_i = freq ^ i
            adjoint = adjoint_at(i, freq_i)
            a = [fields[i][j].astype(f32) for j in range(2)]
            b = [adjoint[j].astype(f32) for j in range(2)]
            weight = omega_ref[freq_i] * (2 * forward - 1).astype(f32)
            term = weight * (a[0] * b[1] - a[1] * b[0])
            result = term if result is None else result + term
        out[0] = result

    @pl.when(group == last_group)
    def _():
        total(lambda i, freq_i: bottom.at[freq_i])

    @pl.when(group != last_group)
    def _():
        total(lambda i, freq_i: fields[freq_count + i])


def run_image(ints, omega, sections, fields, bottom):
    _, rows_here, ny = fields[0].shape
    return pl.pallas_call(
        partial(image_kernel, omega.shape[0], sections - 1),
        out_shape=jax.ShapeDtypeStruct((1, rows_here, ny), f32),
        in_specs=[sm, sm] + [vm] * (len(fields) + 1),
        out_specs=vm,
        compiler_params=pltpu.CompilerParams(vmem_limit_bytes=vmem_bytes),
        name="image",
    )(ints, omega, *fields, bottom)


def swap(values, axis, mask):
    size = lax.axis_size(axis)
    return lax.ppermute(values, axis, [(i, i ^ mask) for i in range(size)])


def doubling_masks(size):
    masks = []
    mask = size // 2
    while mask:
        masks.append(mask)
        mask //= 2
    descending = masks
    ascending = masks[:1] + masks[1:][::-1]
    return descending, ascending


def doubling_orders(masks):
    orders = [[0]]
    seen = [0]
    for mask in masks:
        new = [mask ^ o for o in seen]
        orders.append(new)
        seen = seen + new
    return orders


def first_exchange(pair, axis):
    size = lax.axis_size(axis)
    got = swap(pair, axis, size // 2)
    return [[pair[0:1], got[0:1]], [pair[1:2], got[1:2]]]


def after(values, earlier):
    return lax.optimization_barrier((values, earlier))[0]


def next_exchange(pieces, axis, level):
    masks = doubling_masks(lax.axis_size(axis))
    return [
        have + [swap(jnp.concatenate(have, 0), axis, masks[which][level])]
        for which, have in enumerate(pieces)
    ]


def per_device(source_top, adjoint_bottom, slowness, correction, slowness_ref, omega):
    row_parts = lax.axis_size("rows")
    sections = lax.axis_size("depth")
    group = lax.axis_index("depth")
    part_id = lax.axis_index("rows")
    freq_count = omega.shape[0]
    chains = 2 * freq_count
    rep = sections // chains
    rows_here, ny = slowness.shape[1:]
    nx = rows_here * row_parts
    dims = (nx, ny, rows_here)
    hy = ny // 2
    chain = lax.div(group, rep)
    forward = lax.div(chain, freq_count)
    freq = lax.rem(chain, freq_count)
    side = lax.rem(group, 2)
    half_sections = sections // 2
    masks = doubling_masks(row_parts)
    orders = [doubling_orders(m) for m in masks]
    rounds = len(masks[0])
    ints = jnp.stack([part_id, forward, side, freq, group]).astype(jnp.int32)

    def pick(values, index):
        return lax.dynamic_index_in_dim(values, index, 0, keepdims=False)

    plane, packed, same, other = run_pack(
        ints, slowness_ref, source_top, adjoint_bottom, slowness, correction
    )
    planes = first_exchange(plane, "rows")
    blocks = [packed]
    for k in range(1, sections):
        blocks.append(swap(packed if k < half_sections else (same, other)[k % 2], "depth", k))
    early, late, refs, coef_rows, ends = run_sort(ints, blocks, rows_here, hy)
    early = first_exchange(early, "rows")
    late = first_exchange(late, "rows")
    phases = phase_table(nx, ny, ints, omega, refs)
    rows_up = [(i, (i + 1) % row_parts) for i in range(row_parts)]
    rows_down = [(j, i) for i, j in rows_up]
    edges = [lax.ppermute(ends[0], "rows", rows_up), lax.ppermute(ends[1], "rows", rows_down)]

    def both_sides(pieces, earlier):
        mine, theirs = [], []
        for have in pieces:
            mine += have
            theirs += [swap(piece, "depth", 1) for piece in have[:-1]]
            theirs.append(swap(after(have[-1], earlier), "depth", 1))
        return mine + theirs

    qx, qy = basis_tables(nx), basis_tables(ny)
    for level in range(1, rounds):
        planes = next_exchange(planes, "rows", level)
        early = after(early, (planes, (phases, edges)) if level == rounds - 1 else planes)
        early = next_exchange(early, "rows", level)
        if level < rounds - 1:
            late = next_exchange(after(late, early), "rows", level)
    w = run_first(dims, orders, ints, phases, qx, qy, planes[0] + planes[1])
    late = next_exchange(after(late, w), "rows", rounds - 1)
    coefs = both_sides(early, w)

    row_outs = []
    for slot in range(sections - 1):
        ends = (coef_rows, *edges) if slot == sections - 2 else None
        first, second = run_step(dims, orders, slot, max(slot - 1, 0), ints, omega, w, coefs, phases, qx, qy, ends)
        if ends is None:
            w = first
            row_outs.append(second)
            if slot == 0:
                coefs = both_sides(late, w)
        else:
            row_outs += [first, second]

    def index_for(g, target):
        return target if g >= half_sections else sections - 2 - target

    def payload_for(mask):
        used = sorted(
            {index_for(g, g ^ mask) for g in range(sections) if index_for(g, g ^ mask) >= 0}
        )
        low = used[0]
        stack = jnp.stack(row_outs[low : used[-1] + 1])
        target = group ^ mask
        index = jnp.where(forward == 1, target, sections - 2 - target)
        return pick(stack, jnp.clip(index - low, 0, len(stack) - 1))

    far = [swap(payload_for(i * rep), "depth", i * rep) for i in range(freq_count, chains)]
    near = [payload_for(i * rep) for i in range(freq_count)]
    far, near = lax.optimization_barrier((far, near))
    fields = [f if i == 0 else swap(f, "depth", i * rep) for i, f in enumerate(near)] + far
    return run_image(ints, omega, sections, fields, adjoint_bottom)


def solution(mesh):
    in_specs = (
        P(None, None, "rows", None),
        P(None, None, "rows", None),
        P("depth", "rows", None),
        P("depth", "rows", None),
        P("depth"),
        P(),
    )
    out_specs = P("depth", "rows", None)
    return jax.shard_map(
        per_device, mesh=mesh, in_specs=in_specs, out_specs=out_specs, check_vma=False
    )
```

```python
from functools import partial
import math

import jax
import jax.numpy as jnp
import numpy as np
from jax import lax
from jax.experimental import pallas as pl
from jax.experimental.pallas import tpu as pltpu
from jax.sharding import PartitionSpec as P

bf16 = jnp.bfloat16
f32 = jnp.float32
vmem_bytes = 48 * 1024 * 1024


def basis(length):
    half, quarter = length // 2, length // 4
    n = np.arange(half)[:, None]
    j = np.arange(quarter)[None, :]
    scale = math.sqrt(2.0 / length)
    even_cos = scale * np.cos(2 * np.pi * ((2 * j * n) % length) / length)
    even_sin = scale * np.sin(2 * np.pi * ((2 * j * n) % length) / length)
    even_cos[:, 0] = 1.0 / math.sqrt(length)
    even_sin[:, 0] = (1.0 - 2.0 * (np.arange(half) % 2)) / math.sqrt(length)
    odd_cos = scale * np.cos(2 * np.pi * (((2 * j + 1) * n) % length) / length)
    odd_sin = scale * np.sin(2 * np.pi * (((2 * j + 1) * n) % length) / length)
    even = np.concatenate([even_cos, even_sin], 1).astype(np.float32)
    odd = np.concatenate([odd_cos, odd_sin], 1).astype(np.float32)
    return even, odd


def basis_tables(length):
    even, odd = basis(length)
    return jnp.asarray(np.stack([even, odd, even.T, odd.T]), bf16)


def dot(a, b):
    return jnp.dot(a, b, preferred_element_type=f32)


def fitted(function, top, degree):
    fit = np.polynomial.Chebyshev.interpolate(function, degree, [0.0, top])
    return [float(c) for c in fit.convert(kind=np.polynomial.Polynomial).coef]


def horner(coefs, x):
    total = coefs[-1] * x + coefs[-2]
    for c in coefs[-3::-1]:
        total = total * x + c
    return total


def sinc_root(x):
    return np.sinc(np.sqrt(x) / np.pi)


def cos_root(x):
    return np.cos(np.sqrt(x))


lens_top = 0.45
lens_cos, lens_sin = fitted(cos_root, lens_top, 3), fitted(sinc_root, lens_top, 3)
phase_top = 3.2
phase_cos, phase_sin = fitted(cos_root, phase_top, 7), fitted(sinc_root, phase_top, 7)


def small_cos_sin(a):
    s = a * a
    return horner(lens_cos, s), a * horner(lens_sin, s)


def fill_phase(nx, ny, level, sign, out):
    qx, qy = nx // 4, ny // 4

    def waves(rows, cols, axis, parity, length):
        j = lax.broadcasted_iota(jnp.int32, (rows, cols), axis)
        return (2 * j + parity).astype(f32) * (2.0 * math.pi / length)

    def values(kx, ky):
        squared = level * level - kx * kx - ky * ky
        inside = jnp.maximum(squared, 0.0)
        damping = jnp.exp(-jnp.sqrt(jnp.maximum(-squared, 0.0)))
        sine = jnp.sqrt(inside) * horner(phase_sin, inside)
        return damping * horner(phase_cos, inside), sign * damping * sine

    edge = math.pi
    row_zero = lax.broadcasted_iota(jnp.int32, (qx, qy), 0) == 0
    col_zero = lax.broadcasted_iota(jnp.int32, (qx, qy), 1) == 0
    for px in range(2):
        for py in range(2):
            kx = waves(qx, qy, 0, px, nx)
            ky = waves(qx, qy, 1, py, ny)
            base = values(kx, ky)
            across = values(jnp.full((8, qy), edge), waves(8, qy, 1, py, ny))
            along = values(waves(qx, 1, 0, px, nx), jnp.full((qx, 1), edge))
            corner = values(jnp.full((8, 1), edge), jnp.full((8, 1), edge))
            for sx in range(2):
                for sy in range(2):
                    new_row, new_col = sx and not px, sy and not py
                    for part in range(2):
                        v = base[part]
                        if new_col:
                            v = jnp.where(col_zero, along[part], v)
                        if new_row:
                            v = jnp.where(row_zero, across[part][0:1], v)
                        if new_row and new_col:
                            v = jnp.where(row_zero & col_zero, corner[part][0:1], v)
                        rows = pl.ds((2 * px + sx) * qx, qx)
                        cols = pl.ds((2 * py + sy) * qy, qy)
                        out[part, rows, cols] = v.astype(bf16)


def sort_kernel(rows_here, hy, sections, ints_ref, *refs):
    blocks, (pair, refs_out, coef_rows) = refs[:sections], refs[sections:]
    forward, side, group = ints_ref[1], ints_ref[2], ints_ref[4]
    half_sections = sections // 2

    def block_of(k):
        return blocks[k].at[k % 2] if k < half_sections else blocks[k]

    def chosen(index, body):
        for k in range(sections):
            pl.when(index == k)(partial(body, k))

    for slot in range(half_sections):
        depth = jnp.where(forward == 1, slot, sections - 1 - slot)

        def place(k, slot=slot):
            block = block_of(k)
            for j in range(2):
                pair[j, slot] = block[pl.ds(j * rows_here, rows_here), :]

        chosen(group ^ depth, place)
    for slot in range(sections):
        depth = jnp.where(forward == 1, slot, (sections - slot) % sections)

        def level(k, slot=slot):
            parts = block_of(k)[pl.ds(2 * rows_here, 16), pl.ds(0, 128)].astype(f32)
            refs_out[slot] = jnp.broadcast_to(parts[0:1] + parts[1:2] + parts[2:3], (8, 128))

        chosen(group ^ depth, level)

    for k in range(half_sections):

        @pl.when(jnp.clip(group ^ (sections - 1), 0, half_sections - 1) == k)
        def _(k=k):
            for i in range(2):
                cols = pl.ds(pl.multiple_of((side ^ (k % 2) ^ i) * hy, hy), hy)
                block = blocks[k].at[i]
                for j in range(2):
                    part = block[pl.ds(j * rows_here, rows_here), :]
                    coef_rows[j, :, cols] = part


def run_sort(ints, blocks, rows_here, hy):
    sections = len(blocks)
    return pl.pallas_call(
        partial(sort_kernel, rows_here, hy, sections),
        out_shape=(
            jax.ShapeDtypeStruct((2, sections // 2, rows_here, hy), bf16),
            jax.ShapeDtypeStruct((sections, 8, 128), f32),
            jax.ShapeDtypeStruct((2, rows_here, 2 * hy), bf16),
        ),
        in_specs=[sm] + [vm] * sections,
        out_specs=(vm, vm, vm),
        compiler_params=pltpu.CompilerParams(vmem_limit_bytes=vmem_bytes),
        name="sort_depths",
    )(ints, *blocks)


vm = pl.BlockSpec(memory_space=pltpu.VMEM)
sm = pl.BlockSpec(memory_space=pltpu.SMEM)


def fold_cols(values):
    half = values.shape[1] // 2
    a, b = values[:, :half], values[:, half:]
    return (a + b).astype(bf16), (a - b).astype(bf16)


def transform(nx, ny, folded, phase, qx_ref, qy_ref, mid, spec, out):
    hx, hy = nx // 2, ny // 2
    step = min(128, hx)
    for part in range(2):
        for start in range(0, hx, step):
            top, low = pl.ds(start, step), pl.ds(hx + start, step)
            for par in range(2):
                cols = pl.ds(par * hy, hy)
                a = dot(folded[part, top, cols], qy_ref[par])
                b = dot(folded[part, low, cols], qy_ref[par])
                mid[part, top, cols] = (a + b).astype(bf16)
                mid[part, low, cols] = (a - b).astype(bf16)
    for start in range(0, ny, hy):
        cols = pl.ds(start, hy)
        back = []
        for par in range(2):
            rows = pl.ds(par * hx, hx)
            zr = dot(qx_ref[2 + par], mid[0, rows, cols])
            zi = dot(qx_ref[2 + par], mid[1, rows, cols])
            pr = phase[0, rows, cols].astype(f32)
            pi = phase[1, rows, cols].astype(f32)
            yr = (zr * pr - zi * pi).astype(bf16)
            yi = (zr * pi + zi * pr).astype(bf16)
            back.append((dot(qx_ref[par], yr), dot(qx_ref[par], yi)))
        for part in range(2):
            a, b = back[0][part], back[1][part]
            spec[part, pl.ds(0, hx), cols] = (a + b).astype(bf16)
            spec[part, pl.ds(hx, hx), cols] = (a - b).astype(bf16)
    for part in range(2):
        for start in range(0, nx, 2 * step):
            rows = pl.ds(start, 2 * step)
            a = dot(spec[part, rows, pl.ds(0, hy)], qy_ref[2])
            b = dot(spec[part, rows, pl.ds(hy, hy)], qy_ref[3])
            out[part, rows, pl.ds(0, hy)] = (a + b).astype(bf16)
            out[part, rows, pl.ds(hy, hy)] = (a - b).astype(bf16)


def first_kernel(dims, orders, ints_ref, omega_ref, refs_ref, qx_ref, qy_ref, *rest):
    nx, ny, rows_here = dims
    counts = [len(o) for o in orders]
    pieces, (out, folded, mid, spec, phase) = rest[: sum(counts)], rest[sum(counts) :]
    part_id, forward = ints_ref[0], ints_ref[1]
    at = 0
    for part, order in enumerate(orders):
        for piece_order in order:
            piece = pieces[at]
            at += 1
            for i, offset in enumerate(piece_order):
                block = part_id ^ offset
                rows = pl.ds(pl.multiple_of(block * rows_here, rows_here), rows_here)
                values = piece[i]

                @pl.when(forward == 1)
                def _():
                    a, b = fold_cols(values.astype(f32))
                    folded[part, rows, pl.ds(0, ny // 2)] = a
                    folded[part, rows, pl.ds(ny // 2, ny // 2)] = b

                @pl.when(forward == 0)
                def _():
                    out[part, rows, :] = values

    @pl.when(forward == 1)
    def _():
        level = omega_ref[ints_ref[3]] * refs_ref[0, 0:1, 0:1]
        fill_phase(nx, ny, level, 1.0, phase)
        transform(nx, ny, folded, phase, qx_ref, qy_ref, mid, spec, out)


def laplace_rows(ref, part, start, count):
    center = ref[part, pl.ds(start + 8, count), :]
    width = center.shape[1]
    return (
        ref[part, pl.ds(start + 7, count), :]
        + ref[part, pl.ds(start + 9, count), :]
        + pltpu.roll(center, 1, 1)
        + pltpu.roll(center, width - 1, 1)
        - 4.0 * center
    )


def wrap_rows(ref, nx):
    for part in range(2):
        ref[part, pl.ds(7, 1), :] = ref[part, pl.ds(nx + 7, 1), :]
        ref[part, pl.ds(nx + 8, 1), :] = ref[part, pl.ds(8, 1), :]


def step_kernel(dims, orders, index, edges, last, ints_ref, omega_ref, w_ref, refs_ref, qx_ref, qy_ref, *rest):
    nx, ny, rows_here = dims
    coefs, rest = rest[:2], rest[2:]
    if last:
        coef_rows, edge_rows, out_rows, end_rows, out, plane, halo, folded, mid, spec, phase, tall = rest
    elif edges:
        out, out_rows, edge_out, plane, halo, folded, mid, spec, phase = rest
    else:
        out, out_rows, plane, halo, folded, mid, spec, phase = rest
    part_id, forward, side = ints_ref[0], ints_ref[1], ints_ref[2]
    omega = omega_ref[ints_ref[3]]
    hy = ny // 2
    blocks = nx // rows_here
    place = []
    for which, order in enumerate(orders):
        place.append({offset: which * blocks + i for i, offset in enumerate(sum(order, []))})
    step = min(32, rows_here)

    def portions():
        for offset in range(blocks):
            for sub in range(0, rows_here, step):
                start = pl.multiple_of((part_id ^ offset) * rows_here + sub, step)
                yield offset, sub, start

    def lens_at(q, offset, sub):
        cols = pl.ds(pl.multiple_of((side ^ q) * hy, hy), hy)
        rows = pl.ds(sub, step)
        c = coefs[q][place[0][offset], rows, :].astype(f32)
        cos, sin = small_cos_sin(omega * coefs[q][place[1][offset], rows, :].astype(f32))
        return cols, c, cos, sin

    def keep_edges():
        for i, (beside, first) in enumerate(((blocks - 1, rows_here - 16), (1, 0))):
            wanted = part_id ^ lax.rem(part_id + beside, blocks)
            for j in range(2):
                at = jnp.int32(0)
                for offset in range(blocks):
                    at = jnp.where(wanted == offset, place[j][offset], at)
                for q in range(2):
                    cols = pl.ds(pl.multiple_of((side ^ q) * hy, hy), hy)
                    edge_out[i, j, :, cols] = coefs[q][at, pl.ds(first, 16), :]

    if edges:
        keep_edges()
    chunk = 32

    @pl.when(forward == 1)
    def _():
        for offset, sub, start in portions():
            rows, shifted = pl.ds(start, step), pl.ds(start + 8, step)
            for q in range(2):
                cols, c, lr, li = lens_at(q, offset, sub)
                wr, wi = w_ref[0, rows, cols].astype(f32), w_ref[1, rows, cols].astype(f32)
                ur, ui = wr * lr - wi * li, wr * li + wi * lr
                plane[0, rows, cols] = ur
                plane[1, rows, cols] = ui
                halo[0, shifted, cols] = c * ur
                halo[1, shifted, cols] = c * ui
        wrap_rows(halo, nx)
        for start in range(0, nx, chunk):
            rows = pl.ds(start, chunk)
            ur = plane[0, rows, :] - laplace_rows(halo, 1, start, chunk)
            ui = plane[1, rows, :] + laplace_rows(halo, 0, start, chunk)
            for part, u in enumerate((ur, ui)):
                mid[part, rows, :] = u.astype(bf16)
                a, b = fold_cols(u)
                folded[part, rows, pl.ds(0, hy)] = a
                folded[part, rows, pl.ds(hy, hy)] = b
        mine = pl.ds(pl.multiple_of(part_id * rows_here, rows_here), rows_here)
        for part in range(2):
            out_rows[part] = mid[part, mine, :]

    @pl.when(forward == 0)
    def _():
        for part in range(2):
            halo[part, pl.ds(8, nx), :] = w_ref[part].astype(f32)
        wrap_rows(halo, nx)
        for start in range(0, nx, chunk):
            for part in range(2):
                plane[part, pl.ds(start, chunk), :] = laplace_rows(halo, part, start, chunk)
        flip = (1 - 2 * side).astype(f32)
        for offset, sub, start in portions():
            rows = pl.ds(start, step)
            shifted = pl.ds(start + 8, step)
            halves = []
            for q in range(2):
                cols, c, lr, li = lens_at(q, offset, sub)
                tr = halo[0, shifted, cols] + c * plane[1, rows, cols]
                ti = halo[1, shifted, cols] - c * plane[0, rows, cols]
                halves.append((tr * lr + ti * li, ti * lr - tr * li))
            for part in range(2):
                a, b = halves[0][part], halves[1][part]
                folded[part, rows, pl.ds(0, hy)] = (a + b).astype(bf16)
                folded[part, rows, pl.ds(hy, hy)] = (flip * (a - b)).astype(bf16)

    fill_phase(nx, ny, omega * refs_ref[index + 1, 0:1, 0:1], (2 * forward - 1).astype(f32), phase)
    transform(nx, ny, folded, phase, qx_ref, qy_ref, mid, spec, out)
    first = pl.multiple_of(part_id * rows_here, rows_here)
    mine = pl.ds(first, rows_here)

    @pl.when(forward == 0)
    def _():
        for part in range(2):
            out_rows[part] = out[part, mine, :]

    if not last:
        return

    @pl.when(forward == 0)
    def _():
        end_rows[...] = jnp.zeros_like(end_rows)

    @pl.when(forward == 1)
    def _():
        before = pl.ds(pl.multiple_of(lax.rem(first + nx - 16, nx), 16), 16)
        after = pl.ds(pl.multiple_of(lax.rem(first + rows_here, nx), 16), 16)

        def scaled(values, c, d):
            lr, li = small_cos_sin(omega * d.astype(f32))
            wr, wi = values[0].astype(f32), values[1].astype(f32)
            ur, ui = wr * lr - wi * li, wr * li + wi * lr
            cf = c.astype(f32)
            return ur, ui, cf * ur, cf * ui

        ur, ui, gr, gi = scaled(
            (out[0, mine, :], out[1, mine, :]), coef_rows[0], coef_rows[1]
        )
        tall[0, pl.ds(8, rows_here), :] = gr
        tall[1, pl.ds(8, rows_here), :] = gi
        _, _, gr, gi = scaled(
            (out[0, before, :][15:16], out[1, before, :][15:16]), edge_rows[0, 0, 15:16, :], edge_rows[0, 1, 15:16, :]
        )
        tall[0, pl.ds(7, 1), :] = gr
        tall[1, pl.ds(7, 1), :] = gi
        _, _, gr, gi = scaled(
            (out[0, after, :][0:1], out[1, after, :][0:1]), edge_rows[1, 0, 0:1, :], edge_rows[1, 1, 0:1, :]
        )
        tall[0, pl.ds(rows_here + 8, 1), :] = gr
        tall[1, pl.ds(rows_here + 8, 1), :] = gi
        end_rows[0] = (ur - laplace_rows(tall, 1, 0, rows_here)).astype(bf16)
        end_rows[1] = (ui + laplace_rows(tall, 0, 0, rows_here)).astype(bf16)


def run_first(dims, orders, ints, omega, refs, qx, qy, pieces):
    nx, ny, _ = dims
    return pl.pallas_call(
        partial(first_kernel, dims, orders),
        out_shape=jax.ShapeDtypeStruct((2, nx, ny), bf16),
        in_specs=[sm, sm, vm, vm, vm] + [vm] * len(pieces),
        out_specs=vm,
        scratch_shapes=[pltpu.VMEM((2, nx, ny), bf16)] * 4,
        compiler_params=pltpu.CompilerParams(vmem_limit_bytes=vmem_bytes),
        cost_estimate=pl.CostEstimate(flops=2**30, bytes_accessed=2**22, transcendentals=0),
        name="first_step",
    )(ints, omega, refs, qx, qy, *pieces)


def run_step(dims, orders, index, ints, omega, w, coefs, refs, qx, qy, edges=False, ends=None):
    nx, ny, rows_here = dims
    last = ends is not None
    rows_shape = jax.ShapeDtypeStruct((2, rows_here, ny), bf16)
    full = pltpu.VMEM((2, nx, ny), bf16)
    scratch = [pltpu.VMEM((2, nx, ny), f32), pltpu.VMEM((2, nx + 16, ny), f32)]
    scratch += [full] * 4
    if last:
        outs = (rows_shape, rows_shape)
        scratch = [full] + scratch + [pltpu.VMEM((2, rows_here + 16, ny), f32)]
    else:
        outs = (jax.ShapeDtypeStruct((2, nx, ny), bf16), rows_shape)
        if edges:
            outs += (jax.ShapeDtypeStruct((2, 2, 16, ny), bf16),)
    return pl.pallas_call(
        partial(step_kernel, dims, orders, index, edges, last),
        out_shape=outs,
        in_specs=[sm, sm] + [vm] * (8 if last else 6),
        out_specs=(vm,) * len(outs),
        scratch_shapes=scratch,
        compiler_params=pltpu.CompilerParams(vmem_limit_bytes=vmem_bytes),
        cost_estimate=pl.CostEstimate(flops=2**32, bytes_accessed=2**24, transcendentals=0),
        name="end_step" if last else "depth_step",
    )(ints, omega, w, refs, qx, qy, *coefs, *(ends or ()))


def join_kernel(counts, *refs):
    pieces, outs = refs[: len(counts)], refs[len(counts) :]
    for slot, out in enumerate(outs):
        at = 0
        for piece, count in zip(pieces, counts):
            for i in range(count):
                out[at + i] = piece[i, slot]
            at += count


def run_join(pieces):
    _, slots, rows_here, hy = pieces[0].shape
    counts = [piece.shape[0] for piece in pieces]
    return pl.pallas_call(
        partial(join_kernel, counts),
        out_shape=[jax.ShapeDtypeStruct((sum(counts), rows_here, hy), bf16)] * slots,
        in_specs=[vm] * len(pieces),
        out_specs=[vm] * slots,
        compiler_params=pltpu.CompilerParams(vmem_limit_bytes=vmem_bytes),
        name="join_pieces",
    )(*pieces)


def image_kernel(freq_count, last_group, ints_ref, omega_ref, *refs):
    fields, (bottom, out) = refs[:-2], refs[-2:]
    forward, freq, group = ints_ref[1], ints_ref[3], ints_ref[4]

    def total(adjoint_at):
        result = None
        for i in range(freq_count):
            freq_i = freq ^ i
            adjoint = adjoint_at(i, freq_i)
            a = [fields[i][j].astype(f32) for j in range(2)]
            b = [adjoint[j].astype(f32) for j in range(2)]
            weight = omega_ref[freq_i] * (2 * forward - 1).astype(f32)
            term = weight * (a[0] * b[1] - a[1] * b[0])
            result = term if result is None else result + term
        out[0] = result

    @pl.when(group == last_group)
    def _():
        total(lambda i, freq_i: bottom.at[freq_i])

    @pl.when(group != last_group)
    def _():
        total(lambda i, freq_i: fields[freq_count + i])


def run_image(ints, omega, sections, fields, bottom):
    _, rows_here, ny = fields[0].shape
    return pl.pallas_call(
        partial(image_kernel, omega.shape[0], sections - 1),
        out_shape=jax.ShapeDtypeStruct((1, rows_here, ny), f32),
        in_specs=[sm, sm] + [vm] * (len(fields) + 1),
        out_specs=vm,
        compiler_params=pltpu.CompilerParams(vmem_limit_bytes=vmem_bytes),
        name="image",
    )(ints, omega, *fields, bottom)


def swap(values, axis, mask):
    size = lax.axis_size(axis)
    return lax.ppermute(values, axis, [(i, i ^ mask) for i in range(size)])


def doubling_masks(size):
    masks = []
    mask = size // 2
    while mask:
        masks.append(mask)
        mask //= 2
    descending = masks
    ascending = masks[:1] + masks[1:][::-1]
    return descending, ascending


def doubling_orders(masks):
    orders = [[0]]
    seen = [0]
    for mask in masks:
        new = [mask ^ o for o in seen]
        orders.append(new)
        seen = seen + new
    return orders


def first_exchange(pair, axis):
    size = lax.axis_size(axis)
    got = swap(pair, axis, size // 2)
    return [[pair[0:1], got[0:1]], [pair[1:2], got[1:2]]]


def after(values, earlier):
    return lax.optimization_barrier((values, earlier))[0]


def next_exchange(pieces, axis, level):
    masks = doubling_masks(lax.axis_size(axis))
    return [
        have + [swap(jnp.concatenate(have, 0), axis, masks[which][level])]
        for which, have in enumerate(pieces)
    ]


def per_device(source_top, adjoint_bottom, slowness, correction, slowness_ref, omega):
    row_parts = lax.axis_size("rows")
    sections = lax.axis_size("depth")
    group = lax.axis_index("depth")
    part_id = lax.axis_index("rows")
    freq_count = omega.shape[0]
    chains = 2 * freq_count
    rep = sections // chains
    rows_here, ny = slowness.shape[1:]
    nx = rows_here * row_parts
    dims = (nx, ny, rows_here)
    hy = ny // 2
    chain = lax.div(group, rep)
    forward = lax.div(chain, freq_count)
    freq = lax.rem(chain, freq_count)
    side = lax.rem(group, 2)
    half_sections = sections // 2
    masks = doubling_masks(row_parts)
    orders = [doubling_orders(m) for m in masks]
    rounds = len(masks[0])
    ints = jnp.stack([part_id, forward, side, freq, group]).astype(jnp.int32)

    def pick(values, index):
        return lax.dynamic_index_in_dim(values, index, 0, keepdims=False)

    plane = jnp.where(forward == 1, pick(source_top, freq), pick(adjoint_bottom, freq))
    planes = first_exchange(plane, "rows")
    high = slowness_ref.astype(bf16)
    middle = (slowness_ref - high.astype(f32)).astype(bf16)
    low = (slowness_ref - high.astype(f32) - middle.astype(f32)).astype(bf16)
    terms = jnp.concatenate([high, middle, low, jnp.zeros((13,), bf16)])
    values = jnp.concatenate([correction[0], slowness[0] - slowness_ref[0]], 0).astype(bf16)
    values = jnp.concatenate([values, jnp.broadcast_to(terms[:, None], (16, ny))], 0)
    left, right = values[:, :hy], values[:, hy:]
    same = jnp.where(side == 0, left, right)
    other = jnp.where(side == 0, right, left)
    packed = jnp.stack([same, other])
    blocks = [packed]
    for k in range(1, sections):
        blocks.append(swap(packed if k < half_sections else (same, other)[k % 2], "depth", k))
    pair, refs, coef_rows = run_sort(ints, blocks, rows_here, hy)
    pieces = first_exchange(pair, "rows")
    qx, qy = basis_tables(nx), basis_tables(ny)
    planes = after(planes, pair)
    for level in range(1, rounds):
        planes = next_exchange(planes, "rows", level)
        before = pieces
        pieces = next_exchange(after(pieces, planes), "rows", level)
    w = run_first(dims, orders, ints, omega, refs, qx, qy, after(planes[0] + planes[1], before))
    mine = list(run_join(after(pieces[0] + pieces[1], w)))
    theirs = [swap(m, "depth", 1) for m in mine]
    far = [swap(mine[sections - 1 - slot], "depth", half_sections) for slot in range(half_sections, sections - 1)]
    row_outs = []
    edge_rows = None
    for slot in range(sections - 1):
        ends = (coef_rows, edge_rows) if slot == sections - 2 else None
        w, *rest = run_step(
            dims, orders, slot, ints, omega, w, (mine[slot], theirs[slot]), refs, qx, qy, slot == 0, ends
        )
        if slot == 0:
            edge_rows = swap(rest.pop(), "depth", half_sections)
        if slot == half_sections - 1:
            far = after(far, w)
            mine += far
            theirs += [swap(m, "depth", 1) for m in far]
        if ends:
            rest.insert(0, w)
        row_outs += rest

    def index_for(g, target):
        return target if g >= half_sections else sections - 2 - target

    def payload_for(mask):
        used = sorted(
            {index_for(g, g ^ mask) for g in range(sections) if index_for(g, g ^ mask) >= 0}
        )
        low = used[0]
        stack = jnp.stack(row_outs[low : used[-1] + 1])
        target = group ^ mask
        index = jnp.where(forward == 1, target, sections - 2 - target)
        return pick(stack, jnp.clip(index - low, 0, len(stack) - 1))

    far = [swap(payload_for(i * rep), "depth", i * rep) for i in range(freq_count, chains)]
    near = [payload_for(i * rep) for i in range(freq_count)]
    far, near = lax.optimization_barrier((far, near))
    fields = [f if i == 0 else swap(f, "depth", i * rep) for i, f in enumerate(near)] + far
    return run_image(ints, omega, sections, fields, adjoint_bottom)


def solution(mesh):
    in_specs = (
        P(None, None, "rows", None),
        P(None, None, "rows", None),
        P("depth", "rows", None),
        P("depth", "rows", None),
        P("depth"),
        P(),
    )
    out_specs = P("depth", "rows", None)
    return jax.shard_map(
        per_device, mesh=mesh, in_specs=in_specs, out_specs=out_specs, check_vma=False
    )
```

```python
from functools import partial
import math

import jax
import jax.numpy as jnp
import numpy as np
from jax import lax
from jax.experimental import pallas as pl
from jax.experimental.pallas import tpu as pltpu
from jax.sharding import PartitionSpec as P

bf16 = jnp.bfloat16
f32 = jnp.float32
vmem_bytes = 32 * 1024 * 1024


def basis(length):
    half, quarter = length // 2, length // 4
    n = np.arange(half)[:, None]
    j = np.arange(quarter)[None, :]
    scale = math.sqrt(2.0 / length)
    even_cos = scale * np.cos(2 * np.pi * ((2 * j * n) % length) / length)
    even_sin = scale * np.sin(2 * np.pi * ((2 * j * n) % length) / length)
    even_cos[:, 0] = 1.0 / math.sqrt(length)
    even_sin[:, 0] = (1.0 - 2.0 * (np.arange(half) % 2)) / math.sqrt(length)
    odd_cos = scale * np.cos(2 * np.pi * (((2 * j + 1) * n) % length) / length)
    odd_sin = scale * np.sin(2 * np.pi * (((2 * j + 1) * n) % length) / length)
    even = np.concatenate([even_cos, even_sin], 1).astype(np.float32)
    odd = np.concatenate([odd_cos, odd_sin], 1).astype(np.float32)
    return even, odd


def basis_tables(length):
    even, odd = basis(length)
    half = length // 2
    near = np.eye(half, k=1) + np.eye(half, k=-1)
    across = np.eye(half, k=half - 1) + np.eye(half, k=1 - half)
    tables = [even, odd, even.T, odd.T, near - 4.0 * np.eye(half), near, across]
    return jnp.asarray(np.stack(tables).astype(np.float32), bf16)


def dot(a, b):
    return jnp.dot(a, b, preferred_element_type=f32)


def fitted(function, top, degree):
    fit = np.polynomial.Chebyshev.interpolate(function, degree, [0.0, top])
    return [float(c) for c in fit.convert(kind=np.polynomial.Polynomial).coef]


def horner(coefs, x):
    total = coefs[-1] * x + coefs[-2]
    for c in coefs[-3::-1]:
        total = total * x + c
    return total


def sinc_root(x):
    return np.sinc(np.sqrt(x) / np.pi)


def cos_root(x):
    return np.cos(np.sqrt(x))


lens_top = 0.45
lens_cos, lens_sin = fitted(cos_root, lens_top, 3), fitted(sinc_root, lens_top, 3)
phase_top = 3.2
phase_cos, phase_sin = fitted(cos_root, phase_top, 7), fitted(sinc_root, phase_top, 7)


def small_cos_sin(a):
    s = a * a
    return horner(lens_cos, s), a * horner(lens_sin, s)


def fill_phase(nx, ny, level, sign, out):
    qx, qy = nx // 4, ny // 4

    def waves(rows, cols, axis, parity, length):
        j = lax.broadcasted_iota(jnp.int32, (rows, cols), axis)
        return (2 * j + parity).astype(f32) * (2.0 * math.pi / length)

    def values(kx, ky):
        squared = level * level - kx * kx - ky * ky
        inside = jnp.maximum(squared, 0.0)
        damping = jnp.exp(-jnp.sqrt(jnp.maximum(-squared, 0.0)))
        sine = jnp.sqrt(inside) * horner(phase_sin, inside)
        return damping * horner(phase_cos, inside), sign * damping * sine

    edge = math.pi
    row_zero = lax.broadcasted_iota(jnp.int32, (qx, qy), 0) == 0
    col_zero = lax.broadcasted_iota(jnp.int32, (qx, qy), 1) == 0
    for px in range(2):
        for py in range(2):
            kx = waves(qx, qy, 0, px, nx)
            ky = waves(qx, qy, 1, py, ny)
            base = values(kx, ky)
            across = values(jnp.full((8, qy), edge), waves(8, qy, 1, py, ny))
            along = values(waves(qx, 1, 0, px, nx), jnp.full((qx, 1), edge))
            corner = values(jnp.full((8, 1), edge), jnp.full((8, 1), edge))
            for sx in range(2):
                for sy in range(2):
                    new_row, new_col = sx and not px, sy and not py
                    for part in range(2):
                        v = base[part]
                        if new_col:
                            v = jnp.where(col_zero, along[part], v)
                        if new_row:
                            v = jnp.where(row_zero, across[part][0:1], v)
                        if new_row and new_col:
                            v = jnp.where(row_zero & col_zero, corner[part][0:1], v)
                        rows = pl.ds((2 * px + sx) * qx, qx)
                        cols = pl.ds((2 * py + sy) * qy, qy)
                        out[part, rows, cols] = v.astype(bf16)


def place_of(plan):
    sections, freq_count = plan
    group = lax.axis_index("depth")
    chain = lax.div(group, jnp.int32(sections // (2 * freq_count)))
    forward = lax.div(chain, jnp.int32(freq_count))
    freq = lax.rem(chain, jnp.int32(freq_count))
    return lax.axis_index("rows"), forward, lax.rem(group, jnp.int32(2)), freq, group


vm = pl.BlockSpec(memory_space=pltpu.VMEM)
sm = pl.BlockSpec(memory_space=pltpu.SMEM)


def sort_kernel(rows_here, hy, plan, omega_ref, *refs):
    sections, freq_count = plan
    half_sections = sections // 2
    blocks, refs = refs[:sections], refs[sections:]
    partner, (pair, refs_out, coef_rows) = refs[:half_sections], refs[half_sections:]
    _, forward, side, freq, group = place_of(plan)
    omega = omega_ref[freq]
    for i in range(freq_count):
        refs_out[sections + i] = jnp.full((8, 128), omega_ref[freq ^ i], f32)

    def block_of(k):
        return blocks[k].at[k % 2] if k < half_sections else blocks[k]

    def chosen(index, first, body):
        for k in range(first, sections):
            pl.when(index == k)(partial(body, k))

    for slot in range(half_sections):
        depth = jnp.where(forward == 1, slot, sections - 1 - slot)

        def place(k, slot=slot):
            for j in range(2):
                part = pl.ds(j * rows_here, rows_here)
                pair[j, 0, slot] = blocks[k][part, :]
                pair[j, 1, slot] = partner[k - half_sections][part, :]

        chosen(group ^ depth, half_sections, place)
    for slot in range(sections):
        depth = jnp.where(forward == 1, slot, (sections - slot) % sections)

        def level(k, slot=slot):
            parts = block_of(k)[pl.ds(2 * rows_here, 16), pl.ds(0, 128)].astype(f32)
            refs_out[slot] = jnp.broadcast_to(omega * (parts[0:1] + parts[1:2] + parts[2:3]), (8, 128))

        chosen(group ^ depth, 0, level)

    for k in range(half_sections):

        @pl.when(jnp.clip(group ^ (sections - 1), 0, half_sections - 1) == k)
        def _(k=k):
            for i in range(2):
                cols = pl.ds(pl.multiple_of((side ^ (k % 2) ^ i) * hy, hy), hy)
                block = blocks[k].at[i]
                for j in range(2):
                    coef_rows[j, :, cols] = block[pl.ds(j * rows_here, rows_here), :]


def run_sort(omega, blocks, partner, rows_here, hy):
    sections = len(blocks)
    return pl.pallas_call(
        partial(sort_kernel, rows_here, hy, (sections, omega.shape[0])),
        out_shape=(
            jax.ShapeDtypeStruct((2, 2, sections // 2, rows_here, hy), bf16),
            jax.ShapeDtypeStruct((sections + omega.shape[0], 8, 128), f32),
            jax.ShapeDtypeStruct((2, rows_here, 2 * hy), bf16),
        ),
        in_specs=[sm] + [vm] * (sections + len(partner)),
        out_specs=(vm, vm, vm),
        compiler_params=pltpu.CompilerParams(vmem_limit_bytes=vmem_bytes),
        name="sort_depths",
    )(omega, *blocks, *partner)


def fold_cols(values):
    half = values.shape[1] // 2
    a, b = values[:, :half], values[:, half:]
    return (a + b).astype(bf16), (a - b).astype(bf16)


def add_subtract(mid, part, par, hx, hy, top, low):
    cols = pl.ds(par * hy, hy)
    mid[part, pl.ds(0, hx), cols] = (top + low).astype(bf16)
    mid[part, pl.ds(hx, hx), cols] = (top - low).astype(bf16)


def forward_rows(nx, ny, folded, qy_ref, mid):
    hx, hy = nx // 2, ny // 2
    for part in range(2):
        for par in range(2):
            cols = pl.ds(par * hy, hy)
            top = dot(folded[part, pl.ds(0, hx), cols], qy_ref[par])
            low = dot(folded[part, pl.ds(hx, hx), cols], qy_ref[par])
            add_subtract(mid, part, par, hx, hy, top, low)


def through_columns(nx, ny, mid, phase, qx_ref, spec):
    hx, hy = nx // 2, ny // 2
    for start in range(0, ny, hy):
        cols = pl.ds(start, hy)
        back = []
        for par in range(2):
            rows = pl.ds(par * hx, hx)
            zr = dot(qx_ref[2 + par], mid[0, rows, cols])
            zi = dot(qx_ref[2 + par], mid[1, rows, cols])
            pr = phase[0, rows, cols].astype(f32)
            pi = phase[1, rows, cols].astype(f32)
            yr = (zr * pr - zi * pi).astype(bf16)
            yi = (zr * pi + zi * pr).astype(bf16)
            back.append((dot(qx_ref[par], yr), dot(qx_ref[par], yi)))
        for part in range(2):
            a, b = back[0][part], back[1][part]
            spec[part, pl.ds(0, hx), cols] = (a + b).astype(bf16)
            spec[part, pl.ds(hx, hx), cols] = (a - b).astype(bf16)


def inverse_rows(ny, pieces, spec, qy_ref, out):
    hy = ny // 2
    for part in range(2):
        for start, count in pieces:
            rows = pl.ds(start, count)
            a = dot(spec[part, rows, pl.ds(0, hy)], qy_ref[2])
            b = dot(spec[part, rows, pl.ds(hy, hy)], qy_ref[3])
            out[part, rows, pl.ds(0, hy)] = (a + b).astype(bf16)
            out[part, rows, pl.ds(hy, hy)] = (a - b).astype(bf16)


def laplace_block(src, part, block, hx, hy, qx_ref, qy_ref):
    rows = pl.ds(block * hx, hx)
    left, right = src[part, rows, pl.ds(0, hy)], src[part, rows, pl.ds(hy, hy)]
    sums = []
    for own, other in ((left, right), (right, left)):
        sums.append(dot(qx_ref[4], own) + dot(own, qy_ref[5]) + dot(other, qy_ref[6]))
    return sums


def half_ends(nx):
    hx = nx // 2
    return [(0, nx - 1), (hx - 1, hx), (hx, hx - 1), (nx - 1, 0)]


def one_row(src, part, row):
    return src[part, pl.ds(row // 16 * 16, 16), :].astype(f32)[row % 16 : row % 16 + 1]


def first_kernel(dims, orders, plan, refs_ref, tables, *rest):
    nx, ny, rows_here = dims
    counts = [len(o) for o in orders]
    pieces, (out, folded, mid, spec, phase) = rest[: sum(counts)], rest[sum(counts) :]
    qx_ref = qy_ref = tables
    part_id, forward, _, _, _ = place_of(plan)
    at = 0
    for part, order in enumerate(orders):
        for piece_order in order:
            piece = pieces[at]
            at += 1
            for i, offset in enumerate(piece_order):
                block = part_id ^ offset
                rows = pl.ds(pl.multiple_of(block * rows_here, rows_here), rows_here)
                values = piece[i]

                @pl.when(forward == 1)
                def _():
                    a, b = fold_cols(values.astype(f32))
                    folded[part, rows, pl.ds(0, ny // 2)] = a
                    folded[part, rows, pl.ds(ny // 2, ny // 2)] = b

                @pl.when(forward == 0)
                def _():
                    out[part, rows, :] = values

    @pl.when(forward == 1)
    def _():
        fill_phase(nx, ny, refs_ref[0, 0:1, 0:1], 1.0, phase)
        forward_rows(nx, ny, folded, qy_ref, mid)
        through_columns(nx, ny, mid, phase, qx_ref, spec)
        inverse_rows(ny, [(start, nx // 2) for start in (0, nx // 2)], spec, qy_ref, out)


def laplace_rows(ref, part, start, count):
    center = ref[part, pl.ds(start + 8, count), :]
    width = center.shape[1]
    return (
        ref[part, pl.ds(start + 7, count), :]
        + ref[part, pl.ds(start + 9, count), :]
        + pltpu.roll(center, 1, 1)
        + pltpu.roll(center, width - 1, 1)
        - 4.0 * center
    )


def step_kernel(dims, orders, plan, index, parts, last, w_ref, refs_ref, tables, *rest):
    nx, ny, rows_here = dims
    qx_ref = qy_ref = tables
    coefs, rest = rest[: 2 * parts], rest[2 * parts :]
    coefs = (coefs[:parts], coefs[parts:])
    if last:
        coef_rows, out_rows, end_rows, out, plane, scaled, mid, spec, phase, tall, edge_rows = rest
    else:
        out, out_rows, plane, scaled, mid, spec, phase = rest
    part_id, forward, side, _, _ = place_of(plan)
    omega = refs_ref[plan[0], 0:1, 0:1]
    hy = ny // 2
    blocks = nx // rows_here
    place = []
    for which, order in enumerate(orders):
        share = blocks // parts
        place.append(
            {o: (i // share, which * share + i % share) for i, o in enumerate(sum(order, []))}
        )
    step = min(32, rows_here)

    def portions():
        for offset in range(blocks):
            for sub in range(0, rows_here, step):
                start = pl.multiple_of((part_id ^ offset) * rows_here + sub, step)
                yield offset, sub, start

    def lens_at(q, offset, sub):
        cols = pl.ds(pl.multiple_of((side ^ q) * hy, hy), hy)
        rows = pl.ds(sub, step)
        (ca, ci), (da, di) = place[0][offset], place[1][offset]
        c = coefs[q][ca][ci, rows, :].astype(f32)
        cos, sin = small_cos_sin(omega * coefs[q][da][di, rows, :].astype(f32))
        return cols, c, cos, sin

    hx = nx // 2
    first = pl.multiple_of(part_id * rows_here, rows_here)
    mine = pl.ds(first, rows_here)

    @pl.when(forward == 1)
    def _():
        for offset, sub, start in portions():
            rows = pl.ds(start, step)
            for q in range(2):
                cols, c, lr, li = lens_at(q, offset, sub)
                wr, wi = w_ref[0, rows, cols].astype(f32), w_ref[1, rows, cols].astype(f32)
                ur, ui = wr * lr - wi * li, wr * li + wi * lr
                plane[0, rows, cols] = ur
                plane[1, rows, cols] = ui
                scaled[0, rows, cols] = (c * ur).astype(bf16)
                scaled[1, rows, cols] = (c * ui).astype(bf16)
        for row, beside in half_ends(nx):
            plane[0, pl.ds(row, 1), :] -= one_row(scaled, 1, beside)
            plane[1, pl.ds(row, 1), :] += one_row(scaled, 0, beside)
        spectra = []
        for block in range(2):
            rows = pl.ds(block * hx, hx)
            sums = [laplace_block(scaled, part, block, hx, hy, qx_ref, qy_ref) for part in range(2)]
            for part in range(2):
                left, right = plane[part, rows, pl.ds(0, hy)], plane[part, rows, pl.ds(hy, hy)]
                l, r = sums[1 - part]
                left, right = (left + l, right + r) if part else (left - l, right - r)
                spec[part, rows, pl.ds(0, hy)] = left.astype(bf16)
                spec[part, rows, pl.ds(hy, hy)] = right.astype(bf16)
                spectra.append(
                    (
                        dot((left + right).astype(bf16), qy_ref[0]),
                        dot((left - right).astype(bf16), qy_ref[1]),
                    )
                )
        for part in range(2):
            for par in range(2):
                add_subtract(mid, part, par, hx, hy, spectra[part][par], spectra[2 + part][par])
        for part in range(2):
            out_rows[part] = spec[part, mine, :]

    @pl.when(forward == 0)
    def _():
        for part in range(2):
            for block in range(2):
                rows = pl.ds(block * hx, hx)
                l, r = laplace_block(w_ref, part, block, hx, hy, qx_ref, qy_ref)
                plane[part, rows, pl.ds(0, hy)] = l
                plane[part, rows, pl.ds(hy, hy)] = r
            for row, beside in half_ends(nx):
                plane[part, pl.ds(row, 1), :] += one_row(w_ref, part, beside)
        flip = (1 - 2 * side).astype(f32)
        for offset, sub, start in portions():
            rows = pl.ds(start, step)
            halves = []
            for q in range(2):
                cols, c, lr, li = lens_at(q, offset, sub)
                tr = w_ref[0, rows, cols].astype(f32) + c * plane[1, rows, cols]
                ti = w_ref[1, rows, cols].astype(f32) - c * plane[0, rows, cols]
                halves.append((tr * lr + ti * li, ti * lr - tr * li))
            for part in range(2):
                a, b = halves[0][part], halves[1][part]
                scaled[part, rows, pl.ds(0, hy)] = (a + b).astype(bf16)
                scaled[part, rows, pl.ds(hy, hy)] = (flip * (a - b)).astype(bf16)
        forward_rows(nx, ny, scaled, qy_ref, mid)

    fill_phase(nx, ny, refs_ref[index + 1, 0:1, 0:1], (2 * forward - 1).astype(f32), phase)
    through_columns(nx, ny, mid, phase, qx_ref, spec)
    before_start = pl.multiple_of(lax.rem(first + nx - 16, nx), 16)
    after_start = pl.multiple_of(lax.rem(first + rows_here, nx), 16)
    if last:
        wanted = [(first, rows_here), (before_start, 16), (after_start, 16)]
    else:
        wanted = [(start, hx) for start in (0, hx)]
    inverse_rows(ny, wanted, spec, qy_ref, out)

    @pl.when(forward == 0)
    def _():
        for part in range(2):
            out_rows[part] = out[part, mine, :]

    if not last:
        return
    for q in range(2):
        cols = pl.ds(pl.multiple_of((side ^ q) * hy, hy), hy)
        for i in range(2):
            for j in range(2):
                row = (2 * i + j) * 16
                rows = pl.ds(row % rows_here, 16)
                edge_rows[i, j, :, cols] = coefs[q][-1][2 * (blocks // parts) + row // rows_here, rows, :]

    @pl.when(forward == 0)
    def _():
        end_rows[...] = jnp.zeros_like(end_rows)

    @pl.when(forward == 1)
    def _():
        before = pl.ds(before_start, 16)
        after = pl.ds(after_start, 16)

        def lensed(values, c, d):
            lr, li = small_cos_sin(omega * d.astype(f32))
            wr, wi = values[0].astype(f32), values[1].astype(f32)
            ur, ui = wr * lr - wi * li, wr * li + wi * lr
            cf = c.astype(f32)
            return ur, ui, cf * ur, cf * ui

        ur, ui, gr, gi = lensed(
            (out[0, mine, :], out[1, mine, :]), coef_rows[0], coef_rows[1]
        )
        tall[0, pl.ds(8, rows_here), :] = gr
        tall[1, pl.ds(8, rows_here), :] = gi
        _, _, gr, gi = lensed(
            (out[0, before, :][15:16], out[1, before, :][15:16]), edge_rows[0, 0, 15:16, :], edge_rows[0, 1, 15:16, :]
        )
        tall[0, pl.ds(7, 1), :] = gr
        tall[1, pl.ds(7, 1), :] = gi
        _, _, gr, gi = lensed(
            (out[0, after, :][0:1], out[1, after, :][0:1]), edge_rows[1, 0, 0:1, :], edge_rows[1, 1, 0:1, :]
        )
        tall[0, pl.ds(rows_here + 8, 1), :] = gr
        tall[1, pl.ds(rows_here + 8, 1), :] = gi
        end_rows[0] = (ur - laplace_rows(tall, 1, 0, rows_here)).astype(bf16)
        end_rows[1] = (ui + laplace_rows(tall, 0, 0, rows_here)).astype(bf16)


def run_first(dims, orders, plan, refs, tables, pieces):
    nx, ny, _ = dims
    return pl.pallas_call(
        partial(first_kernel, dims, orders, plan),
        out_shape=jax.ShapeDtypeStruct((2, nx, ny), bf16),
        in_specs=[vm, vm] + [vm] * len(pieces),
        out_specs=vm,
        scratch_shapes=[pltpu.VMEM((2, nx, ny), bf16)] * 4,
        compiler_params=pltpu.CompilerParams(vmem_limit_bytes=vmem_bytes),
        cost_estimate=pl.CostEstimate(flops=2**30, bytes_accessed=2**22, transcendentals=0),
        name="first_step",
    )(refs, tables, *pieces)


def run_step(dims, orders, plan, index, w, coefs, refs, tables, coef_rows=None):
    nx, ny, rows_here = dims
    last = coef_rows is not None
    rows_shape = jax.ShapeDtypeStruct((2, rows_here, ny), bf16)
    full = pltpu.VMEM((2, nx, ny), bf16)
    scratch = [pltpu.VMEM((2, nx, ny), f32)]
    scratch += [full] * 4
    if last:
        outs = (rows_shape, rows_shape)
        scratch = [full] + scratch + [pltpu.VMEM((2, rows_here + 16, ny), f32)]
        scratch += [pltpu.VMEM((2, 2, 16, ny), bf16)]
    else:
        outs = (jax.ShapeDtypeStruct((2, nx, ny), bf16), rows_shape)
    return pl.pallas_call(
        partial(step_kernel, dims, orders, plan, index, len(coefs) // 2, last),
        out_shape=outs,
        in_specs=[vm] * (3 + len(coefs) + (1 if last else 0)),
        out_specs=(vm,) * len(outs),
        scratch_shapes=scratch,
        compiler_params=pltpu.CompilerParams(vmem_limit_bytes=vmem_bytes),
        cost_estimate=pl.CostEstimate(flops=2**32, bytes_accessed=2**24, transcendentals=0),
        name="end_step" if last else "depth_step",
    )(w, refs, tables, *coefs, *([coef_rows] if last else []))


def join_kernel(counts, wanted, sides, *refs):
    count = len(counts)
    kept = (len(refs) - count - len(wanted)) // 2
    pieces, outs = refs[kept : kept + count], refs[2 * kept + count :]
    for (slot, chosen), out in zip(wanted, outs):
        at = 0
        for which in chosen:
            for i in range(counts[which]):
                out[at + i] = pieces[which][i, slot]
            at += counts[which]
    if not sides:
        return
    rows_here = pieces[0].shape[2]
    size = sum(counts) // 2
    part_id = lax.axis_index("rows")
    for i, (beside, first) in enumerate(((size - 1, rows_here - 16), (1, 0))):
        offset_wanted = part_id ^ lax.rem(part_id + beside, size)
        for j, (order, chosen) in enumerate(sides):
            places = [(which, k) for which in chosen for k in range(counts[which])]
            row = (2 * i + j) * 16
            target = outs[-1].at[at + row // rows_here, pl.ds(row % rows_here, 16)]
            for offset, (which, k) in zip(order, places):

                @pl.when(offset_wanted == offset)
                def _(which=which, k=k, first=first, target=target):
                    target[...] = pieces[which][k, 0, pl.ds(first, 16), :]


def run_join(pieces, wanted, kept=(), sides=()):
    _, _, rows_here, hy = pieces[0].shape
    counts = [piece.shape[0] for piece in pieces]
    shapes = [(sum(counts[i] for i in chosen), rows_here, hy) for _, chosen in wanted]
    if sides:
        shapes[-1] = (shapes[-1][0] + -(-64 // rows_here), rows_here, hy)
    return pl.pallas_call(
        partial(join_kernel, counts, wanted, sides),
        out_shape=[jax.ShapeDtypeStruct(k.shape, k.dtype) for k in kept]
        + [jax.ShapeDtypeStruct(shape, bf16) for shape in shapes],
        in_specs=[vm] * (len(kept) + len(pieces)),
        out_specs=[vm] * (len(kept) + len(shapes)),
        input_output_aliases={i: i for i in range(len(kept))},
        compiler_params=pltpu.CompilerParams(vmem_limit_bytes=vmem_bytes),
        cost_estimate=pl.CostEstimate(flops=0, bytes_accessed=2**18, transcendentals=0),
        name="join_pieces",
    )(*kept, *pieces)


def image_kernel(plan, refs_ref, *refs):
    sections, freq_count = plan
    fields, (bottom, out) = refs[:-2], refs[-2:]
    _, forward, _, freq, group = place_of(plan)

    def total(adjoint_at):
        result = None
        for i in range(freq_count):
            freq_i = freq ^ i
            adjoint = adjoint_at(i, freq_i)
            a = [fields[i][j].astype(f32) for j in range(2)]
            b = [adjoint[j].astype(f32) for j in range(2)]
            weight = refs_ref[sections + i, 0:1, 0:1] * (2 * forward - 1).astype(f32)
            term = weight * (a[0] * b[1] - a[1] * b[0])
            result = term if result is None else result + term
        out[0] = result

    @pl.when(group == sections - 1)
    def _():
        total(lambda i, freq_i: bottom.at[freq_i])

    @pl.when(group != sections - 1)
    def _():
        total(lambda i, freq_i: fields[freq_count + i])


def run_image(plan, refs, fields, bottom):
    _, rows_here, ny = fields[0].shape
    return pl.pallas_call(
        partial(image_kernel, plan),
        out_shape=jax.ShapeDtypeStruct((1, rows_here, ny), f32),
        in_specs=[vm] * (len(fields) + 2),
        out_specs=vm,
        compiler_params=pltpu.CompilerParams(vmem_limit_bytes=vmem_bytes),
        name="image",
    )(refs, *fields, bottom)


def swap(values, axis, mask):
    axes = axis if isinstance(axis, tuple) else (axis,)
    size = math.prod(lax.axis_size(a) for a in axes)
    return lax.ppermute(values, axis, [(i, i ^ mask) for i in range(size)])


def doubling_masks(size):
    masks = []
    mask = size // 2
    while mask:
        masks.append(mask)
        mask //= 2
    descending = masks
    ascending = masks[:1] + masks[1:][::-1]
    return descending, ascending


def doubling_orders(masks):
    orders = [[0]]
    seen = [0]
    for mask in masks:
        new = [mask ^ o for o in seen]
        orders.append(new)
        seen = seen + new
    return orders


def first_exchange(pair, axis):
    size = lax.axis_size(axis)
    got = swap(pair, axis, size // 2)
    return [[pair[0:1], got[0:1]], [pair[1:2], got[1:2]]]


def after(values, earlier):
    return lax.optimization_barrier((values, earlier))[0]


def next_exchange(pieces, axis, level):
    masks = doubling_masks(lax.axis_size(axis))
    return [
        have + [swap(jnp.concatenate(have, 0), axis, masks[which][level])]
        for which, have in enumerate(pieces)
    ]


def per_device(source_top, adjoint_bottom, slowness, correction, slowness_ref, omega):
    row_parts = lax.axis_size("rows")
    sections = lax.axis_size("depth")
    group = lax.axis_index("depth")
    part_id = lax.axis_index("rows")
    freq_count = omega.shape[0]
    chains = 2 * freq_count
    rep = sections // chains
    rows_here, ny = slowness.shape[1:]
    nx = rows_here * row_parts
    dims = (nx, ny, rows_here)
    hy = ny // 2
    chain = lax.div(group, rep)
    forward = lax.div(chain, freq_count)
    freq = lax.rem(chain, freq_count)
    side = lax.rem(group, 2)
    half_sections = sections // 2
    masks = doubling_masks(row_parts)
    orders = [doubling_orders(m) for m in masks]
    rounds = len(masks[0])
    plan = (sections, freq_count)

    def pick(values, index):
        return lax.dynamic_index_in_dim(values, index, 0, keepdims=False)

    plane = jnp.where(forward == 1, pick(source_top, freq), pick(adjoint_bottom, freq))
    high = slowness_ref.astype(bf16)
    middle = (slowness_ref - high.astype(f32)).astype(bf16)
    low = (slowness_ref - high.astype(f32) - middle.astype(f32)).astype(bf16)
    terms = jnp.concatenate([high, middle, low, jnp.zeros((13,), bf16)])
    values = jnp.concatenate([correction[0], slowness[0] - slowness_ref[0]], 0).astype(bf16)
    values = jnp.concatenate([values, jnp.broadcast_to(terms[:, None], (16, ny))], 0)
    left, right = values[:, :hy], values[:, hy:]
    same = jnp.where(side == 0, left, right)
    other = jnp.where(side == 0, right, left)
    packed = jnp.stack([same, other])
    blocks, partner = [packed], []
    for k in range(1, sections):
        blocks.append(swap(packed if k < half_sections else (same, other)[k % 2], "depth", k))
    for k in range(half_sections, sections):
        sent = (same, other)[k % 2][: 2 * rows_here]
        mask = k * row_parts + row_parts // 2
        partner.append(swap(sent, ("depth", "rows"), mask))
    planes = first_exchange(plane, "rows")
    assert nx == ny
    tables = basis_tables(nx)
    for level in range(1, rounds):
        planes = next_exchange(planes, "rows", level)
        if level == 1:
            blocks, partner = after((blocks, partner), planes)
            pair, refs, coef_rows = run_sort(omega, blocks, partner, rows_here, hy)
            pieces = [[pair[0]], [pair[1]]]
        before = pieces = after(pieces, planes)
        pieces = next_exchange(pieces, "rows", level)
    w = run_first(dims, orders, plan, refs, tables, after(planes[0] + planes[1], before))
    far_slots = [sections - 1 - slot for slot in range(half_sections, sections - 1)]
    early = before[0] + before[1]
    head = run_join(early, [(slot, range(len(early))) for slot in far_slots])
    head = [swap(h, "depth", half_sections) for h in head]
    last = after([have[-1] for have in pieces], (w, head))
    each = len(before[0])
    order = [*range(each), 2 * each, *range(each, 2 * each), 2 * each + 1]
    wanted = [(slot, order) for slot in range(half_sections)]
    wanted += [(slot, order[each :: each + 1]) for slot in far_slots]
    sides = [
        (sum(orders[j], []), order[j * (each + 1) : (j + 1) * (each + 1)]) for j in range(2)
    ]
    w, refs, *joined = run_join(early + last, wanted, (w, refs), sides)
    mine, rest = joined[:half_sections], joined[half_sections:]
    coefs = [[m, swap(m, "depth", 1)] for m in mine]
    far = [[h, swap(r, "depth", half_sections)] for h, r in zip(head, rest)]
    row_outs = []
    for slot in range(sections - 1):
        last = slot == sections - 2
        w, *rest = run_step(
            dims, orders, plan, slot, w, coefs[slot], refs, tables, coef_rows if last else None
        )
        if slot == half_sections - 2:
            coefs += [have + [swap(part, "depth", 1) for part in have] for have in after(far, w)]
        row_outs += [w, *rest] if last else rest

    def index_for(g, target):
        return target if g >= half_sections else sections - 2 - target

    def payload_for(mask):
        used = sorted(
            {index_for(g, g ^ mask) for g in range(sections) if index_for(g, g ^ mask) >= 0}
        )
        low = used[0]
        stack = jnp.stack(row_outs[low : used[-1] + 1])
        target = group ^ mask
        index = jnp.where(forward == 1, target, sections - 2 - target)
        return pick(stack, jnp.clip(index - low, 0, len(stack) - 1))

    far = [swap(payload_for(i * rep), "depth", i * rep) for i in range(freq_count, chains)]
    near = [payload_for(i * rep) for i in range(freq_count)]
    far, near = lax.optimization_barrier((far, near))
    fields = [f if i == 0 else swap(f, "depth", i * rep) for i, f in enumerate(near)] + far
    return run_image(plan, refs, fields, adjoint_bottom)


def solution(mesh):
    in_specs = (
        P(None, None, "rows", None),
        P(None, None, "rows", None),
        P("depth", "rows", None),
        P("depth", "rows", None),
        P("depth"),
        P(),
    )
    out_specs = P("depth", "rows", None)
    return jax.shard_map(
        per_device, mesh=mesh, in_specs=in_specs, out_specs=out_specs, check_vma=False
    )
```

```python
from functools import partial
import math

import jax
import jax.numpy as jnp
import numpy as np
from jax import lax
from jax.experimental import pallas as pl
from jax.experimental.pallas import tpu as pltpu
from jax.sharding import PartitionSpec as P

bf16 = jnp.bfloat16
f32 = jnp.float32
vmem_bytes = 32 * 1024 * 1024


def basis(length):
    half, quarter = length // 2, length // 4
    n = np.arange(half)[:, None]
    j = np.arange(quarter)[None, :]
    scale = math.sqrt(2.0 / length)
    even_cos = scale * np.cos(2 * np.pi * ((2 * j * n) % length) / length)
    even_sin = scale * np.sin(2 * np.pi * ((2 * j * n) % length) / length)
    even_cos[:, 0] = 1.0 / math.sqrt(length)
    even_sin[:, 0] = (1.0 - 2.0 * (np.arange(half) % 2)) / math.sqrt(length)
    odd_cos = scale * np.cos(2 * np.pi * (((2 * j + 1) * n) % length) / length)
    odd_sin = scale * np.sin(2 * np.pi * (((2 * j + 1) * n) % length) / length)
    even = np.concatenate([even_cos, even_sin], 1).astype(np.float32)
    odd = np.concatenate([odd_cos, odd_sin], 1).astype(np.float32)
    return even, odd


def basis_tables(length):
    even, odd = basis(length)
    half = length // 2
    near = np.eye(half, k=1) + np.eye(half, k=-1)
    across = np.eye(half, k=half - 1) + np.eye(half, k=1 - half)
    tables = [even, odd, even.T, odd.T, near - 4.0 * np.eye(half), near, across]
    return jnp.asarray(np.stack(tables).astype(np.float32), bf16)


def dot(a, b):
    return jnp.dot(a, b, preferred_element_type=f32)


def fitted(function, top, degree):
    fit = np.polynomial.Chebyshev.interpolate(function, degree, [0.0, top])
    return [float(c) for c in fit.convert(kind=np.polynomial.Polynomial).coef]


def horner(coefs, x):
    total = coefs[-1] * x + coefs[-2]
    for c in coefs[-3::-1]:
        total = total * x + c
    return total


def sinc_root(x):
    return np.sinc(np.sqrt(x) / np.pi)


def cos_root(x):
    return np.cos(np.sqrt(x))


lens_top = 0.45
lens_cos, lens_sin = fitted(cos_root, lens_top, 3), fitted(sinc_root, lens_top, 3)
phase_top = 3.2
phase_cos, phase_sin = fitted(cos_root, phase_top, 7), fitted(sinc_root, phase_top, 7)


def small_cos_sin(a):
    s = a * a
    return horner(lens_cos, s), a * horner(lens_sin, s)


def fill_phase(nx, ny, level, sign, out):
    qx, qy = nx // 4, ny // 4

    def waves(rows, cols, axis, parity, length):
        j = lax.broadcasted_iota(jnp.int32, (rows, cols), axis)
        return (2 * j + parity).astype(f32) * (2.0 * math.pi / length)

    def values(kx, ky):
        squared = level * level - kx * kx - ky * ky
        inside = jnp.maximum(squared, 0.0)
        damping = jnp.exp(-jnp.sqrt(jnp.maximum(-squared, 0.0)))
        sine = jnp.sqrt(inside) * horner(phase_sin, inside)
        return damping * horner(phase_cos, inside), sign * damping * sine

    edge = math.pi
    row_zero = lax.broadcasted_iota(jnp.int32, (qx, qy), 0) == 0
    col_zero = lax.broadcasted_iota(jnp.int32, (qx, qy), 1) == 0
    for px in range(2):
        for py in range(2):
            kx = waves(qx, qy, 0, px, nx)
            ky = waves(qx, qy, 1, py, ny)
            base = values(kx, ky)
            across = values(jnp.full((8, qy), edge), waves(8, qy, 1, py, ny))
            along = values(waves(qx, 1, 0, px, nx), jnp.full((qx, 1), edge))
            corner = values(jnp.full((8, 1), edge), jnp.full((8, 1), edge))
            for sx in range(2):
                for sy in range(2):
                    new_row, new_col = sx and not px, sy and not py
                    for part in range(2):
                        v = base[part]
                        if new_col:
                            v = jnp.where(col_zero, along[part], v)
                        if new_row:
                            v = jnp.where(row_zero, across[part][0:1], v)
                        if new_row and new_col:
                            v = jnp.where(row_zero & col_zero, corner[part][0:1], v)
                        rows = pl.ds((2 * px + sx) * qx, qx)
                        cols = pl.ds((2 * py + sy) * qy, qy)
                        out[part, rows, cols] = v.astype(bf16)


def place_of(plan):
    sections, freq_count = plan
    group = lax.axis_index("depth")
    chain = lax.div(group, jnp.int32(sections // (2 * freq_count)))
    forward = lax.div(chain, jnp.int32(freq_count))
    freq = lax.rem(chain, jnp.int32(freq_count))
    return lax.axis_index("rows"), forward, lax.rem(group, jnp.int32(2)), freq, group


vm = pl.BlockSpec(memory_space=pltpu.VMEM)
sm = pl.BlockSpec(memory_space=pltpu.SMEM)


def sort_kernel(rows_here, hy, plan, omega_ref, *refs):
    sections, freq_count = plan
    half_sections = sections // 2
    blocks, refs = refs[:sections], refs[sections:]
    partner, (pair, refs_out, coef_rows) = refs[:half_sections], refs[half_sections:]
    _, forward, side, freq, group = place_of(plan)
    omega = omega_ref[freq]
    for i in range(freq_count):
        refs_out[sections + i] = jnp.full((8, 128), omega_ref[freq ^ i], f32)

    def block_of(k):
        return blocks[k].at[k % 2] if k < half_sections else blocks[k]

    def chosen(index, first, body):
        for k in range(first, sections):
            pl.when(index == k)(partial(body, k))

    for slot in range(half_sections):
        depth = jnp.where(forward == 1, slot, sections - 1 - slot)

        def place(k, slot=slot):
            for j in range(2):
                part = pl.ds(j * rows_here, rows_here)
                pair[j, 0, slot] = blocks[k][part, :]
                pair[j, 1, slot] = partner[k - half_sections][part, :]

        chosen(group ^ depth, half_sections, place)
    for slot in range(sections):
        depth = jnp.where(forward == 1, slot, (sections - slot) % sections)

        def level(k, slot=slot):
            parts = block_of(k)[pl.ds(2 * rows_here, 16), pl.ds(0, 128)].astype(f32)
            refs_out[slot] = jnp.broadcast_to(omega * (parts[0:1] + parts[1:2] + parts[2:3]), (8, 128))

        chosen(group ^ depth, 0, level)

    for k in range(half_sections):

        @pl.when(jnp.clip(group ^ (sections - 1), 0, half_sections - 1) == k)
        def _(k=k):
            for i in range(2):
                cols = pl.ds(pl.multiple_of((side ^ (k % 2) ^ i) * hy, hy), hy)
                block = blocks[k].at[i]
                for j in range(2):
                    coef_rows[j, :, cols] = block[pl.ds(j * rows_here, rows_here), :]


def run_sort(omega, blocks, partner, rows_here, hy):
    sections = len(blocks)
    return pl.pallas_call(
        partial(sort_kernel, rows_here, hy, (sections, omega.shape[0])),
        out_shape=(
            jax.ShapeDtypeStruct((2, 2, sections // 2, rows_here, hy), bf16),
            jax.ShapeDtypeStruct((sections + omega.shape[0], 8, 128), f32),
            jax.ShapeDtypeStruct((2, rows_here, 2 * hy), bf16),
        ),
        in_specs=[sm] + [vm] * (sections + len(partner)),
        out_specs=(vm, vm, vm),
        compiler_params=pltpu.CompilerParams(vmem_limit_bytes=vmem_bytes),
        name="sort_depths",
    )(omega, *blocks, *partner)


def fold_cols(values):
    half = values.shape[1] // 2
    a, b = values[:, :half], values[:, half:]
    return (a + b).astype(bf16), (a - b).astype(bf16)


def add_subtract(mid, part, par, hx, hy, top, low):
    cols = pl.ds(par * hy, hy)
    mid[part, pl.ds(0, hx), cols] = (top + low).astype(bf16)
    mid[part, pl.ds(hx, hx), cols] = (top - low).astype(bf16)


def forward_rows(nx, ny, folded, qy_ref, mid):
    hx, hy = nx // 2, ny // 2
    for part in range(2):
        for par in range(2):
            cols = pl.ds(par * hy, hy)
            top = dot(folded[part, pl.ds(0, hx), cols], qy_ref[par])
            low = dot(folded[part, pl.ds(hx, hx), cols], qy_ref[par])
            add_subtract(mid, part, par, hx, hy, top, low)


def through_columns(nx, ny, mid, phase, qx_ref, spec):
    hx, hy = nx // 2, ny // 2
    for start in range(0, ny, hy):
        cols = pl.ds(start, hy)
        back = []
        for par in range(2):
            rows = pl.ds(par * hx, hx)
            zr = dot(qx_ref[2 + par], mid[0, rows, cols])
            zi = dot(qx_ref[2 + par], mid[1, rows, cols])
            pr = phase[0, rows, cols].astype(f32)
            pi = phase[1, rows, cols].astype(f32)
            yr = (zr * pr - zi * pi).astype(bf16)
            yi = (zr * pi + zi * pr).astype(bf16)
            back.append((dot(qx_ref[par], yr), dot(qx_ref[par], yi)))
        for part in range(2):
            a, b = back[0][part], back[1][part]
            spec[part, pl.ds(0, hx), cols] = (a + b).astype(bf16)
            spec[part, pl.ds(hx, hx), cols] = (a - b).astype(bf16)


def inverse_rows(ny, pieces, spec, qy_ref, out):
    hy = ny // 2
    for part in range(2):
        for start, count in pieces:
            rows = pl.ds(start, count)
            a = dot(spec[part, rows, pl.ds(0, hy)], qy_ref[2])
            b = dot(spec[part, rows, pl.ds(hy, hy)], qy_ref[3])
            out[part, rows, pl.ds(0, hy)] = (a + b).astype(bf16)
            out[part, rows, pl.ds(hy, hy)] = (a - b).astype(bf16)


def laplace_block(src, part, block, hx, hy, qx_ref, qy_ref):
    rows = pl.ds(block * hx, hx)
    left, right = src[part, rows, pl.ds(0, hy)], src[part, rows, pl.ds(hy, hy)]
    sums = []
    for own, other in ((left, right), (right, left)):
        sums.append(dot(qx_ref[4], own) + dot(own, qy_ref[5]) + dot(other, qy_ref[6]))
    return sums


def half_ends(nx):
    hx = nx // 2
    return [(0, nx - 1), (hx - 1, hx), (hx, hx - 1), (nx - 1, 0)]


def one_row(src, part, row):
    return src[part, pl.ds(row // 16 * 16, 16), :].astype(f32)[row % 16 : row % 16 + 1]


def first_kernel(dims, orders, plan, refs_ref, tables, *rest):
    nx, ny, rows_here = dims
    counts = [len(o) for o in orders]
    pieces, (out, folded, mid, spec, phase) = rest[: sum(counts)], rest[sum(counts) :]
    qx_ref = qy_ref = tables
    part_id, forward, _, _, _ = place_of(plan)
    at = 0
    for part, order in enumerate(orders):
        for piece_order in order:
            piece = pieces[at]
            at += 1
            for i, offset in enumerate(piece_order):
                block = part_id ^ offset
                rows = pl.ds(pl.multiple_of(block * rows_here, rows_here), rows_here)
                values = piece[i]

                @pl.when(forward == 1)
                def _():
                    a, b = fold_cols(values.astype(f32))
                    folded[part, rows, pl.ds(0, ny // 2)] = a
                    folded[part, rows, pl.ds(ny // 2, ny // 2)] = b

                @pl.when(forward == 0)
                def _():
                    out[part, rows, :] = values

    @pl.when(forward == 1)
    def _():
        fill_phase(nx, ny, refs_ref[0, 0:1, 0:1], 1.0, phase)
        forward_rows(nx, ny, folded, qy_ref, mid)
        through_columns(nx, ny, mid, phase, qx_ref, spec)
        inverse_rows(ny, [(start, nx // 2) for start in (0, nx // 2)], spec, qy_ref, out)


def laplace_rows(ref, part, start, count):
    center = ref[part, pl.ds(start + 8, count), :]
    width = center.shape[1]
    return (
        ref[part, pl.ds(start + 7, count), :]
        + ref[part, pl.ds(start + 9, count), :]
        + pltpu.roll(center, 1, 1)
        + pltpu.roll(center, width - 1, 1)
        - 4.0 * center
    )


def step_kernel(dims, orders, plan, index, parts, last, w_ref, refs_ref, tables, *rest):
    nx, ny, rows_here = dims
    qx_ref = qy_ref = tables
    coefs, rest = rest[: 2 * parts], rest[2 * parts :]
    coefs = (coefs[:parts], coefs[parts:])
    if last:
        coef_rows, out_rows, end_rows, out, plane, scaled, mid, spec, phase, tall, edge_rows = rest
    else:
        out, out_rows, plane, scaled, mid, spec, phase = rest
    part_id, forward, side, _, _ = place_of(plan)
    omega = refs_ref[plan[0], 0:1, 0:1]
    hy = ny // 2
    blocks = nx // rows_here
    place = []
    for which, order in enumerate(orders):
        share = blocks // parts
        place.append(
            {o: (i // share, which * share + i % share) for i, o in enumerate(sum(order, []))}
        )
    step = min(32, rows_here)

    def portions():
        for offset in range(blocks):
            for sub in range(0, rows_here, step):
                start = pl.multiple_of((part_id ^ offset) * rows_here + sub, step)
                yield offset, sub, start

    def lens_at(q, offset, sub):
        cols = pl.ds(pl.multiple_of((side ^ q) * hy, hy), hy)
        rows = pl.ds(sub, step)
        (ca, ci), (da, di) = place[0][offset], place[1][offset]
        c = coefs[q][ca][ci, rows, :].astype(f32)
        cos, sin = small_cos_sin(omega * coefs[q][da][di, rows, :].astype(f32))
        return cols, c, cos, sin

    hx = nx // 2
    first = pl.multiple_of(part_id * rows_here, rows_here)
    mine = pl.ds(first, rows_here)

    @pl.when(forward == 1)
    def _():
        for offset, sub, start in portions():
            rows = pl.ds(start, step)
            for q in range(2):
                cols, c, lr, li = lens_at(q, offset, sub)
                wr, wi = w_ref[0, rows, cols].astype(f32), w_ref[1, rows, cols].astype(f32)
                ur, ui = wr * lr - wi * li, wr * li + wi * lr
                plane[0, rows, cols] = ur
                plane[1, rows, cols] = ui
                scaled[0, rows, cols] = (c * ur).astype(bf16)
                scaled[1, rows, cols] = (c * ui).astype(bf16)
        for row, beside in half_ends(nx):
            plane[0, pl.ds(row, 1), :] -= one_row(scaled, 1, beside)
            plane[1, pl.ds(row, 1), :] += one_row(scaled, 0, beside)
        spectra = []
        for block in range(2):
            rows = pl.ds(block * hx, hx)
            sums = [laplace_block(scaled, part, block, hx, hy, qx_ref, qy_ref) for part in range(2)]
            for part in range(2):
                left, right = plane[part, rows, pl.ds(0, hy)], plane[part, rows, pl.ds(hy, hy)]
                l, r = sums[1 - part]
                left, right = (left + l, right + r) if part else (left - l, right - r)
                spec[part, rows, pl.ds(0, hy)] = left.astype(bf16)
                spec[part, rows, pl.ds(hy, hy)] = right.astype(bf16)
                spectra.append(
                    (
                        dot((left + right).astype(bf16), qy_ref[0]),
                        dot((left - right).astype(bf16), qy_ref[1]),
                    )
                )
        for part in range(2):
            for par in range(2):
                add_subtract(mid, part, par, hx, hy, spectra[part][par], spectra[2 + part][par])
        for part in range(2):
            out_rows[part] = spec[part, mine, :]

    @pl.when(forward == 0)
    def _():
        for part in range(2):
            for block in range(2):
                rows = pl.ds(block * hx, hx)
                l, r = laplace_block(w_ref, part, block, hx, hy, qx_ref, qy_ref)
                plane[part, rows, pl.ds(0, hy)] = l
                plane[part, rows, pl.ds(hy, hy)] = r
            for row, beside in half_ends(nx):
                plane[part, pl.ds(row, 1), :] += one_row(w_ref, part, beside)
        flip = (1 - 2 * side).astype(f32)
        for offset, sub, start in portions():
            rows = pl.ds(start, step)
            halves = []
            for q in range(2):
                cols, c, lr, li = lens_at(q, offset, sub)
                tr = w_ref[0, rows, cols].astype(f32) + c * plane[1, rows, cols]
                ti = w_ref[1, rows, cols].astype(f32) - c * plane[0, rows, cols]
                halves.append((tr * lr + ti * li, ti * lr - tr * li))
            for part in range(2):
                a, b = halves[0][part], halves[1][part]
                scaled[part, rows, pl.ds(0, hy)] = (a + b).astype(bf16)
                scaled[part, rows, pl.ds(hy, hy)] = (flip * (a - b)).astype(bf16)
        forward_rows(nx, ny, scaled, qy_ref, mid)

    fill_phase(nx, ny, refs_ref[index + 1, 0:1, 0:1], (2 * forward - 1).astype(f32), phase)
    through_columns(nx, ny, mid, phase, qx_ref, spec)
    before_start = pl.multiple_of(lax.rem(first + nx - 16, nx), 16)
    after_start = pl.multiple_of(lax.rem(first + rows_here, nx), 16)
    if last:
        wanted = [(first, rows_here), (before_start, 16), (after_start, 16)]
    else:
        wanted = [(start, hx) for start in (0, hx)]
    inverse_rows(ny, wanted, spec, qy_ref, out)

    @pl.when(forward == 0)
    def _():
        for part in range(2):
            out_rows[part] = out[part, mine, :]

    if not last:
        return
    for q in range(2):
        cols = pl.ds(pl.multiple_of((side ^ q) * hy, hy), hy)
        for i in range(2):
            for j in range(2):
                row = (2 * i + j) * 16
                rows = pl.ds(row % rows_here, 16)
                edge_rows[i, j, :, cols] = coefs[q][-1][2 * (blocks // parts) + row // rows_here, rows, :]

    @pl.when(forward == 0)
    def _():
        end_rows[...] = jnp.zeros_like(end_rows)

    @pl.when(forward == 1)
    def _():
        before = pl.ds(before_start, 16)
        after = pl.ds(after_start, 16)

        def lensed(values, c, d):
            lr, li = small_cos_sin(omega * d.astype(f32))
            wr, wi = values[0].astype(f32), values[1].astype(f32)
            ur, ui = wr * lr - wi * li, wr * li + wi * lr
            cf = c.astype(f32)
            return ur, ui, cf * ur, cf * ui

        ur, ui, gr, gi = lensed(
            (out[0, mine, :], out[1, mine, :]), coef_rows[0], coef_rows[1]
        )
        tall[0, pl.ds(8, rows_here), :] = gr
        tall[1, pl.ds(8, rows_here), :] = gi
        _, _, gr, gi = lensed(
            (out[0, before, :][15:16], out[1, before, :][15:16]), edge_rows[0, 0, 15:16, :], edge_rows[0, 1, 15:16, :]
        )
        tall[0, pl.ds(7, 1), :] = gr
        tall[1, pl.ds(7, 1), :] = gi
        _, _, gr, gi = lensed(
            (out[0, after, :][0:1], out[1, after, :][0:1]), edge_rows[1, 0, 0:1, :], edge_rows[1, 1, 0:1, :]
        )
        tall[0, pl.ds(rows_here + 8, 1), :] = gr
        tall[1, pl.ds(rows_here + 8, 1), :] = gi
        end_rows[0] = (ur - laplace_rows(tall, 1, 0, rows_here)).astype(bf16)
        end_rows[1] = (ui + laplace_rows(tall, 0, 0, rows_here)).astype(bf16)


def run_first(dims, orders, plan, refs, tables, pieces):
    nx, ny, _ = dims
    return pl.pallas_call(
        partial(first_kernel, dims, orders, plan),
        out_shape=jax.ShapeDtypeStruct((2, nx, ny), bf16),
        in_specs=[vm, vm] + [vm] * len(pieces),
        out_specs=vm,
        scratch_shapes=[pltpu.VMEM((2, nx, ny), bf16)] * 4,
        compiler_params=pltpu.CompilerParams(vmem_limit_bytes=vmem_bytes),
        cost_estimate=pl.CostEstimate(flops=2**30, bytes_accessed=2**22, transcendentals=0),
        name="first_step",
    )(refs, tables, *pieces)


def run_step(dims, orders, plan, index, w, coefs, refs, tables, coef_rows=None):
    nx, ny, rows_here = dims
    last = coef_rows is not None
    rows_shape = jax.ShapeDtypeStruct((2, rows_here, ny), bf16)
    full = pltpu.VMEM((2, nx, ny), bf16)
    scratch = [pltpu.VMEM((2, nx, ny), f32)]
    scratch += [full] * 4
    if last:
        outs = (rows_shape, rows_shape)
        scratch = [full] + scratch + [pltpu.VMEM((2, rows_here + 16, ny), f32)]
        scratch += [pltpu.VMEM((2, 2, 16, ny), bf16)]
    else:
        outs = (jax.ShapeDtypeStruct((2, nx, ny), bf16), rows_shape)
    return pl.pallas_call(
        partial(step_kernel, dims, orders, plan, index, len(coefs) // 2, last),
        out_shape=outs,
        in_specs=[vm] * (3 + len(coefs) + (1 if last else 0)),
        out_specs=(vm,) * len(outs),
        scratch_shapes=scratch,
        compiler_params=pltpu.CompilerParams(vmem_limit_bytes=vmem_bytes),
        cost_estimate=pl.CostEstimate(flops=2**32, bytes_accessed=2**24, transcendentals=0),
        name="end_step" if last else "depth_step",
    )(w, refs, tables, *coefs, *([coef_rows] if last else []))


def join_kernel(counts, wanted, sides, *refs):
    count = len(counts)
    kept = (len(refs) - count - len(wanted)) // 2
    pieces, outs = refs[kept : kept + count], refs[2 * kept + count :]
    for (slot, chosen), out in zip(wanted, outs):
        at = 0
        for which in chosen:
            for i in range(counts[which]):
                out[at + i] = pieces[which][i, slot]
            at += counts[which]
    if not sides:
        return
    rows_here = pieces[0].shape[2]
    size = sum(counts) // 2
    part_id = lax.axis_index("rows")
    for i, (beside, first) in enumerate(((size - 1, rows_here - 16), (1, 0))):
        offset_wanted = part_id ^ lax.rem(part_id + beside, size)
        for j, (order, chosen) in enumerate(sides):
            places = [(which, k) for which in chosen for k in range(counts[which])]
            row = (2 * i + j) * 16
            target = outs[-1].at[at + row // rows_here, pl.ds(row % rows_here, 16)]
            for offset, (which, k) in zip(order, places):

                @pl.when(offset_wanted == offset)
                def _(which=which, k=k, first=first, target=target):
                    target[...] = pieces[which][k, 0, pl.ds(first, 16), :]


def run_join(pieces, wanted, kept=(), sides=()):
    _, _, rows_here, hy = pieces[0].shape
    counts = [piece.shape[0] for piece in pieces]
    shapes = [(sum(counts[i] for i in chosen), rows_here, hy) for _, chosen in wanted]
    if sides:
        shapes[-1] = (shapes[-1][0] + -(-64 // rows_here), rows_here, hy)
    return pl.pallas_call(
        partial(join_kernel, counts, wanted, sides),
        out_shape=[jax.ShapeDtypeStruct(k.shape, k.dtype) for k in kept]
        + [jax.ShapeDtypeStruct(shape, bf16) for shape in shapes],
        in_specs=[vm] * (len(kept) + len(pieces)),
        out_specs=[vm] * (len(kept) + len(shapes)),
        input_output_aliases={i: i for i in range(len(kept))},
        compiler_params=pltpu.CompilerParams(vmem_limit_bytes=vmem_bytes),
        cost_estimate=pl.CostEstimate(flops=0, bytes_accessed=2**18, transcendentals=0),
        name="join_pieces",
    )(*kept, *pieces)


def image_kernel(plan, refs_ref, *refs):
    sections, freq_count = plan
    fields, (bottom, out) = refs[:-2], refs[-2:]
    _, forward, _, freq, group = place_of(plan)

    def total(adjoint_at):
        result = None
        for i in range(freq_count):
            freq_i = freq ^ i
            adjoint = adjoint_at(i, freq_i)
            a = [fields[i][j].astype(f32) for j in range(2)]
            b = [adjoint[j].astype(f32) for j in range(2)]
            weight = refs_ref[sections + i, 0:1, 0:1] * (2 * forward - 1).astype(f32)
            term = weight * (a[0] * b[1] - a[1] * b[0])
            result = term if result is None else result + term
        out[0] = result

    @pl.when(group == sections - 1)
    def _():
        total(lambda i, freq_i: bottom.at[freq_i])

    @pl.when(group != sections - 1)
    def _():
        total(lambda i, freq_i: fields[freq_count + i])


def run_image(plan, refs, fields, bottom):
    _, rows_here, ny = fields[0].shape
    return pl.pallas_call(
        partial(image_kernel, plan),
        out_shape=jax.ShapeDtypeStruct((1, rows_here, ny), f32),
        in_specs=[vm] * (len(fields) + 2),
        out_specs=vm,
        compiler_params=pltpu.CompilerParams(vmem_limit_bytes=vmem_bytes),
        name="image",
    )(refs, *fields, bottom)


def swap(values, axis, mask):
    axes = axis if isinstance(axis, tuple) else (axis,)
    size = math.prod(lax.axis_size(a) for a in axes)
    return lax.ppermute(values, axis, [(i, i ^ mask) for i in range(size)])


def doubling_masks(size):
    masks = []
    mask = size // 2
    while mask:
        masks.append(mask)
        mask //= 2
    descending = masks
    ascending = masks[:1] + masks[1:][::-1]
    return descending, ascending


def doubling_orders(masks):
    orders = [[0]]
    seen = [0]
    for mask in masks:
        new = [mask ^ o for o in seen]
        orders.append(new)
        seen = seen + new
    return orders


def first_exchange(pair, axis):
    size = lax.axis_size(axis)
    got = swap(pair, axis, size // 2)
    return [[pair[0:1], got[0:1]], [pair[1:2], got[1:2]]]


def after(values, earlier):
    return lax.optimization_barrier((values, earlier))[0]


def next_exchange(pieces, axis, level):
    masks = doubling_masks(lax.axis_size(axis))
    return [
        have + [swap(jnp.concatenate(have, 0), axis, masks[which][level])]
        for which, have in enumerate(pieces)
    ]


def per_device(source_top, adjoint_bottom, slowness, correction, slowness_ref, omega):
    row_parts = lax.axis_size("rows")
    sections = lax.axis_size("depth")
    group = lax.axis_index("depth")
    part_id = lax.axis_index("rows")
    freq_count = omega.shape[0]
    chains = 2 * freq_count
    rep = sections // chains
    rows_here, ny = slowness.shape[1:]
    nx = rows_here * row_parts
    dims = (nx, ny, rows_here)
    hy = ny // 2
    chain = lax.div(group, rep)
    forward = lax.div(chain, freq_count)
    freq = lax.rem(chain, freq_count)
    side = lax.rem(group, 2)
    half_sections = sections // 2
    masks = doubling_masks(row_parts)
    orders = [doubling_orders(m) for m in masks]
    rounds = len(masks[0])
    plan = (sections, freq_count)

    def pick(values, index):
        return lax.dynamic_index_in_dim(values, index, 0, keepdims=False)

    plane = jnp.where(forward == 1, pick(source_top, freq), pick(adjoint_bottom, freq))
    high = slowness_ref.astype(bf16)
    middle = (slowness_ref - high.astype(f32)).astype(bf16)
    low = (slowness_ref - high.astype(f32) - middle.astype(f32)).astype(bf16)
    terms = jnp.concatenate([high, middle, low, jnp.zeros((13,), bf16)])
    values = jnp.concatenate([correction[0], slowness[0] - slowness_ref[0]], 0).astype(bf16)
    values = jnp.concatenate([values, jnp.broadcast_to(terms[:, None], (16, ny))], 0)
    left, right = values[:, :hy], values[:, hy:]
    same = jnp.where(side == 0, left, right)
    other = jnp.where(side == 0, right, left)
    packed = jnp.stack([same, other])
    blocks, partner = [packed], []
    for k in range(1, sections):
        blocks.append(swap(packed if k < half_sections else (same, other)[k % 2], "depth", k))
    for k in range(half_sections, sections):
        sent = (same, other)[k % 2][: 2 * rows_here]
        mask = k * row_parts + row_parts // 2
        partner.append(swap(sent, ("depth", "rows"), mask))
    planes = first_exchange(plane, "rows")
    assert nx == ny
    tables = basis_tables(nx)
    for level in range(1, rounds):
        planes = next_exchange(planes, "rows", level)
        if level == 1:
            blocks, partner = after((blocks, partner), planes)
            pair, refs, coef_rows = run_sort(omega, blocks, partner, rows_here, hy)
            pieces = [[pair[0]], [pair[1]]]
            planes = after(planes, pair)
        before = pieces
        pieces = next_exchange(pieces, "rows", level)
    w = run_first(dims, orders, plan, refs, tables, after(planes[0] + planes[1], before))
    far_slots = [sections - 1 - slot for slot in range(half_sections, sections - 1)]
    early = before[0] + before[1]
    head = run_join(early, [(slot, range(len(early))) for slot in far_slots])
    head = [swap(h, "depth", half_sections) for h in head]
    last = after([have[-1] for have in pieces], (w, head))
    each = len(before[0])
    order = [*range(each), 2 * each, *range(each, 2 * each), 2 * each + 1]
    wanted = [(slot, order) for slot in range(half_sections)]
    wanted += [(slot, order[each :: each + 1]) for slot in far_slots]
    sides = [
        (sum(orders[j], []), order[j * (each + 1) : (j + 1) * (each + 1)]) for j in range(2)
    ]
    w, refs, *joined = run_join(early + last, wanted, (w, refs), sides)
    mine, rest = joined[:half_sections], joined[half_sections:]
    coefs = [[m, swap(m, "depth", 1)] for m in mine]
    far = [[h, swap(r, "depth", half_sections)] for h, r in zip(head, rest)]
    row_outs = []
    for slot in range(sections - 1):
        last = slot == sections - 2
        w, *rest = run_step(
            dims, orders, plan, slot, w, coefs[slot], refs, tables, coef_rows if last else None
        )
        if slot == half_sections - 1:
            coefs += [have + [swap(part, "depth", 1) for part in have] for have in after(far, w)]
        row_outs += [w, *rest] if last else rest

    def index_for(g, target):
        return target if g >= half_sections else sections - 2 - target

    def payload_for(mask):
        used = sorted(
            {index_for(g, g ^ mask) for g in range(sections) if index_for(g, g ^ mask) >= 0}
        )
        low = used[0]
        stack = jnp.stack(row_outs[low : used[-1] + 1])
        target = group ^ mask
        index = jnp.where(forward == 1, target, sections - 2 - target)
        return pick(stack, jnp.clip(index - low, 0, len(stack) - 1))

    far = [swap(payload_for(i * rep), "depth", i * rep) for i in range(freq_count, chains)]
    near = [payload_for(i * rep) for i in range(freq_count)]
    far, near = lax.optimization_barrier((far, near))
    fields = [f if i == 0 else swap(f, "depth", i * rep) for i, f in enumerate(near)] + far
    return run_image(plan, refs, fields, adjoint_bottom)


def solution(mesh):
    in_specs = (
        P(None, None, "rows", None),
        P(None, None, "rows", None),
        P("depth", "rows", None),
        P("depth", "rows", None),
        P("depth"),
        P(),
    )
    out_specs = P("depth", "rows", None)
    return jax.shard_map(
        per_device, mesh=mesh, in_specs=in_specs, out_specs=out_specs, check_vma=False
    )
```

```python
from functools import partial
import math

import jax
import jax.numpy as jnp
import numpy as np
from jax import lax
from jax.experimental import pallas as pl
from jax.experimental.pallas import tpu as pltpu
from jax.sharding import PartitionSpec as P

bf16 = jnp.bfloat16
f32 = jnp.float32
vmem_bytes = 32 * 1024 * 1024


def basis(length):
    half, quarter = length // 2, length // 4
    n = np.arange(half)[:, None]
    j = np.arange(quarter)[None, :]
    scale = math.sqrt(2.0 / length)
    even_cos = scale * np.cos(2 * np.pi * ((2 * j * n) % length) / length)
    even_sin = scale * np.sin(2 * np.pi * ((2 * j * n) % length) / length)
    even_cos[:, 0] = 1.0 / math.sqrt(length)
    even_sin[:, 0] = (1.0 - 2.0 * (np.arange(half) % 2)) / math.sqrt(length)
    odd_cos = scale * np.cos(2 * np.pi * (((2 * j + 1) * n) % length) / length)
    odd_sin = scale * np.sin(2 * np.pi * (((2 * j + 1) * n) % length) / length)
    even = np.concatenate([even_cos, even_sin], 1).astype(np.float32)
    odd = np.concatenate([odd_cos, odd_sin], 1).astype(np.float32)
    return even, odd


def basis_tables(length):
    even, odd = basis(length)
    half = length // 2
    near = np.eye(half, k=1) + np.eye(half, k=-1)
    across = np.eye(half, k=half - 1) + np.eye(half, k=1 - half)
    tables = [even, odd, even.T, odd.T, near - 4.0 * np.eye(half), near, across]
    return jnp.asarray(np.stack(tables).astype(np.float32), bf16)


def dot(a, b):
    return jnp.dot(a, b, preferred_element_type=f32)


def fitted(function, top, degree):
    fit = np.polynomial.Chebyshev.interpolate(function, degree, [0.0, top])
    return [float(c) for c in fit.convert(kind=np.polynomial.Polynomial).coef]


def horner(coefs, x):
    total = coefs[-1] * x + coefs[-2]
    for c in coefs[-3::-1]:
        total = total * x + c
    return total


def sinc_root(x):
    return np.sinc(np.sqrt(x) / np.pi)


def cos_root(x):
    return np.cos(np.sqrt(x))


lens_top = 0.45
lens_cos, lens_sin = fitted(cos_root, lens_top, 3), fitted(sinc_root, lens_top, 3)
phase_top = 3.2
phase_cos, phase_sin = fitted(cos_root, phase_top, 7), fitted(sinc_root, phase_top, 7)


def small_cos_sin(a):
    s = a * a
    return horner(lens_cos, s), a * horner(lens_sin, s)


def fill_phase(nx, ny, level, sign, out):
    qx, qy = nx // 4, ny // 4

    def waves(rows, cols, axis, parity, length):
        j = lax.broadcasted_iota(jnp.int32, (rows, cols), axis)
        return (2 * j + parity).astype(f32) * (2.0 * math.pi / length)

    def values(kx, ky):
        squared = level * level - kx * kx - ky * ky
        inside = jnp.maximum(squared, 0.0)
        damping = jnp.exp(-jnp.sqrt(jnp.maximum(-squared, 0.0)))
        sine = jnp.sqrt(inside) * horner(phase_sin, inside)
        return damping * horner(phase_cos, inside), sign * damping * sine

    edge = math.pi
    row_zero = lax.broadcasted_iota(jnp.int32, (qx, qy), 0) == 0
    col_zero = lax.broadcasted_iota(jnp.int32, (qx, qy), 1) == 0
    for px in range(2):
        for py in range(2):
            kx = waves(qx, qy, 0, px, nx)
            ky = waves(qx, qy, 1, py, ny)
            base = values(kx, ky)
            across = values(jnp.full((8, qy), edge), waves(8, qy, 1, py, ny))
            along = values(waves(qx, 1, 0, px, nx), jnp.full((qx, 1), edge))
            corner = values(jnp.full((8, 1), edge), jnp.full((8, 1), edge))
            for sx in range(2):
                for sy in range(2):
                    new_row, new_col = sx and not px, sy and not py
                    for part in range(2):
                        v = base[part]
                        if new_col:
                            v = jnp.where(col_zero, along[part], v)
                        if new_row:
                            v = jnp.where(row_zero, across[part][0:1], v)
                        if new_row and new_col:
                            v = jnp.where(row_zero & col_zero, corner[part][0:1], v)
                        rows = pl.ds((2 * px + sx) * qx, qx)
                        cols = pl.ds((2 * py + sy) * qy, qy)
                        out[part, rows, cols] = v.astype(bf16)


def place_of(plan):
    sections, freq_count = plan
    group = lax.axis_index("depth")
    chain = lax.div(group, jnp.int32(sections // (2 * freq_count)))
    forward = lax.div(chain, jnp.int32(freq_count))
    freq = lax.rem(chain, jnp.int32(freq_count))
    return lax.axis_index("rows"), forward, lax.rem(group, jnp.int32(2)), freq, group


vm = pl.BlockSpec(memory_space=pltpu.VMEM)
sm = pl.BlockSpec(memory_space=pltpu.SMEM)


def sort_kernel(rows_here, hy, plan, omega_ref, *refs):
    sections, freq_count = plan
    half_sections = sections // 2
    blocks, refs = refs[:sections], refs[sections:]
    partner, (pair, refs_out, coef_rows) = refs[:half_sections], refs[half_sections:]
    _, forward, side, freq, group = place_of(plan)
    omega = omega_ref[freq]
    for i in range(freq_count):
        refs_out[sections + i] = jnp.full((8, 128), omega_ref[freq ^ i], f32)

    def block_of(k):
        return blocks[k].at[k % 2] if k < half_sections else blocks[k]

    def chosen(index, first, body):
        for k in range(first, sections):
            pl.when(index == k)(partial(body, k))

    for slot in range(half_sections):
        depth = jnp.where(forward == 1, slot, sections - 1 - slot)

        def place(k, slot=slot):
            for j in range(2):
                part = pl.ds(j * rows_here, rows_here)
                pair[j, 0, slot] = blocks[k][part, :]
                pair[j, 1, slot] = partner[k - half_sections][part, :]

        chosen(group ^ depth, half_sections, place)
    for slot in range(sections):
        depth = jnp.where(forward == 1, slot, (sections - slot) % sections)

        def level(k, slot=slot):
            parts = block_of(k)[pl.ds(2 * rows_here, 16), pl.ds(0, 128)].astype(f32)
            refs_out[slot] = jnp.broadcast_to(omega * (parts[0:1] + parts[1:2] + parts[2:3]), (8, 128))

        chosen(group ^ depth, 0, level)

    for k in range(half_sections):

        @pl.when(jnp.clip(group ^ (sections - 1), 0, half_sections - 1) == k)
        def _(k=k):
            for i in range(2):
                cols = pl.ds(pl.multiple_of((side ^ (k % 2) ^ i) * hy, hy), hy)
                block = blocks[k].at[i]
                for j in range(2):
                    coef_rows[j, :, cols] = block[pl.ds(j * rows_here, rows_here), :]


def run_sort(omega, blocks, partner, rows_here, hy):
    sections = len(blocks)
    return pl.pallas_call(
        partial(sort_kernel, rows_here, hy, (sections, omega.shape[0])),
        out_shape=(
            jax.ShapeDtypeStruct((2, 2, sections // 2, rows_here, hy), bf16),
            jax.ShapeDtypeStruct((sections + omega.shape[0], 8, 128), f32),
            jax.ShapeDtypeStruct((2, rows_here, 2 * hy), bf16),
        ),
        in_specs=[sm] + [vm] * (sections + len(partner)),
        out_specs=(vm, vm, vm),
        compiler_params=pltpu.CompilerParams(vmem_limit_bytes=vmem_bytes),
        name="sort_depths",
    )(omega, *blocks, *partner)


def fold_cols(values):
    half = values.shape[1] // 2
    a, b = values[:, :half], values[:, half:]
    return (a + b).astype(bf16), (a - b).astype(bf16)


def add_subtract(mid, part, par, hx, hy, top, low):
    cols = pl.ds(par * hy, hy)
    mid[part, pl.ds(0, hx), cols] = (top + low).astype(bf16)
    mid[part, pl.ds(hx, hx), cols] = (top - low).astype(bf16)


def forward_rows(nx, ny, folded, qy_ref, mid):
    hx, hy = nx // 2, ny // 2
    for part in range(2):
        for par in range(2):
            cols = pl.ds(par * hy, hy)
            top = dot(folded[part, pl.ds(0, hx), cols], qy_ref[par])
            low = dot(folded[part, pl.ds(hx, hx), cols], qy_ref[par])
            add_subtract(mid, part, par, hx, hy, top, low)


def through_columns(nx, ny, mid, phase, qx_ref, spec):
    hx, hy = nx // 2, ny // 2
    for start in range(0, ny, hy):
        cols = pl.ds(start, hy)
        back = []
        for par in range(2):
            rows = pl.ds(par * hx, hx)
            zr = dot(qx_ref[2 + par], mid[0, rows, cols])
            zi = dot(qx_ref[2 + par], mid[1, rows, cols])
            pr = phase[0, rows, cols].astype(f32)
            pi = phase[1, rows, cols].astype(f32)
            yr = (zr * pr - zi * pi).astype(bf16)
            yi = (zr * pi + zi * pr).astype(bf16)
            back.append((dot(qx_ref[par], yr), dot(qx_ref[par], yi)))
        for part in range(2):
            a, b = back[0][part], back[1][part]
            spec[part, pl.ds(0, hx), cols] = (a + b).astype(bf16)
            spec[part, pl.ds(hx, hx), cols] = (a - b).astype(bf16)


def inverse_rows(ny, pieces, spec, qy_ref, out):
    hy = ny // 2
    for part in range(2):
        for start, count in pieces:
            rows = pl.ds(start, count)
            a = dot(spec[part, rows, pl.ds(0, hy)], qy_ref[2])
            b = dot(spec[part, rows, pl.ds(hy, hy)], qy_ref[3])
            out[part, rows, pl.ds(0, hy)] = (a + b).astype(bf16)
            out[part, rows, pl.ds(hy, hy)] = (a - b).astype(bf16)


def laplace_block(src, part, block, hx, hy, qx_ref, qy_ref):
    rows = pl.ds(block * hx, hx)
    left, right = src[part, rows, pl.ds(0, hy)], src[part, rows, pl.ds(hy, hy)]
    sums = []
    for own, other in ((left, right), (right, left)):
        sums.append(dot(qx_ref[4], own) + dot(own, qy_ref[5]) + dot(other, qy_ref[6]))
    return sums


def half_ends(nx):
    hx = nx // 2
    return [(0, nx - 1), (hx - 1, hx), (hx, hx - 1), (nx - 1, 0)]


def one_row(src, part, row):
    return src[part, pl.ds(row // 16 * 16, 16), :].astype(f32)[row % 16 : row % 16 + 1]


def first_kernel(dims, orders, plan, refs_ref, tables, *rest):
    nx, ny, rows_here = dims
    counts = [len(o) for o in orders]
    pieces, (out, folded, mid, spec, phase) = rest[: sum(counts)], rest[sum(counts) :]
    qx_ref = qy_ref = tables
    part_id, forward, _, _, _ = place_of(plan)
    at = 0
    for part, order in enumerate(orders):
        for piece_order in order:
            piece = pieces[at]
            at += 1
            for i, offset in enumerate(piece_order):
                block = part_id ^ offset
                rows = pl.ds(pl.multiple_of(block * rows_here, rows_here), rows_here)
                values = piece[i]

                @pl.when(forward == 1)
                def _():
                    a, b = fold_cols(values.astype(f32))
                    folded[part, rows, pl.ds(0, ny // 2)] = a
                    folded[part, rows, pl.ds(ny // 2, ny // 2)] = b

                @pl.when(forward == 0)
                def _():
                    out[part, rows, :] = values

    @pl.when(forward == 1)
    def _():
        fill_phase(nx, ny, refs_ref[0, 0:1, 0:1], 1.0, phase)
        forward_rows(nx, ny, folded, qy_ref, mid)
        through_columns(nx, ny, mid, phase, qx_ref, spec)
        inverse_rows(ny, [(start, nx // 2) for start in (0, nx // 2)], spec, qy_ref, out)


def laplace_rows(ref, part, start, count):
    center = ref[part, pl.ds(start + 8, count), :]
    width = center.shape[1]
    return (
        ref[part, pl.ds(start + 7, count), :]
        + ref[part, pl.ds(start + 9, count), :]
        + pltpu.roll(center, 1, 1)
        + pltpu.roll(center, width - 1, 1)
        - 4.0 * center
    )


def step_kernel(dims, orders, plan, index, parts, last, w_ref, refs_ref, tables, *rest):
    nx, ny, rows_here = dims
    qx_ref = qy_ref = tables
    coefs, rest = rest[: 2 * parts], rest[2 * parts :]
    coefs = (coefs[:parts], coefs[parts:])
    if last:
        coef_rows, out_rows, end_rows, out, plane, scaled, mid, spec, phase, tall, edge_rows = rest
    else:
        out, out_rows, plane, scaled, mid, spec, phase = rest
    part_id, forward, side, _, _ = place_of(plan)
    omega = refs_ref[plan[0], 0:1, 0:1]
    hy = ny // 2
    blocks = nx // rows_here
    place = []
    for which, order in enumerate(orders):
        share = blocks // parts
        place.append(
            {o: (i // share, which * share + i % share) for i, o in enumerate(sum(order, []))}
        )
    step = min(32, rows_here)

    def portions():
        for offset in range(blocks):
            for sub in range(0, rows_here, step):
                start = pl.multiple_of((part_id ^ offset) * rows_here + sub, step)
                yield offset, sub, start

    def lens_at(q, offset, sub):
        cols = pl.ds(pl.multiple_of((side ^ q) * hy, hy), hy)
        rows = pl.ds(sub, step)
        (ca, ci), (da, di) = place[0][offset], place[1][offset]
        c = coefs[q][ca][ci, rows, :].astype(f32)
        cos, sin = small_cos_sin(omega * coefs[q][da][di, rows, :].astype(f32))
        return cols, c, cos, sin

    hx = nx // 2
    first = pl.multiple_of(part_id * rows_here, rows_here)
    mine = pl.ds(first, rows_here)

    @pl.when(forward == 1)
    def _():
        for offset, sub, start in portions():
            rows = pl.ds(start, step)
            for q in range(2):
                cols, c, lr, li = lens_at(q, offset, sub)
                wr, wi = w_ref[0, rows, cols].astype(f32), w_ref[1, rows, cols].astype(f32)
                ur, ui = wr * lr - wi * li, wr * li + wi * lr
                plane[0, rows, cols] = ur
                plane[1, rows, cols] = ui
                scaled[0, rows, cols] = (c * ur).astype(bf16)
                scaled[1, rows, cols] = (c * ui).astype(bf16)
        for row, beside in half_ends(nx):
            plane[0, pl.ds(row, 1), :] -= one_row(scaled, 1, beside)
            plane[1, pl.ds(row, 1), :] += one_row(scaled, 0, beside)
        spectra = []
        for block in range(2):
            rows = pl.ds(block * hx, hx)
            sums = [laplace_block(scaled, part, block, hx, hy, qx_ref, qy_ref) for part in range(2)]
            for part in range(2):
                left, right = plane[part, rows, pl.ds(0, hy)], plane[part, rows, pl.ds(hy, hy)]
                l, r = sums[1 - part]
                left, right = (left + l, right + r) if part else (left - l, right - r)
                spec[part, rows, pl.ds(0, hy)] = left.astype(bf16)
                spec[part, rows, pl.ds(hy, hy)] = right.astype(bf16)
                spectra.append(
                    (
                        dot((left + right).astype(bf16), qy_ref[0]),
                        dot((left - right).astype(bf16), qy_ref[1]),
                    )
                )
        for part in range(2):
            for par in range(2):
                add_subtract(mid, part, par, hx, hy, spectra[part][par], spectra[2 + part][par])
        for part in range(2):
            out_rows[part] = spec[part, mine, :]

    @pl.when(forward == 0)
    def _():
        for part in range(2):
            for block in range(2):
                rows = pl.ds(block * hx, hx)
                l, r = laplace_block(w_ref, part, block, hx, hy, qx_ref, qy_ref)
                plane[part, rows, pl.ds(0, hy)] = l
                plane[part, rows, pl.ds(hy, hy)] = r
            for row, beside in half_ends(nx):
                plane[part, pl.ds(row, 1), :] += one_row(w_ref, part, beside)
        flip = (1 - 2 * side).astype(f32)
        for offset, sub, start in portions():
            rows = pl.ds(start, step)
            halves = []
            for q in range(2):
                cols, c, lr, li = lens_at(q, offset, sub)
                tr = w_ref[0, rows, cols].astype(f32) + c * plane[1, rows, cols]
                ti = w_ref[1, rows, cols].astype(f32) - c * plane[0, rows, cols]
                halves.append((tr * lr + ti * li, ti * lr - tr * li))
            for part in range(2):
                a, b = halves[0][part], halves[1][part]
                scaled[part, rows, pl.ds(0, hy)] = (a + b).astype(bf16)
                scaled[part, rows, pl.ds(hy, hy)] = (flip * (a - b)).astype(bf16)
        forward_rows(nx, ny, scaled, qy_ref, mid)

    fill_phase(nx, ny, refs_ref[index + 1, 0:1, 0:1], (2 * forward - 1).astype(f32), phase)
    through_columns(nx, ny, mid, phase, qx_ref, spec)
    before_start = pl.multiple_of(lax.rem(first + nx - 16, nx), 16)
    after_start = pl.multiple_of(lax.rem(first + rows_here, nx), 16)
    if last:
        wanted = [(first, rows_here), (before_start, 16), (after_start, 16)]
    else:
        wanted = [(start, hx) for start in (0, hx)]
    inverse_rows(ny, wanted, spec, qy_ref, out)

    @pl.when(forward == 0)
    def _():
        for part in range(2):
            out_rows[part] = out[part, mine, :]

    if not last:
        return
    for q in range(2):
        cols = pl.ds(pl.multiple_of((side ^ q) * hy, hy), hy)
        for i in range(2):
            for j in range(2):
                row = (2 * i + j) * 16
                rows = pl.ds(row % rows_here, 16)
                edge_rows[i, j, :, cols] = coefs[q][-1][2 * (blocks // parts) + row // rows_here, rows, :]

    @pl.when(forward == 0)
    def _():
        end_rows[...] = jnp.zeros_like(end_rows)

    @pl.when(forward == 1)
    def _():
        before = pl.ds(before_start, 16)
        after = pl.ds(after_start, 16)

        def lensed(values, c, d):
            lr, li = small_cos_sin(omega * d.astype(f32))
            wr, wi = values[0].astype(f32), values[1].astype(f32)
            ur, ui = wr * lr - wi * li, wr * li + wi * lr
            cf = c.astype(f32)
            return ur, ui, cf * ur, cf * ui

        ur, ui, gr, gi = lensed(
            (out[0, mine, :], out[1, mine, :]), coef_rows[0], coef_rows[1]
        )
        tall[0, pl.ds(8, rows_here), :] = gr
        tall[1, pl.ds(8, rows_here), :] = gi
        _, _, gr, gi = lensed(
            (out[0, before, :][15:16], out[1, before, :][15:16]), edge_rows[0, 0, 15:16, :], edge_rows[0, 1, 15:16, :]
        )
        tall[0, pl.ds(7, 1), :] = gr
        tall[1, pl.ds(7, 1), :] = gi
        _, _, gr, gi = lensed(
            (out[0, after, :][0:1], out[1, after, :][0:1]), edge_rows[1, 0, 0:1, :], edge_rows[1, 1, 0:1, :]
        )
        tall[0, pl.ds(rows_here + 8, 1), :] = gr
        tall[1, pl.ds(rows_here + 8, 1), :] = gi
        end_rows[0] = (ur - laplace_rows(tall, 1, 0, rows_here)).astype(bf16)
        end_rows[1] = (ui + laplace_rows(tall, 0, 0, rows_here)).astype(bf16)


def run_first(dims, orders, plan, refs, tables, pieces):
    nx, ny, _ = dims
    return pl.pallas_call(
        partial(first_kernel, dims, orders, plan),
        out_shape=jax.ShapeDtypeStruct((2, nx, ny), bf16),
        in_specs=[vm, vm] + [vm] * len(pieces),
        out_specs=vm,
        scratch_shapes=[pltpu.VMEM((2, nx, ny), bf16)] * 4,
        compiler_params=pltpu.CompilerParams(vmem_limit_bytes=vmem_bytes),
        cost_estimate=pl.CostEstimate(flops=2**30, bytes_accessed=2**22, transcendentals=0),
        name="first_step",
    )(refs, tables, *pieces)


def run_step(dims, orders, plan, index, w, coefs, refs, tables, coef_rows=None):
    nx, ny, rows_here = dims
    last = coef_rows is not None
    rows_shape = jax.ShapeDtypeStruct((2, rows_here, ny), bf16)
    full = pltpu.VMEM((2, nx, ny), bf16)
    scratch = [pltpu.VMEM((2, nx, ny), f32)]
    scratch += [full] * 4
    if last:
        outs = (rows_shape, rows_shape)
        scratch = [full] + scratch + [pltpu.VMEM((2, rows_here + 16, ny), f32)]
        scratch += [pltpu.VMEM((2, 2, 16, ny), bf16)]
    else:
        outs = (jax.ShapeDtypeStruct((2, nx, ny), bf16), rows_shape)
    return pl.pallas_call(
        partial(step_kernel, dims, orders, plan, index, len(coefs) // 2, last),
        out_shape=outs,
        in_specs=[vm] * (3 + len(coefs) + (1 if last else 0)),
        out_specs=(vm,) * len(outs),
        scratch_shapes=scratch,
        compiler_params=pltpu.CompilerParams(vmem_limit_bytes=vmem_bytes),
        cost_estimate=pl.CostEstimate(flops=2**32, bytes_accessed=2**24, transcendentals=0),
        name="end_step" if last else "depth_step",
    )(w, refs, tables, *coefs, *([coef_rows] if last else []))


def join_kernel(counts, wanted, sides, *refs):
    count = len(counts)
    kept = (len(refs) - count - len(wanted)) // 2
    pieces, outs = refs[kept : kept + count], refs[2 * kept + count :]
    for (slot, chosen), out in zip(wanted, outs):
        at = 0
        for which in chosen:
            for i in range(counts[which]):
                out[at + i] = pieces[which][i, slot]
            at += counts[which]
    if not sides:
        return
    rows_here = pieces[0].shape[2]
    size = sum(counts) // 2
    part_id = lax.axis_index("rows")
    for i, (beside, first) in enumerate(((size - 1, rows_here - 16), (1, 0))):
        offset_wanted = part_id ^ lax.rem(part_id + beside, size)
        for j, (order, chosen) in enumerate(sides):
            places = [(which, k) for which in chosen for k in range(counts[which])]
            row = (2 * i + j) * 16
            target = outs[-1].at[at + row // rows_here, pl.ds(row % rows_here, 16)]
            for offset, (which, k) in zip(order, places):

                @pl.when(offset_wanted == offset)
                def _(which=which, k=k, first=first, target=target):
                    target[...] = pieces[which][k, 0, pl.ds(first, 16), :]


def run_join(pieces, wanted, kept=(), sides=()):
    _, _, rows_here, hy = pieces[0].shape
    counts = [piece.shape[0] for piece in pieces]
    shapes = [(sum(counts[i] for i in chosen), rows_here, hy) for _, chosen in wanted]
    if sides:
        shapes[-1] = (shapes[-1][0] + -(-64 // rows_here), rows_here, hy)
    return pl.pallas_call(
        partial(join_kernel, counts, wanted, sides),
        out_shape=[jax.ShapeDtypeStruct(k.shape, k.dtype) for k in kept]
        + [jax.ShapeDtypeStruct(shape, bf16) for shape in shapes],
        in_specs=[vm] * (len(kept) + len(pieces)),
        out_specs=[vm] * (len(kept) + len(shapes)),
        input_output_aliases={i: i for i in range(len(kept))},
        compiler_params=pltpu.CompilerParams(vmem_limit_bytes=vmem_bytes),
        cost_estimate=pl.CostEstimate(flops=0, bytes_accessed=2**18, transcendentals=0),
        name="join_pieces",
    )(*kept, *pieces)


def image_kernel(plan, refs_ref, *refs):
    sections, freq_count = plan
    fields, (bottom, out) = refs[:-2], refs[-2:]
    _, forward, _, freq, group = place_of(plan)

    def total(adjoint_at):
        result = None
        for i in range(freq_count):
            freq_i = freq ^ i
            adjoint = adjoint_at(i, freq_i)
            a = [fields[i][j].astype(f32) for j in range(2)]
            b = [adjoint[j].astype(f32) for j in range(2)]
            weight = refs_ref[sections + i, 0:1, 0:1] * (2 * forward - 1).astype(f32)
            term = weight * (a[0] * b[1] - a[1] * b[0])
            result = term if result is None else result + term
        out[0] = result

    @pl.when(group == sections - 1)
    def _():
        total(lambda i, freq_i: bottom.at[freq_i])

    @pl.when(group != sections - 1)
    def _():
        total(lambda i, freq_i: fields[freq_count + i])


def run_image(plan, refs, fields, bottom):
    _, rows_here, ny = fields[0].shape
    return pl.pallas_call(
        partial(image_kernel, plan),
        out_shape=jax.ShapeDtypeStruct((1, rows_here, ny), f32),
        in_specs=[vm] * (len(fields) + 2),
        out_specs=vm,
        compiler_params=pltpu.CompilerParams(vmem_limit_bytes=vmem_bytes),
        name="image",
    )(refs, *fields, bottom)


def swap(values, axis, mask):
    axes = axis if isinstance(axis, tuple) else (axis,)
    size = math.prod(lax.axis_size(a) for a in axes)
    return lax.ppermute(values, axis, [(i, i ^ mask) for i in range(size)])


def doubling_masks(size):
    masks = []
    mask = size // 2
    while mask:
        masks.append(mask)
        mask //= 2
    descending = masks
    ascending = masks[:1] + masks[1:][::-1]
    return descending, ascending


def doubling_orders(masks):
    orders = [[0]]
    seen = [0]
    for mask in masks:
        new = [mask ^ o for o in seen]
        orders.append(new)
        seen = seen + new
    return orders


def first_exchange(pair, axis):
    size = lax.axis_size(axis)
    got = swap(pair, axis, size // 2)
    return [[pair[0:1], got[0:1]], [pair[1:2], got[1:2]]]


def after(values, earlier):
    return lax.optimization_barrier((values, earlier))[0]


def next_exchange(pieces, axis, level):
    masks = doubling_masks(lax.axis_size(axis))
    return [
        have + [swap(jnp.concatenate(have, 0), axis, masks[which][level])]
        for which, have in enumerate(pieces)
    ]


def per_device(source_top, adjoint_bottom, slowness, correction, slowness_ref, omega):
    row_parts = lax.axis_size("rows")
    sections = lax.axis_size("depth")
    group = lax.axis_index("depth")
    part_id = lax.axis_index("rows")
    freq_count = omega.shape[0]
    chains = 2 * freq_count
    rep = sections // chains
    rows_here, ny = slowness.shape[1:]
    nx = rows_here * row_parts
    dims = (nx, ny, rows_here)
    hy = ny // 2
    chain = lax.div(group, rep)
    forward = lax.div(chain, freq_count)
    freq = lax.rem(chain, freq_count)
    side = lax.rem(group, 2)
    half_sections = sections // 2
    masks = doubling_masks(row_parts)
    orders = [doubling_orders(m) for m in masks]
    rounds = len(masks[0])
    plan = (sections, freq_count)

    def pick(values, index):
        return lax.dynamic_index_in_dim(values, index, 0, keepdims=False)

    plane = jnp.where(forward == 1, pick(source_top, freq), pick(adjoint_bottom, freq))
    high = slowness_ref.astype(bf16)
    middle = (slowness_ref - high.astype(f32)).astype(bf16)
    low = (slowness_ref - high.astype(f32) - middle.astype(f32)).astype(bf16)
    terms = jnp.concatenate([high, middle, low, jnp.zeros((13,), bf16)])
    values = jnp.concatenate([correction[0], slowness[0] - slowness_ref[0]], 0).astype(bf16)
    values = jnp.concatenate([values, jnp.broadcast_to(terms[:, None], (16, ny))], 0)
    left, right = values[:, :hy], values[:, hy:]
    same = jnp.where(side == 0, left, right)
    other = jnp.where(side == 0, right, left)
    packed = jnp.stack([same, other])
    blocks, partner = [packed], []
    for k in range(1, sections):
        blocks.append(swap(packed if k < half_sections else (same, other)[k % 2], "depth", k))
    for k in range(half_sections, sections):
        sent = (same, other)[k % 2][: 2 * rows_here]
        mask = k * row_parts + row_parts // 2
        partner.append(swap(sent, ("depth", "rows"), mask))
    planes = first_exchange(plane, "rows")
    assert nx == ny
    tables = basis_tables(nx)
    for level in range(1, rounds):
        planes = next_exchange(planes, "rows", level)
        if level == 1:
            blocks, partner = after((blocks, partner), planes)
            pair, refs, coef_rows = run_sort(omega, blocks, partner, rows_here, hy)
            pieces = [[pair[0]], [pair[1]]]
            planes = after(planes, pair)
        before = pieces
        pieces = next_exchange(pieces, "rows", level)
    w = run_first(dims, orders, plan, refs, tables, after(planes[0] + planes[1], before))
    far_slots = [sections - 1 - slot for slot in range(half_sections, sections - 1)]
    early = before[0] + before[1]
    head = run_join(early, [(slot, range(len(early))) for slot in far_slots])
    head = [swap(h, "depth", half_sections) for h in head]
    last = after([have[-1] for have in pieces], (w, head))
    each = len(before[0])
    order = [*range(each), 2 * each, *range(each, 2 * each), 2 * each + 1]
    wanted = [(slot, order) for slot in range(half_sections)]
    wanted += [(slot, order[each :: each + 1]) for slot in far_slots]
    sides = [
        (sum(orders[j], []), order[j * (each + 1) : (j + 1) * (each + 1)]) for j in range(2)
    ]
    w, refs, *joined = run_join(early + last, wanted, (w, refs), sides)
    mine, rest = joined[:half_sections], joined[half_sections:]
    coefs = [[m, swap(m, "depth", 1)] for m in mine]
    far = [[h, swap(r, "depth", half_sections)] for h, r in zip(head, rest)]
    row_outs = []
    for slot in range(sections - 1):
        last = slot == sections - 2
        w, *rest = run_step(
            dims, orders, plan, slot, w, coefs[slot], refs, tables, coef_rows if last else None
        )
        if slot == half_sections - 1:
            coefs += [have + [swap(part, "depth", 1) for part in have] for have in after(far, w)]
        row_outs += [w, *rest] if last else rest

    def index_for(g, target):
        return target if g >= half_sections else sections - 2 - target

    def payload_for(mask):
        used = sorted(
            {index_for(g, g ^ mask) for g in range(sections) if index_for(g, g ^ mask) >= 0}
        )
        low = used[0]
        stack = jnp.stack(row_outs[low : used[-1] + 1])
        target = group ^ mask
        index = jnp.where(forward == 1, target, sections - 2 - target)
        return pick(stack, jnp.clip(index - low, 0, len(stack) - 1))

    far = [swap(payload_for(i * rep), "depth", i * rep) for i in range(freq_count, chains)]
    near = [payload_for(i * rep) for i in range(freq_count)]
    fields = [f if i == 0 else swap(f, "depth", i * rep) for i, f in enumerate(near)] + far
    return run_image(plan, refs, fields, adjoint_bottom)


def solution(mesh):
    in_specs = (
        P(None, None, "rows", None),
        P(None, None, "rows", None),
        P("depth", "rows", None),
        P("depth", "rows", None),
        P("depth"),
        P(),
    )
    out_specs = P("depth", "rows", None)
    return jax.shard_map(
        per_device, mesh=mesh, in_specs=in_specs, out_specs=out_specs, check_vma=False
    )
```

```python
from functools import partial
import math

import jax
import jax.numpy as jnp
import numpy as np
from jax import lax
from jax.experimental import pallas as pl
from jax.experimental.pallas import tpu as pltpu
from jax.sharding import PartitionSpec as P

bf16 = jnp.bfloat16
f32 = jnp.float32
vmem_bytes = 32 * 1024 * 1024


def basis(length):
    half, quarter = length // 2, length // 4
    n = np.arange(half)[:, None]
    j = np.arange(quarter)[None, :]
    scale = math.sqrt(2.0 / length)
    even_cos = scale * np.cos(2 * np.pi * ((2 * j * n) % length) / length)
    even_sin = scale * np.sin(2 * np.pi * ((2 * j * n) % length) / length)
    even_cos[:, 0] = 1.0 / math.sqrt(length)
    even_sin[:, 0] = (1.0 - 2.0 * (np.arange(half) % 2)) / math.sqrt(length)
    odd_cos = scale * np.cos(2 * np.pi * (((2 * j + 1) * n) % length) / length)
    odd_sin = scale * np.sin(2 * np.pi * (((2 * j + 1) * n) % length) / length)
    even = np.concatenate([even_cos, even_sin], 1).astype(np.float32)
    odd = np.concatenate([odd_cos, odd_sin], 1).astype(np.float32)
    return even, odd


def basis_tables(length):
    even, odd = basis(length)
    half = length // 2
    near = np.eye(half, k=1) + np.eye(half, k=-1)
    across = np.eye(half, k=half - 1) + np.eye(half, k=1 - half)
    tables = [even, odd, even.T, odd.T, near - 4.0 * np.eye(half), near, across]
    return jnp.asarray(np.stack(tables).astype(np.float32), bf16)


def dot(a, b):
    return jnp.dot(a, b, preferred_element_type=f32)


def fitted(function, top, degree):
    fit = np.polynomial.Chebyshev.interpolate(function, degree, [0.0, top])
    return [float(c) for c in fit.convert(kind=np.polynomial.Polynomial).coef]


def horner(coefs, x):
    total = coefs[-1] * x + coefs[-2]
    for c in coefs[-3::-1]:
        total = total * x + c
    return total


def sinc_root(x):
    return np.sinc(np.sqrt(x) / np.pi)


def cos_root(x):
    return np.cos(np.sqrt(x))


lens_top = 0.45
lens_cos, lens_sin = fitted(cos_root, lens_top, 3), fitted(sinc_root, lens_top, 3)
phase_top = 3.2
phase_cos, phase_sin = fitted(cos_root, phase_top, 7), fitted(sinc_root, phase_top, 7)


def small_cos_sin(a):
    s = a * a
    return horner(lens_cos, s), a * horner(lens_sin, s)


def fill_phase(nx, ny, level, sign, out):
    qx, qy = nx // 4, ny // 4

    def waves(rows, cols, axis, parity, length):
        j = lax.broadcasted_iota(jnp.int32, (rows, cols), axis)
        return (2 * j + parity).astype(f32) * (2.0 * math.pi / length)

    def values(kx, ky):
        squared = level * level - kx * kx - ky * ky
        inside = jnp.maximum(squared, 0.0)
        damping = jnp.exp(-jnp.sqrt(jnp.maximum(-squared, 0.0)))
        sine = jnp.sqrt(inside) * horner(phase_sin, inside)
        return damping * horner(phase_cos, inside), sign * damping * sine

    edge = math.pi
    row_zero = lax.broadcasted_iota(jnp.int32, (qx, qy), 0) == 0
    col_zero = lax.broadcasted_iota(jnp.int32, (qx, qy), 1) == 0
    for px in range(2):
        for py in range(2):
            kx = waves(qx, qy, 0, px, nx)
            ky = waves(qx, qy, 1, py, ny)
            base = values(kx, ky)
            across = values(jnp.full((8, qy), edge), waves(8, qy, 1, py, ny))
            along = values(waves(qx, 1, 0, px, nx), jnp.full((qx, 1), edge))
            corner = values(jnp.full((8, 1), edge), jnp.full((8, 1), edge))
            for sx in range(2):
                for sy in range(2):
                    new_row, new_col = sx and not px, sy and not py
                    for part in range(2):
                        v = base[part]
                        if new_col:
                            v = jnp.where(col_zero, along[part], v)
                        if new_row:
                            v = jnp.where(row_zero, across[part][0:1], v)
                        if new_row and new_col:
                            v = jnp.where(row_zero & col_zero, corner[part][0:1], v)
                        rows = pl.ds((2 * px + sx) * qx, qx)
                        cols = pl.ds((2 * py + sy) * qy, qy)
                        out[part, rows, cols] = v.astype(bf16)


def place_of(plan):
    sections, freq_count = plan
    group = lax.axis_index("depth")
    chain = lax.div(group, jnp.int32(sections // (2 * freq_count)))
    forward = lax.div(chain, jnp.int32(freq_count))
    freq = lax.rem(chain, jnp.int32(freq_count))
    return lax.axis_index("rows"), forward, lax.rem(group, jnp.int32(2)), freq, group


vm = pl.BlockSpec(memory_space=pltpu.VMEM)
sm = pl.BlockSpec(memory_space=pltpu.SMEM)


def sort_kernel(rows_here, hy, plan, omega_ref, *refs):
    sections, freq_count = plan
    half_sections = sections // 2
    blocks, refs = refs[:sections], refs[sections:]
    partner, (pair, refs_out, coef_rows) = refs[:half_sections], refs[half_sections:]
    _, forward, side, freq, group = place_of(plan)
    omega = omega_ref[freq]
    for i in range(freq_count):
        refs_out[sections + i] = jnp.full((8, 128), omega_ref[freq ^ i], f32)

    def block_of(k):
        return blocks[k].at[k % 2] if k < half_sections else blocks[k]

    def chosen(index, first, body):
        for k in range(first, sections):
            pl.when(index == k)(partial(body, k))

    for slot in range(half_sections):
        depth = jnp.where(forward == 1, slot, sections - 1 - slot)

        def place(k, slot=slot):
            for j in range(2):
                part = pl.ds(j * rows_here, rows_here)
                pair[j, 0, slot] = blocks[k][part, :]
                pair[j, 1, slot] = partner[k - half_sections][part, :]

        chosen(group ^ depth, half_sections, place)
    for slot in range(sections):
        depth = jnp.where(forward == 1, slot, (sections - slot) % sections)

        def level(k, slot=slot):
            parts = block_of(k)[pl.ds(2 * rows_here, 16), pl.ds(0, 128)].astype(f32)
            refs_out[slot] = jnp.broadcast_to(omega * (parts[0:1] + parts[1:2] + parts[2:3]), (8, 128))

        chosen(group ^ depth, 0, level)

    for k in range(half_sections):

        @pl.when(jnp.clip(group ^ (sections - 1), 0, half_sections - 1) == k)
        def _(k=k):
            for i in range(2):
                cols = pl.ds(pl.multiple_of((side ^ (k % 2) ^ i) * hy, hy), hy)
                block = blocks[k].at[i]
                for j in range(2):
                    coef_rows[j, :, cols] = block[pl.ds(j * rows_here, rows_here), :]


def run_sort(omega, blocks, partner, rows_here, hy):
    sections = len(blocks)
    return pl.pallas_call(
        partial(sort_kernel, rows_here, hy, (sections, omega.shape[0])),
        out_shape=(
            jax.ShapeDtypeStruct((2, 2, sections // 2, rows_here, hy), bf16),
            jax.ShapeDtypeStruct((sections + omega.shape[0], 8, 128), f32),
            jax.ShapeDtypeStruct((2, rows_here, 2 * hy), bf16),
        ),
        in_specs=[sm] + [vm] * (sections + len(partner)),
        out_specs=(vm, vm, vm),
        compiler_params=pltpu.CompilerParams(vmem_limit_bytes=vmem_bytes),
        name="sort_depths",
    )(omega, *blocks, *partner)


def fold_cols(values):
    half = values.shape[1] // 2
    a, b = values[:, :half], values[:, half:]
    return (a + b).astype(bf16), (a - b).astype(bf16)


def add_subtract(mid, part, par, hx, hy, top, low):
    cols = pl.ds(par * hy, hy)
    mid[part, pl.ds(0, hx), cols] = (top + low).astype(bf16)
    mid[part, pl.ds(hx, hx), cols] = (top - low).astype(bf16)


def forward_rows(nx, ny, folded, qy_ref, mid):
    hx, hy = nx // 2, ny // 2
    for part in range(2):
        for par in range(2):
            cols = pl.ds(par * hy, hy)
            top = dot(folded[part, pl.ds(0, hx), cols], qy_ref[par])
            low = dot(folded[part, pl.ds(hx, hx), cols], qy_ref[par])
            add_subtract(mid, part, par, hx, hy, top, low)


def through_columns(nx, ny, mid, phase, qx_ref, spec):
    hx, hy = nx // 2, ny // 2
    for start in range(0, ny, hy):
        cols = pl.ds(start, hy)
        back = []
        for par in range(2):
            rows = pl.ds(par * hx, hx)
            zr = dot(qx_ref[2 + par], mid[0, rows, cols])
            zi = dot(qx_ref[2 + par], mid[1, rows, cols])
            pr = phase[0, rows, cols].astype(f32)
            pi = phase[1, rows, cols].astype(f32)
            yr = (zr * pr - zi * pi).astype(bf16)
            yi = (zr * pi + zi * pr).astype(bf16)
            back.append((dot(qx_ref[par], yr), dot(qx_ref[par], yi)))
        for part in range(2):
            a, b = back[0][part], back[1][part]
            spec[part, pl.ds(0, hx), cols] = (a + b).astype(bf16)
            spec[part, pl.ds(hx, hx), cols] = (a - b).astype(bf16)


def inverse_rows(ny, pieces, spec, qy_ref, out):
    hy = ny // 2
    for part in range(2):
        for start, count in pieces:
            rows = pl.ds(start, count)
            a = dot(spec[part, rows, pl.ds(0, hy)], qy_ref[2])
            b = dot(spec[part, rows, pl.ds(hy, hy)], qy_ref[3])
            out[part, rows, pl.ds(0, hy)] = (a + b).astype(bf16)
            out[part, rows, pl.ds(hy, hy)] = (a - b).astype(bf16)


def laplace_block(src, part, block, hx, hy, qx_ref, qy_ref):
    rows = pl.ds(block * hx, hx)
    left, right = src[part, rows, pl.ds(0, hy)], src[part, rows, pl.ds(hy, hy)]
    sums = []
    for own, other in ((left, right), (right, left)):
        sums.append(dot(qx_ref[4], own) + dot(own, qy_ref[5]) + dot(other, qy_ref[6]))
    return sums


def half_ends(nx):
    hx = nx // 2
    return [(0, nx - 1), (hx - 1, hx), (hx, hx - 1), (nx - 1, 0)]


def one_row(src, part, row):
    return src[part, pl.ds(row // 16 * 16, 16), :].astype(f32)[row % 16 : row % 16 + 1]


def first_kernel(dims, orders, plan, refs_ref, tables, *rest):
    nx, ny, rows_here = dims
    counts = [len(o) for o in orders]
    pieces, (out, folded, mid, spec, phase) = rest[: sum(counts)], rest[sum(counts) :]
    qx_ref = qy_ref = tables
    part_id, forward, _, _, _ = place_of(plan)
    at = 0
    for part, order in enumerate(orders):
        for piece_order in order:
            piece = pieces[at]
            at += 1
            for i, offset in enumerate(piece_order):
                block = part_id ^ offset
                rows = pl.ds(pl.multiple_of(block * rows_here, rows_here), rows_here)
                values = piece[i]

                @pl.when(forward == 1)
                def _():
                    a, b = fold_cols(values.astype(f32))
                    folded[part, rows, pl.ds(0, ny // 2)] = a
                    folded[part, rows, pl.ds(ny // 2, ny // 2)] = b

                @pl.when(forward == 0)
                def _():
                    out[part, rows, :] = values

    @pl.when(forward == 1)
    def _():
        fill_phase(nx, ny, refs_ref[0, 0:1, 0:1], 1.0, phase)
        forward_rows(nx, ny, folded, qy_ref, mid)
        through_columns(nx, ny, mid, phase, qx_ref, spec)
        inverse_rows(ny, [(start, nx // 2) for start in (0, nx // 2)], spec, qy_ref, out)


def laplace_rows(ref, part, start, count):
    center = ref[part, pl.ds(start + 8, count), :]
    width = center.shape[1]
    return (
        ref[part, pl.ds(start + 7, count), :]
        + ref[part, pl.ds(start + 9, count), :]
        + pltpu.roll(center, 1, 1)
        + pltpu.roll(center, width - 1, 1)
        - 4.0 * center
    )


def step_kernel(dims, orders, plan, index, parts, last, w_ref, refs_ref, tables, *rest):
    nx, ny, rows_here = dims
    qx_ref = qy_ref = tables
    coefs, rest = rest[: 2 * parts], rest[2 * parts :]
    coefs = (coefs[:parts], coefs[parts:])
    if last:
        coef_rows, out_rows, end_rows, out, plane, scaled, mid, spec, phase, tall, edge_rows = rest
    else:
        out, out_rows, plane, scaled, mid, spec, phase = rest
    part_id, forward, side, _, _ = place_of(plan)
    omega = refs_ref[plan[0], 0:1, 0:1]
    hy = ny // 2
    blocks = nx // rows_here
    place = []
    for which, order in enumerate(orders):
        share = blocks // parts
        place.append(
            {o: (i // share, which * share + i % share) for i, o in enumerate(sum(order, []))}
        )
    step = min(16, rows_here)

    def portions():
        for offset in range(blocks):
            for sub in range(0, rows_here, step):
                start = pl.multiple_of((part_id ^ offset) * rows_here + sub, step)
                yield offset, sub, start

    def lens_at(q, offset, sub):
        cols = pl.ds(pl.multiple_of((side ^ q) * hy, hy), hy)
        rows = pl.ds(sub, step)
        (ca, ci), (da, di) = place[0][offset], place[1][offset]
        c = coefs[q][ca][ci, rows, :].astype(f32)
        cos, sin = small_cos_sin(omega * coefs[q][da][di, rows, :].astype(f32))
        return cols, c, cos, sin

    hx = nx // 2
    first = pl.multiple_of(part_id * rows_here, rows_here)
    mine = pl.ds(first, rows_here)

    @pl.when(forward == 1)
    def _():
        for offset, sub, start in portions():
            rows = pl.ds(start, step)
            for q in range(2):
                cols, c, lr, li = lens_at(q, offset, sub)
                wr, wi = w_ref[0, rows, cols].astype(f32), w_ref[1, rows, cols].astype(f32)
                ur, ui = wr * lr - wi * li, wr * li + wi * lr
                plane[0, rows, cols] = ur
                plane[1, rows, cols] = ui
                scaled[0, rows, cols] = (c * ur).astype(bf16)
                scaled[1, rows, cols] = (c * ui).astype(bf16)
        for row, beside in half_ends(nx):
            plane[0, pl.ds(row, 1), :] -= one_row(scaled, 1, beside)
            plane[1, pl.ds(row, 1), :] += one_row(scaled, 0, beside)
        spectra = []
        for block in range(2):
            rows = pl.ds(block * hx, hx)
            sums = [laplace_block(scaled, part, block, hx, hy, qx_ref, qy_ref) for part in range(2)]
            for part in range(2):
                left, right = plane[part, rows, pl.ds(0, hy)], plane[part, rows, pl.ds(hy, hy)]
                l, r = sums[1 - part]
                left, right = (left + l, right + r) if part else (left - l, right - r)
                spec[part, rows, pl.ds(0, hy)] = left.astype(bf16)
                spec[part, rows, pl.ds(hy, hy)] = right.astype(bf16)
                spectra.append(
                    (
                        dot((left + right).astype(bf16), qy_ref[0]),
                        dot((left - right).astype(bf16), qy_ref[1]),
                    )
                )
        for part in range(2):
            for par in range(2):
                add_subtract(mid, part, par, hx, hy, spectra[part][par], spectra[2 + part][par])
        for part in range(2):
            out_rows[part] = spec[part, mine, :]

    @pl.when(forward == 0)
    def _():
        for part in range(2):
            for block in range(2):
                rows = pl.ds(block * hx, hx)
                l, r = laplace_block(w_ref, part, block, hx, hy, qx_ref, qy_ref)
                plane[part, rows, pl.ds(0, hy)] = l
                plane[part, rows, pl.ds(hy, hy)] = r
            for row, beside in half_ends(nx):
                plane[part, pl.ds(row, 1), :] += one_row(w_ref, part, beside)
        flip = (1 - 2 * side).astype(f32)
        for offset, sub, start in portions():
            rows = pl.ds(start, step)
            halves = []
            for q in range(2):
                cols, c, lr, li = lens_at(q, offset, sub)
                tr = w_ref[0, rows, cols].astype(f32) + c * plane[1, rows, cols]
                ti = w_ref[1, rows, cols].astype(f32) - c * plane[0, rows, cols]
                halves.append((tr * lr + ti * li, ti * lr - tr * li))
            for part in range(2):
                a, b = halves[0][part], halves[1][part]
                scaled[part, rows, pl.ds(0, hy)] = (a + b).astype(bf16)
                scaled[part, rows, pl.ds(hy, hy)] = (flip * (a - b)).astype(bf16)
        forward_rows(nx, ny, scaled, qy_ref, mid)

    fill_phase(nx, ny, refs_ref[index + 1, 0:1, 0:1], (2 * forward - 1).astype(f32), phase)
    through_columns(nx, ny, mid, phase, qx_ref, spec)
    before_start = pl.multiple_of(lax.rem(first + nx - 16, nx), 16)
    after_start = pl.multiple_of(lax.rem(first + rows_here, nx), 16)
    if last:
        wanted = [(first, rows_here), (before_start, 16), (after_start, 16)]
    else:
        wanted = [(start, hx) for start in (0, hx)]
    inverse_rows(ny, wanted, spec, qy_ref, out)

    @pl.when(forward == 0)
    def _():
        for part in range(2):
            out_rows[part] = out[part, mine, :]

    if not last:
        return
    for q in range(2):
        cols = pl.ds(pl.multiple_of((side ^ q) * hy, hy), hy)
        for i in range(2):
            for j in range(2):
                row = (2 * i + j) * 16
                rows = pl.ds(row % rows_here, 16)
                edge_rows[i, j, :, cols] = coefs[q][-1][2 * (blocks // parts) + row // rows_here, rows, :]

    @pl.when(forward == 0)
    def _():
        end_rows[...] = jnp.zeros_like(end_rows)

    @pl.when(forward == 1)
    def _():
        before = pl.ds(before_start, 16)
        after = pl.ds(after_start, 16)

        def lensed(values, c, d):
            lr, li = small_cos_sin(omega * d.astype(f32))
            wr, wi = values[0].astype(f32), values[1].astype(f32)
            ur, ui = wr * lr - wi * li, wr * li + wi * lr
            cf = c.astype(f32)
            return ur, ui, cf * ur, cf * ui

        ur, ui, gr, gi = lensed(
            (out[0, mine, :], out[1, mine, :]), coef_rows[0], coef_rows[1]
        )
        tall[0, pl.ds(8, rows_here), :] = gr
        tall[1, pl.ds(8, rows_here), :] = gi
        _, _, gr, gi = lensed(
            (out[0, before, :][15:16], out[1, before, :][15:16]), edge_rows[0, 0, 15:16, :], edge_rows[0, 1, 15:16, :]
        )
        tall[0, pl.ds(7, 1), :] = gr
        tall[1, pl.ds(7, 1), :] = gi
        _, _, gr, gi = lensed(
            (out[0, after, :][0:1], out[1, after, :][0:1]), edge_rows[1, 0, 0:1, :], edge_rows[1, 1, 0:1, :]
        )
        tall[0, pl.ds(rows_here + 8, 1), :] = gr
        tall[1, pl.ds(rows_here + 8, 1), :] = gi
        end_rows[0] = (ur - laplace_rows(tall, 1, 0, rows_here)).astype(bf16)
        end_rows[1] = (ui + laplace_rows(tall, 0, 0, rows_here)).astype(bf16)


def run_first(dims, orders, plan, refs, tables, pieces):
    nx, ny, _ = dims
    return pl.pallas_call(
        partial(first_kernel, dims, orders, plan),
        out_shape=jax.ShapeDtypeStruct((2, nx, ny), bf16),
        in_specs=[vm, vm] + [vm] * len(pieces),
        out_specs=vm,
        scratch_shapes=[pltpu.VMEM((2, nx, ny), bf16)] * 4,
        compiler_params=pltpu.CompilerParams(vmem_limit_bytes=vmem_bytes),
        cost_estimate=pl.CostEstimate(flops=2**30, bytes_accessed=2**22, transcendentals=0),
        name="first_step",
    )(refs, tables, *pieces)


def run_step(dims, orders, plan, index, w, coefs, refs, tables, coef_rows=None):
    nx, ny, rows_here = dims
    last = coef_rows is not None
    rows_shape = jax.ShapeDtypeStruct((2, rows_here, ny), bf16)
    full = pltpu.VMEM((2, nx, ny), bf16)
    scratch = [pltpu.VMEM((2, nx, ny), f32)]
    scratch += [full] * 4
    if last:
        outs = (rows_shape, rows_shape)
        scratch = [full] + scratch + [pltpu.VMEM((2, rows_here + 16, ny), f32)]
        scratch += [pltpu.VMEM((2, 2, 16, ny), bf16)]
    else:
        outs = (jax.ShapeDtypeStruct((2, nx, ny), bf16), rows_shape)
    return pl.pallas_call(
        partial(step_kernel, dims, orders, plan, index, len(coefs) // 2, last),
        out_shape=outs,
        in_specs=[vm] * (3 + len(coefs) + (1 if last else 0)),
        out_specs=(vm,) * len(outs),
        scratch_shapes=scratch,
        compiler_params=pltpu.CompilerParams(vmem_limit_bytes=vmem_bytes),
        cost_estimate=pl.CostEstimate(flops=2**32, bytes_accessed=2**24, transcendentals=0),
        name="end_step" if last else "depth_step",
    )(w, refs, tables, *coefs, *([coef_rows] if last else []))


def join_kernel(counts, wanted, sides, *refs):
    count = len(counts)
    kept = (len(refs) - count - len(wanted)) // 2
    pieces, outs = refs[kept : kept + count], refs[2 * kept + count :]
    for (slot, chosen), out in zip(wanted, outs):
        at = 0
        for which in chosen:
            for i in range(counts[which]):
                out[at + i] = pieces[which][i, slot]
            at += counts[which]
    if not sides:
        return
    rows_here = pieces[0].shape[2]
    size = sum(counts) // 2
    part_id = lax.axis_index("rows")
    for i, (beside, first) in enumerate(((size - 1, rows_here - 16), (1, 0))):
        offset_wanted = part_id ^ lax.rem(part_id + beside, size)
        for j, (order, chosen) in enumerate(sides):
            places = [(which, k) for which in chosen for k in range(counts[which])]
            row = (2 * i + j) * 16
            target = outs[-1].at[at + row // rows_here, pl.ds(row % rows_here, 16)]
            for offset, (which, k) in zip(order, places):

                @pl.when(offset_wanted == offset)
                def _(which=which, k=k, first=first, target=target):
                    target[...] = pieces[which][k, 0, pl.ds(first, 16), :]


def run_join(pieces, wanted, kept=(), sides=()):
    _, _, rows_here, hy = pieces[0].shape
    counts = [piece.shape[0] for piece in pieces]
    shapes = [(sum(counts[i] for i in chosen), rows_here, hy) for _, chosen in wanted]
    if sides:
        shapes[-1] = (shapes[-1][0] + -(-64 // rows_here), rows_here, hy)
    return pl.pallas_call(
        partial(join_kernel, counts, wanted, sides),
        out_shape=[jax.ShapeDtypeStruct(k.shape, k.dtype) for k in kept]
        + [jax.ShapeDtypeStruct(shape, bf16) for shape in shapes],
        in_specs=[vm] * (len(kept) + len(pieces)),
        out_specs=[vm] * (len(kept) + len(shapes)),
        input_output_aliases={i: i for i in range(len(kept))},
        compiler_params=pltpu.CompilerParams(vmem_limit_bytes=vmem_bytes),
        cost_estimate=pl.CostEstimate(flops=0, bytes_accessed=2**18, transcendentals=0),
        name="join_pieces",
    )(*kept, *pieces)


def image_kernel(plan, refs_ref, *refs):
    sections, freq_count = plan
    fields, (bottom, out) = refs[:-2], refs[-2:]
    _, forward, _, freq, group = place_of(plan)

    def total(adjoint_at):
        result = None
        for i in range(freq_count):
            freq_i = freq ^ i
            adjoint = adjoint_at(i, freq_i)
            a = [fields[i][j].astype(f32) for j in range(2)]
            b = [adjoint[j].astype(f32) for j in range(2)]
            weight = refs_ref[sections + i, 0:1, 0:1] * (2 * forward - 1).astype(f32)
            term = weight * (a[0] * b[1] - a[1] * b[0])
            result = term if result is None else result + term
        out[0] = result

    @pl.when(group == sections - 1)
    def _():
        total(lambda i, freq_i: bottom.at[freq_i])

    @pl.when(group != sections - 1)
    def _():
        total(lambda i, freq_i: fields[freq_count + i])


def run_image(plan, refs, fields, bottom):
    _, rows_here, ny = fields[0].shape
    return pl.pallas_call(
        partial(image_kernel, plan),
        out_shape=jax.ShapeDtypeStruct((1, rows_here, ny), f32),
        in_specs=[vm] * (len(fields) + 2),
        out_specs=vm,
        compiler_params=pltpu.CompilerParams(vmem_limit_bytes=vmem_bytes),
        name="image",
    )(refs, *fields, bottom)


def swap(values, axis, mask):
    axes = axis if isinstance(axis, tuple) else (axis,)
    size = math.prod(lax.axis_size(a) for a in axes)
    return lax.ppermute(values, axis, [(i, i ^ mask) for i in range(size)])


def doubling_masks(size):
    masks = []
    mask = size // 2
    while mask:
        masks.append(mask)
        mask //= 2
    descending = masks
    ascending = masks[:1] + masks[1:][::-1]
    return descending, ascending


def doubling_orders(masks):
    orders = [[0]]
    seen = [0]
    for mask in masks:
        new = [mask ^ o for o in seen]
        orders.append(new)
        seen = seen + new
    return orders


def first_exchange(pair, axis):
    size = lax.axis_size(axis)
    got = swap(pair, axis, size // 2)
    return [[pair[0:1], got[0:1]], [pair[1:2], got[1:2]]]


def after(values, earlier):
    return lax.optimization_barrier((values, earlier))[0]


def next_exchange(pieces, axis, level):
    masks = doubling_masks(lax.axis_size(axis))
    return [
        have + [swap(jnp.concatenate(have, 0), axis, masks[which][level])]
        for which, have in enumerate(pieces)
    ]


def per_device(source_top, adjoint_bottom, slowness, correction, slowness_ref, omega):
    row_parts = lax.axis_size("rows")
    sections = lax.axis_size("depth")
    group = lax.axis_index("depth")
    part_id = lax.axis_index("rows")
    freq_count = omega.shape[0]
    chains = 2 * freq_count
    rep = sections // chains
    rows_here, ny = slowness.shape[1:]
    nx = rows_here * row_parts
    dims = (nx, ny, rows_here)
    hy = ny // 2
    chain = lax.div(group, rep)
    forward = lax.div(chain, freq_count)
    freq = lax.rem(chain, freq_count)
    side = lax.rem(group, 2)
    half_sections = sections // 2
    masks = doubling_masks(row_parts)
    orders = [doubling_orders(m) for m in masks]
    rounds = len(masks[0])
    plan = (sections, freq_count)

    def pick(values, index):
        return lax.dynamic_index_in_dim(values, index, 0, keepdims=False)

    plane = jnp.where(forward == 1, pick(source_top, freq), pick(adjoint_bottom, freq))
    high = slowness_ref.astype(bf16)
    middle = (slowness_ref - high.astype(f32)).astype(bf16)
    low = (slowness_ref - high.astype(f32) - middle.astype(f32)).astype(bf16)
    terms = jnp.concatenate([high, middle, low, jnp.zeros((13,), bf16)])
    values = jnp.concatenate([correction[0], slowness[0] - slowness_ref[0]], 0).astype(bf16)
    values = jnp.concatenate([values, jnp.broadcast_to(terms[:, None], (16, ny))], 0)
    left, right = values[:, :hy], values[:, hy:]
    same = jnp.where(side == 0, left, right)
    other = jnp.where(side == 0, right, left)
    packed = jnp.stack([same, other])
    blocks, partner = [packed], []
    for k in range(1, sections):
        blocks.append(swap(packed if k < half_sections else (same, other)[k % 2], "depth", k))
    for k in range(half_sections, sections):
        sent = (same, other)[k % 2][: 2 * rows_here]
        mask = k * row_parts + row_parts // 2
        partner.append(swap(sent, ("depth", "rows"), mask))
    planes = first_exchange(plane, "rows")
    assert nx == ny
    tables = basis_tables(nx)
    for level in range(1, rounds):
        planes = next_exchange(planes, "rows", level)
        if level == 1:
            blocks, partner = after((blocks, partner), planes)
            pair, refs, coef_rows = run_sort(omega, blocks, partner, rows_here, hy)
            pieces = [[pair[0]], [pair[1]]]
            planes = after(planes, pair)
        before = pieces
        pieces = next_exchange(pieces, "rows", level)
    w = run_first(dims, orders, plan, refs, tables, after(planes[0] + planes[1], before))
    far_slots = [sections - 1 - slot for slot in range(half_sections, sections - 1)]
    early = before[0] + before[1]
    head = run_join(early, [(slot, range(len(early))) for slot in far_slots])
    head = [swap(h, "depth", half_sections) for h in head]
    last = after([have[-1] for have in pieces], (w, head))
    each = len(before[0])
    order = [*range(each), 2 * each, *range(each, 2 * each), 2 * each + 1]
    wanted = [(slot, order) for slot in range(half_sections)]
    wanted += [(slot, order[each :: each + 1]) for slot in far_slots]
    sides = [
        (sum(orders[j], []), order[j * (each + 1) : (j + 1) * (each + 1)]) for j in range(2)
    ]
    w, refs, *joined = run_join(early + last, wanted, (w, refs), sides)
    mine, rest = joined[:half_sections], joined[half_sections:]
    coefs = [[m, swap(m, "depth", 1)] for m in mine]
    far = [[h, swap(r, "depth", half_sections)] for h, r in zip(head, rest)]
    row_outs = []
    for slot in range(sections - 1):
        last = slot == sections - 2
        w, *rest = run_step(
            dims, orders, plan, slot, w, coefs[slot], refs, tables, coef_rows if last else None
        )
        if slot == half_sections - 1:
            coefs += [have + [swap(part, "depth", 1) for part in have] for have in after(far, w)]
        row_outs += [w, *rest] if last else rest

    def index_for(g, target):
        return target if g >= half_sections else sections - 2 - target

    def payload_for(mask):
        used = sorted(
            {index_for(g, g ^ mask) for g in range(sections) if index_for(g, g ^ mask) >= 0}
        )
        low = used[0]
        stack = jnp.stack(row_outs[low : used[-1] + 1])
        target = group ^ mask
        index = jnp.where(forward == 1, target, sections - 2 - target)
        return pick(stack, jnp.clip(index - low, 0, len(stack) - 1))

    far = [swap(payload_for(i * rep), "depth", i * rep) for i in range(freq_count, chains)]
    near = [payload_for(i * rep) for i in range(freq_count)]
    fields = [f if i == 0 else swap(f, "depth", i * rep) for i, f in enumerate(near)] + far
    return run_image(plan, refs, fields, adjoint_bottom)


def solution(mesh):
    in_specs = (
        P(None, None, "rows", None),
        P(None, None, "rows", None),
        P("depth", "rows", None),
        P("depth", "rows", None),
        P("depth"),
        P(),
    )
    out_specs = P("depth", "rows", None)
    return jax.shard_map(
        per_device, mesh=mesh, in_specs=in_specs, out_specs=out_specs, check_vma=False
    )
```
